256 devices in a mesh: doc: 8 (over x_hi, y), seq: 32 (over x_lo, z, core).
Axes of the slice: x: 4 (x_hi: 2, x_lo: 2; x = x_hi * 2 + x_lo), y: 4, z: 8, core: 2. Of those that a mesh axis runs over, the one named last changes fastest.
Arguments:
- hidden_in: bfloat16 [32768, 2048], P(('doc', 'seq')), parts along dimension 0
- length: int32 [8], P('doc'), parts along dimension 0, may hold values from 2048 to 4096
- attn_gain: float32 [2048], replicated, may hold values from 0.1 to 1.9
- global_gain: float32 [2048], replicated, may hold values from 0.1 to 1.9
- w_query: bfloat16 [2048, 1024], P(None, 'seq')
- w_key: bfloat16 [2048, 1024], P(None, 'seq')
- w_value: bfloat16 [2048, 1024], P(None, 'seq'), may hold values from -0.125 to 0.125
- w_out: bfloat16 [1024, 2048], P(None, 'seq'), may hold values from -0.75 to 0.75
Outputs:
- attended: bfloat16 [32768, 2048], P(('doc', 'seq')), parts along dimension 0
The draws below stay inside these ranges and needn't reach their ends.
There are 8 independent parts, one for each index of `doc`. The reference program is written for one: setup_inputs(seed, part) draws one part's arguments, and reference() takes and returns one part's arrays. A program takes and returns all parts, laid end to end along the dimension named above; an argument that names none is the same for every part. Nothing has to cross between parts.
All inputs are finite; a program needn't handle non-finite values.
Results may differ from the reference program's by a relative error of at most 0.034.
Values may be sent and summed in bfloat16 or wider, within the bound.
No kernel may reach another device: no remote copies, remote signals or barrier semaphores. Data moves between devices by JAX's collectives and lax.ppermute only.
A program may use at most 64 MiB of HBM per device.

```python
import math
import jax
import jax.numpy as jnp
from jax import lax

D = 2048
HEAD_DIM = 64
HEADS = 16
BLOCK = 16
RADIUS = 127
INNER = 1024
SEQ = 4096


def draw_hidden_in(key, part):
    noise_key = jax.random.fold_in(key, 3)
    scale_key = jax.random.fold_in(key, 4)
    row_scale = jnp.exp(jax.random.uniform(scale_key, (SEQ, 1), jnp.float32, 0.0, math.log(10.0)))
    base_noise = jax.random.normal(noise_key, (SEQ, D), jnp.float32)
    return (base_noise * row_scale).astype(jnp.bfloat16)


def draw_length(key, part):
    drawn = jax.random.randint(jax.random.fold_in(key, 7), (1,), SEQ // 2, SEQ + 1, dtype=jnp.int32)
    full_doc = part % 2 == 1
    return jnp.where(full_doc, jnp.full((1,), SEQ, jnp.int32), drawn).astype(jnp.int32)


def weight_pair(key):
    query_key = jax.random.fold_in(key, 21)
    noise_key = jax.random.fold_in(key, 22)
    scale = 0.5 / math.sqrt(D)
    query_float = jax.random.normal(query_key, (D, HEADS * HEAD_DIM), jnp.float32) * scale
    other_float = jax.random.normal(noise_key, (D, HEADS * HEAD_DIM), jnp.float32) * scale
    key_float = other_float
    return (query_float, key_float)


def draw_w_query(key, part):
    return weight_pair(key)[0].astype(jnp.bfloat16)


def draw_w_key(key, part):
    return weight_pair(key)[1].astype(jnp.bfloat16)


def level_of(stream_key, dims, cuts, smallest, largest):
    loudness = 1.0
    for axis_at, blocks in cuts:
        steps = jax.random.uniform(jax.random.fold_in(jax.random.fold_in(stream_key, 6), axis_at), (blocks,), jnp.float32, smallest / len(cuts), largest / len(cuts))
        loudness = loudness * jnp.repeat(jnp.exp(steps), dims[axis_at] // blocks).reshape((-1,) + (1,) * (len(dims) - 1 - axis_at))
    return loudness


def normal_values(key, dims, scale, bound, split=(), held_as=jnp.bfloat16):
    gain = level_of(key, dims, split, -0.22, 0.18) if split else 1.0
    result = jax.random.normal(key, dims, jnp.float32) * scale * gain
    return jnp.minimum(jnp.maximum(result, -bound), bound).astype(held_as)


def setup_inputs(seed: int = 0, part: int = 0) -> dict:
    splits = jax.random.split(jax.random.key(seed), 9)
    part_keys = jax.random.split(jax.random.fold_in(splits[8], part), 9)
    return {
        "hidden_in": draw_hidden_in(jax.random.fold_in(jax.random.fold_in(splits[8], part), 71), part),
        "length": draw_length(jax.random.fold_in(jax.random.fold_in(splits[8], part), 71), part),
        "attn_gain": jnp.clip(1.0 + 0.18 * jax.random.normal(splits[2], (D,), jnp.float32), 0.1, 1.9),
        "global_gain": jnp.clip(1.0 + 0.18 * jax.random.normal(splits[3], (D,), jnp.float32), 0.1, 1.9),
        "w_query": draw_w_query(jax.random.fold_in(splits[8], 71), part),
        "w_key": draw_w_key(jax.random.fold_in(splits[8], 71), part),
        "w_value": normal_values(splits[6], (D, INNER), D ** -0.5, 0.125, ((1, 32),)),
        "w_out": normal_values(splits[7], (INNER, D), (INNER // 16) ** -0.5, 0.75, ((1, 32),)),
    }


NEGATIVE = -1e+30
EPSILON = 1e-06

def rms_norm(values, gain_row):
    mean_square = lax.optimization_barrier(jnp.mean(values * values, axis=-1, keepdims=True))
    return values * lax.rsqrt(mean_square + EPSILON) * gain_row

def reference(hidden_in, length, attn_gain, global_gain, w_query, w_key, w_value, w_out):
    seq_len = hidden_in.shape[0]
    inner_width = w_query.shape[1]
    normed = rms_norm(hidden_in.astype(jnp.float32), attn_gain).astype(jnp.bfloat16)
    queries = jnp.dot(normed, w_query, preferred_element_type=jnp.float32).astype(jnp.bfloat16)
    keys_all = jnp.dot(normed, w_key, preferred_element_type=jnp.float32).astype(jnp.bfloat16)
    values_all = jnp.dot(normed, w_value, preferred_element_type=jnp.float32).astype(jnp.bfloat16)
    doc_limit = length[0]
    positions = jnp.arange(seq_len, dtype=jnp.int32)
    is_valid = (positions < doc_limit).astype(jnp.float32)
    block_count = seq_len // BLOCK
    block_sums = lax.optimization_barrier(jnp.sum((normed.astype(jnp.float32) * is_valid[:, None]).reshape(block_count, BLOCK, D), axis=1))
    global_normed = rms_norm(block_sums, global_gain).astype(jnp.bfloat16)
    global_keys = jnp.dot(global_normed, w_key, preferred_element_type=jnp.float32).astype(jnp.bfloat16)
    global_values = jnp.dot(global_normed, w_value, preferred_element_type=jnp.float32).astype(jnp.bfloat16)
    global_keys = global_keys.reshape(block_count, HEADS, HEAD_DIM).astype(jnp.float32)
    global_values = global_values.reshape(block_count, HEADS, HEAD_DIM).astype(jnp.float32)
    global_ok = jnp.arange(block_count, dtype=jnp.int32) * BLOCK < doc_limit
    padded_keys = jnp.pad(keys_all, ((RADIUS, RADIUS), (0, 0)))
    padded_values = jnp.pad(values_all, ((RADIUS, RADIUS), (0, 0)))
    query_rows = math.gcd(seq_len, 512)
    near_span = query_rows + 2 * RADIUS

    def one_block(start_row):
        block_queries = lax.dynamic_slice_in_dim(queries, start_row, query_rows, 0)
        block_queries = block_queries.reshape(query_rows, HEADS, HEAD_DIM).astype(jnp.float32)
        near_keys = lax.dynamic_slice_in_dim(padded_keys, start_row, near_span, 0)
        near_keys = near_keys.reshape(near_span, HEADS, HEAD_DIM).astype(jnp.float32)
        near_values = lax.dynamic_slice_in_dim(padded_values, start_row, near_span, 0)
        near_values = near_values.reshape(near_span, HEADS, HEAD_DIM).astype(jnp.float32)
        near_raw = jnp.einsum('qhd,khd->hqk', block_queries, near_keys)
        query_pos = start_row + jnp.arange(query_rows, dtype=jnp.int32)
        key_pos = start_row - RADIUS + jnp.arange(near_span, dtype=jnp.int32)
        allowed = (jnp.abs(query_pos[:, None] - key_pos[None, :]) <= RADIUS) & (key_pos[None, :] >= 0) & (key_pos[None, :] < doc_limit)
        near_raw = jnp.where(allowed[None], near_raw, NEGATIVE)
        distant = jnp.einsum('qhd,ghd->hqg', block_queries, global_keys)
        distant = jnp.where(global_ok[None, None, :], distant, NEGATIVE)
        highest = jnp.maximum(lax.optimization_barrier(jnp.max(near_raw, axis=-1)), lax.optimization_barrier(jnp.max(distant, axis=-1)))
        near_weights = jnp.exp(near_raw - highest[..., None])
        far_weights = jnp.exp(distant - highest[..., None])
        denominator = lax.optimization_barrier(jnp.sum(near_weights, axis=-1)) + lax.optimization_barrier(jnp.sum(far_weights, axis=-1))
        near_low = lax.optimization_barrier(near_weights.astype(jnp.bfloat16)).astype(jnp.float32)
        far_low = lax.optimization_barrier(far_weights.astype(jnp.bfloat16)).astype(jnp.float32)
        context = jnp.einsum('hqk,khd->qhd', near_low, near_values) + jnp.einsum('hqg,ghd->qhd', far_low, global_values)
        context = context / jnp.transpose(denominator)[:, :, None]
        return context.reshape(query_rows, inner_width).astype(jnp.bfloat16)
    starts = jnp.arange(seq_len // query_rows, dtype=jnp.int32) * query_rows
    context = lax.map(one_block, starts).reshape(seq_len, inner_width)
    return jnp.dot(context, w_out, preferred_element_type=jnp.float32).astype(jnp.bfloat16)
```

```python
import functools

import jax
import jax.numpy as jnp
from jax import lax
from jax.experimental import pallas as pl
from jax.experimental.pallas import tpu as pltpu
from jax.sharding import PartitionSpec as P

HEAD_DIM = 64
BLOCK = 16
RADIUS = 127
NEGATIVE = -1e30
EPSILON = 1e-06

X, Z, C = 2, 8, 2
SEQ_SHARDS = X * Z * C
TOK = 128
HALF = 32
HEADS_LOCAL = 4
WIDE = HEADS_LOCAL * HEAD_DIM


def place(x, z, core):
    return (x * Z + z) * C + core


def pairs(move):
    return [
        (place(x, z, c), place(*move(x, z, c))) for x in range(X) for z in range(Z) for c in range(C)
    ]


OTHER_CORE = pairs(lambda x, z, c: (x, z, 1 - c))
OTHER_X = pairs(lambda x, z, c: (1 - x, z, c))
AHEAD = pairs(lambda x, z, c: (x, (z + (1 if c == 0 else -1)) % Z, c))
BEHIND = pairs(lambda x, z, c: (x, (z - (1 if c == 0 else -1)) % Z, c))
UP = pairs(lambda x, z, c: (x, (z + 1) % Z, c))
DOWN = pairs(lambda x, z, c: (x, (z - 1) % Z, c))


def send(value, route):
    return lax.ppermute(value, "seq", route)


def rms_norm(values, gain_row):
    mean_square = jnp.mean(values * values, axis=-1, keepdims=True)
    return values * lax.rsqrt(mean_square + EPSILON) * gain_row


def dot_nt(left, right):
    return lax.dot_general(
        left, right, (((1,), (1,)), ((), ())), preferred_element_type=jnp.float32
    )


def attention_kernel(scalars, far_pos, q_ref, k_ref, v_ref, kl_ref, vl_ref, kr_ref, vr_ref, gk_ref, gv_ref, out_ref):
    limit = scalars[0]
    lane_head = (lax.broadcasted_iota(jnp.int32, (TOK, WIDE), 1) % 128) // HALF
    row = lax.broadcasted_iota(jnp.int32, (HEADS_LOCAL * TOK, TOK), 0) % TOK
    col = lax.broadcasted_iota(jnp.int32, (HEADS_LOCAL * TOK, TOK), 1)
    far_ok = far_pos[...] < limit
    for seg in range(2):
        for part in range(2):
            base = scalars[1 + seg] + part * TOK
            at = (seg * 2 + part) * TOK
            queries = q_ref[at : at + TOK, :]
            stacked = jnp.concatenate(
                [jnp.where(lane_head == h, queries, jnp.zeros_like(queries)) for h in range(HEADS_LOCAL)],
                axis=0,
            )
            side = slice(seg * TOK, (seg + 1) * TOK)
            if part == 0:
                left = (kl_ref, vl_ref, side)
                right = (k_ref, v_ref, slice(at + TOK, at + 2 * TOK))
            else:
                left = (k_ref, v_ref, slice(at - TOK, at))
                right = (kr_ref, vr_ref, side)
            mid = (k_ref, v_ref, slice(at, at + TOK))
            s_left = dot_nt(stacked, left[0][left[2], :])
            s_mid = dot_nt(stacked, mid[0][mid[2], :])
            s_right = dot_nt(stacked, right[0][right[2], :])
            s_far = dot_nt(stacked, gk_ref[...])
            low = base - TOK
            ok_left = (col > row) & (col + low >= 0) & (col + low < limit)
            ok_mid = col + base < limit
            ok_right = (col < row) & (col + (base + TOK) < limit)
            s_left = jnp.where(ok_left, s_left, NEGATIVE)
            s_mid = jnp.where(ok_mid, s_mid, NEGATIVE)
            s_right = jnp.where(ok_right, s_right, NEGATIVE)
            s_far = jnp.where(far_ok, s_far, NEGATIVE)
            near_top = jnp.maximum(jnp.maximum(s_left, s_mid), s_right)
            far_top = jnp.maximum(s_far[:, :128], s_far[:, 128:])
            top = jnp.max(jnp.maximum(near_top, far_top), axis=-1, keepdims=True)
            w_left = jnp.exp(s_left - top)
            w_mid = jnp.exp(s_mid - top)
            w_right = jnp.exp(s_right - top)
            w_far = jnp.exp(s_far - top)
            total = jnp.sum(
                w_left + w_mid + w_right + w_far[:, :128] + w_far[:, 128:], axis=-1, keepdims=True
            )

            def mix(weights, values):
                return jnp.dot(
                    weights.astype(jnp.bfloat16), values, preferred_element_type=jnp.float32
                )

            mixed = (
                mix(w_left, left[1][left[2], :])
                + mix(w_mid, mid[1][mid[2], :])
                + mix(w_right, right[1][right[2], :])
                + mix(w_far, gv_ref[...])
            )
            mixed = mixed / total
            context = jnp.zeros((TOK, WIDE), jnp.float32)
            for h in range(HEADS_LOCAL):
                context = jnp.where(lane_head == h, mixed[h * TOK : (h + 1) * TOK, :], context)
            out_ref[at : at + TOK, :] = context.astype(jnp.bfloat16)


def attention(scalars, far_pos, *arrays):
    vmem = pl.BlockSpec(memory_space=pltpu.VMEM)
    return pl.pallas_call(
        attention_kernel,
        out_shape=jax.ShapeDtypeStruct((4 * TOK, WIDE), jnp.bfloat16),
        in_specs=[pl.BlockSpec(memory_space=pltpu.SMEM)] + [vmem] * (1 + len(arrays)),
        out_specs=vmem,
        compiler_params=pltpu.CompilerParams(vmem_limit_bytes=40 * 1024 * 1024),
        cost_estimate=pl.CostEstimate(
            flops=4 * 4 * TOK * 640 * WIDE * 4, bytes_accessed=3 << 20, transcendentals=4 * 4 * TOK * 640
        ),
    )(scalars, far_pos, *arrays)


def per_device(hidden_in, length, attn_gain, global_gain, w_query, w_key, w_value, w_out):
    width = hidden_in.shape[1]
    me = lax.axis_index("seq")
    core = me % C
    z = (me // C) % Z
    x = me // (C * Z)
    sign = 1 - 2 * core
    limit = length[0]
    bf16 = jnp.bfloat16

    mine = jnp.stack([w_query.T, w_key.T, w_value.T]).reshape(3, 2, 16, width)
    first = mine[:, 0].reshape(48, width)
    second = mine[:, 1].reshape(48, width)

    normed = rms_norm(hidden_in.astype(jnp.float32), attn_gain).astype(bf16)
    is_valid = (me * TOK + jnp.arange(TOK, dtype=jnp.int32) < limit).astype(jnp.float32)
    block_sums = jnp.sum(
        (normed.astype(jnp.float32) * is_valid[:, None]).reshape(TOK // BLOCK, BLOCK, width), axis=1
    )
    global_mine = rms_norm(block_sums, global_gain).astype(bf16)
    global_there = send(global_mine, OTHER_X)
    global_pair = jnp.concatenate(
        [jnp.where(x == 0, global_mine, global_there), jnp.where(x == 0, global_there, global_mine)], axis=0
    )
    second = jnp.concatenate([second, global_pair], axis=0)

    weights = jnp.zeros((3, Z, 2, 16, width), bf16)
    globals_z = jnp.zeros((Z, 16, width), bf16)

    def store(weights, globals_z, one, two, at):
        weights = lax.dynamic_update_slice(weights, one.reshape(3, 1, 1, 16, width), (0, at, 0, 0, 0))
        weights = lax.dynamic_update_slice(weights, two[:48].reshape(3, 1, 1, 16, width), (0, at, 1, 0, 0))
        globals_z = lax.dynamic_update_slice(globals_z, two[48:][None], (at, 0, 0))
        return weights, globals_z

    weights, globals_z = store(weights, globals_z, first, second, z)
    a_one, a_two, b_one, b_two = first, second, first, second
    for step in range(1, 5):
        a_one = send(a_one, AHEAD)
        if step < 4:
            b_one = send(b_one, BEHIND)
        a_two = send(a_two, AHEAD)
        if step < 4:
            b_two = send(b_two, BEHIND)
        weights, globals_z = store(weights, globals_z, a_one, a_two, (z - sign * step) % Z)
        if step < 4:
            weights, globals_z = store(weights, globals_z, b_one, b_two, (z + sign * step) % Z)

    across = send(normed, OTHER_X)
    beside = send(normed, OTHER_CORE)
    beside_across = send(across, OTHER_CORE)
    rows = jnp.zeros((X, C, TOK, width), bf16)
    for block, bx, bc in (
        (normed, x, core),
        (across, 1 - x, core),
        (beside, x, 1 - core),
        (beside_across, 1 - x, 1 - core),
    ):
        rows = lax.dynamic_update_slice(rows, block[None, None], (bx, bc, 0, 0))
    rows = rows.reshape(4 * TOK, width)

    g_mine = globals_z.reshape(Z * 16, width)
    g_there = send(g_mine, OTHER_CORE)
    g_rows = jnp.concatenate(
        [jnp.where(core == 0, g_mine, g_there), jnp.where(core == 0, g_there, g_mine)], axis=0
    )

    flat = weights.reshape(3 * Z * HALF, width)
    projected = dot_nt(rows, flat).astype(bf16)
    g_projected = dot_nt(g_rows, flat[Z * HALF :]).astype(bf16)

    def swap(table):
        kinds = table.shape[1] // (Z * HALF)
        split = table.reshape(table.shape[0], kinds, 2, 128)
        low = split[:, :, 0].reshape(-1, kinds * 128)
        high = split[:, :, 1].reshape(-1, kinds * 128)
        keep = jnp.where(core == 0, low, high)
        got = send(jnp.where(core == 0, high, low), OTHER_CORE)
        left = jnp.where(core == 0, keep, got)
        right = jnp.where(core == 0, got, keep)
        return [
            jnp.concatenate([left[:, i * 128 : (i + 1) * 128], right[:, i * 128 : (i + 1) * 128]], axis=1)
            for i in range(kinds)
        ]

    queries, keys, values = swap(projected)
    far_keys, far_values = swap(g_projected)

    keys_values = jnp.concatenate([keys, values], axis=1).reshape(2, 2, TOK, 2 * WIDE)
    from_low = send(keys_values[:, 1], UP)
    from_high = send(keys_values[:, 0], DOWN)
    from_low = jnp.where(z == 0, from_low[::-1], from_low).reshape(2 * TOK, 2 * WIDE)
    from_high = jnp.where(z == Z - 1, from_high[::-1], from_high).reshape(2 * TOK, 2 * WIDE)

    at = jnp.arange(2 * Z * 16, dtype=jnp.int32)
    g_core, g_z, g_x, g_k = at // 128, (at // 16) % Z, (at // 8) % 2, at % 8
    far_pos = (((g_x * Z + g_z) * C + g_core) * TOK + g_k * BLOCK)[None, :]
    scalars = jnp.stack([limit, z * 2 * TOK, (Z + z) * 2 * TOK]).astype(jnp.int32)
    context = attention(
        scalars,
        far_pos,
        queries,
        keys,
        values,
        from_low[:, :WIDE],
        from_low[:, WIDE:],
        from_high[:, :WIDE],
        from_high[:, WIDE:],
        far_keys,
        far_values,
    )

    out_t = w_out.T.reshape(64, X, 2, HEADS_LOCAL, 2, HALF)
    out_t = jnp.transpose(out_t, (0, 2, 1, 4, 3, 5)).reshape(64, 2, 2 * WIDE)
    keep = jnp.where(core == 0, out_t[:, 0], out_t[:, 1])
    got = send(jnp.where(core == 0, out_t[:, 1], out_t[:, 0]), OTHER_CORE)
    chip = jnp.concatenate([jnp.where(core == 0, keep, got), jnp.where(core == 0, got, keep)], axis=0)
    chip_there = send(chip, OTHER_X)
    both = jnp.stack([jnp.where(x == 0, chip, chip_there), jnp.where(x == 0, chip_there, chip)])
    out_weights = jnp.zeros((X, Z, 2 * 64, 2 * WIDE), bf16)

    def put(out_weights, block, where):
        return lax.dynamic_update_slice(out_weights, block[:, None], (0, where, 0, 0))

    out_weights = put(out_weights, both, z)
    ahead, behind = both, both
    for step in range(1, 5):
        ahead = send(ahead, AHEAD)
        out_weights = put(out_weights, ahead, (z - sign * step) % Z)
        if step < 4:
            behind = send(behind, BEHIND)
            out_weights = put(out_weights, behind, (z + sign * step) % Z)
    out_weights = out_weights.reshape(-1, 2 * WIDE)

    context = context.reshape(2, 2 * TOK, WIDE)
    own = jnp.where(x == 0, context[0], context[1])
    theirs = send(jnp.where(x == 0, context[1], context[0]), OTHER_X)
    full = jnp.concatenate([jnp.where(x == 0, own, theirs), jnp.where(x == 0, theirs, own)], axis=1)
    partial = dot_nt(full, out_weights).reshape(2, TOK, -1)
    own_part = jnp.where(core == 0, partial[0], partial[1])
    sent = jnp.where(core == 0, partial[1], partial[0]).astype(bf16)
    return (own_part + send(sent, OTHER_CORE).astype(jnp.float32)).astype(bf16)


def solution(mesh):
    placed = (
        P(("doc", "seq"), None),
        P("doc"),
        P(),
        P(),
        P(None, "seq"),
        P(None, "seq"),
        P(None, "seq"),
        P(None, "seq"),
    )
    return jax.shard_map(
        per_device, mesh=mesh, in_specs=placed, out_specs=P(("doc", "seq"), None), check_vma=False
    )
```

```python
import jax
import jax.numpy as jnp
from jax import lax
from jax.experimental import pallas as pl
from jax.experimental.pallas import tpu as pltpu
from jax.sharding import PartitionSpec as P

HEAD_DIM = 64
BLOCK = 16
RADIUS = 127
NEGATIVE = -1e30
EPSILON = 1e-06

X, Z, C = 2, 8, 2
SEQ_SHARDS = X * Z * C
TOK = 128
HALF = 32
HEADS_LOCAL = 4
WIDE = HEADS_LOCAL * HEAD_DIM


def place(x, z, core):
    return (x * Z + z) * C + core


def pairs(move):
    return [
        (place(x, z, c), place(*move(x, z, c))) for x in range(X) for z in range(Z) for c in range(C)
    ]


OTHER_CORE = pairs(lambda x, z, c: (x, z, 1 - c))
OTHER_X = pairs(lambda x, z, c: (1 - x, z, c))
AHEAD = pairs(lambda x, z, c: (x, (z + (1 if c == 0 else -1)) % Z, c))
BEHIND = pairs(lambda x, z, c: (x, (z - (1 if c == 0 else -1)) % Z, c))
UP = pairs(lambda x, z, c: (x, (z + 1) % Z, c))
DOWN = pairs(lambda x, z, c: (x, (z - 1) % Z, c))


def send(value, route):
    return lax.ppermute(value, "seq", route)


def rms_norm(values, gain_row):
    mean_square = jnp.mean(values * values, axis=-1, keepdims=True)
    return values * lax.rsqrt(mean_square + EPSILON) * gain_row


def dot_nt(left, right):
    return lax.dot_general(
        left, right, (((1,), (1,)), ((), ())), preferred_element_type=jnp.float32
    )


STEPS = ((0, 0), (0, 1), (1, 1), (0, 2), (1, 2), (0, 3), (1, 3), (0, 4))
SHARDS = len(STEPS)
ROWS = 4 * TOK
G_ROWS = Z * 16
VMEM_LIMIT = 48 * 1024 * 1024


def z_of(z, core, way, hops):
    delta = -hops if way == 0 else hops
    return (z + delta * (1 - 2 * core)) & (Z - 1)


def project_kernel(index, *refs):
    blocks, firsts, seconds = refs[:4], refs[4 : 4 + SHARDS], refs[4 + SHARDS : 4 + 2 * SHARDS]
    g_most, g_last, keep_ref, send_ref, rows, g_rows, table = refs[4 + 2 * SHARDS :]
    z, core, x = index[0], index[1], index[2]
    low_core = core == 0
    for ref, bx, bc in zip(blocks, (x, 1 - x, x, 1 - x), (core, core, 1 - core, 1 - core)):
        rows[pl.ds(pl.multiple_of((bx * 2 + bc) * TOK, TOK), TOK), :] = ref[...]
    g_own = pl.multiple_of(core * G_ROWS, G_ROWS)
    g_other = pl.multiple_of((1 - core) * G_ROWS, G_ROWS)
    for j, (way, hops) in enumerate(STEPS):
        at = z_of(z, core, way, hops) * HALF
        for kind in range(3):
            here = pl.multiple_of(kind * 256 + at, 16)
            table[pl.ds(here, 16), :] = firsts[j][kind * 16 : kind * 16 + 16, :]
            there = pl.multiple_of(kind * 256 + at + 16, 16)
            table[pl.ds(there, 16), :] = seconds[j][kind * 16 : kind * 16 + 16, :]
        g_rows[pl.ds(g_own + j * 16, 16), :] = seconds[j][48:64, :]
    g_rows[pl.ds(g_other, 112), :] = g_most[...]
    g_rows[pl.ds(g_other + 112, 16), :] = g_last[...]
    for kind in range(3):
        out = dot_nt(rows[...], table[kind * 256 : kind * 256 + 256, :]).astype(jnp.bfloat16)
        lanes = slice(kind * 128, kind * 128 + 128)
        keep_ref[:, lanes] = jnp.where(low_core, out[:, :128], out[:, 128:])
        send_ref[:, lanes] = jnp.where(low_core, out[:, 128:], out[:, :128])
    for kind in (1, 2):
        out = dot_nt(g_rows[...], table[kind * 256 : kind * 256 + 256, :]).astype(jnp.bfloat16)
        at = slice((kind - 1) * 256, kind * 256)
        keep_ref[at, 384:] = jnp.where(low_core, out[:, :128], out[:, 128:])
        send_ref[at, 384:] = jnp.where(low_core, out[:, 128:], out[:, :128])


def attention_kernel(index, far_pos, keep_ref, got_ref, below_ref, above_ref, out_ref):
    z, x, limit = index[0], index[2], index[3]
    lane_head = (lax.broadcasted_iota(jnp.int32, (TOK, WIDE), 1) % 128) // HALF
    row = lax.broadcasted_iota(jnp.int32, (HEADS_LOCAL * TOK, TOK), 0) % TOK
    col = lax.broadcasted_iota(jnp.int32, (HEADS_LOCAL * TOK, TOK), 1)
    far_ok = far_pos[...] < limit
    far_keys = jnp.concatenate([keep_ref[:256, 384:], got_ref[:256, 384:]], axis=1)
    far_values = jnp.concatenate([keep_ref[256:, 384:], got_ref[256:, 384:]], axis=1)

    def local(kind, at):
        lanes = slice(kind * 128, kind * 128 + 128)
        return jnp.concatenate([keep_ref[at : at + TOK, lanes], got_ref[at : at + TOK, lanes]], axis=1)

    def halo(ref, kind, seg):
        at = pl.ds(pl.multiple_of(seg * TOK, TOK), TOK)
        lanes = kind * 128 - 128
        return jnp.concatenate([ref[at, lanes : lanes + 128], ref[at, lanes + 256 : lanes + 384]], axis=1)

    for seg in range(2):
        below_seg = jnp.where(z == 0, 1 - seg, seg)
        above_seg = jnp.where(z == Z - 1, 1 - seg, seg)
        for part in range(2):
            base = (seg * Z + z) * 2 * TOK + part * TOK
            at = (seg * 2 + part) * TOK
            queries = local(0, at)
            stacked = jnp.concatenate(
                [jnp.where(lane_head == h, queries, jnp.zeros_like(queries)) for h in range(HEADS_LOCAL)],
                axis=0,
            )

            def neighbours(kind):
                if part == 0:
                    return halo(below_ref, kind, below_seg), local(kind, at), local(kind, at + TOK)
                return local(kind, at - TOK), local(kind, at), halo(above_ref, kind, above_seg)

            k_left, k_mid, k_right = neighbours(1)
            v_left, v_mid, v_right = neighbours(2)
            low = base - TOK
            ok_left = (col > row) & (col + low >= 0) & (col + low < limit)
            ok_mid = col + base < limit
            ok_right = (col < row) & (col + (base + TOK) < limit)
            s_left = jnp.where(ok_left, dot_nt(stacked, k_left), NEGATIVE)
            s_mid = jnp.where(ok_mid, dot_nt(stacked, k_mid), NEGATIVE)
            s_right = jnp.where(ok_right, dot_nt(stacked, k_right), NEGATIVE)
            s_far = jnp.where(far_ok, dot_nt(stacked, far_keys), NEGATIVE)
            near_top = jnp.maximum(jnp.maximum(s_left, s_mid), s_right)
            far_top = jnp.maximum(s_far[:, :128], s_far[:, 128:])
            top = jnp.max(jnp.maximum(near_top, far_top), axis=-1, keepdims=True)
            w_left = jnp.exp(s_left - top)
            w_mid = jnp.exp(s_mid - top)
            w_right = jnp.exp(s_right - top)
            w_far = jnp.exp(s_far - top)
            total = jnp.sum(
                w_left + w_mid + w_right + w_far[:, :128] + w_far[:, 128:], axis=-1, keepdims=True
            )

            def mix(weights, values):
                return jnp.dot(
                    weights.astype(jnp.bfloat16), values, preferred_element_type=jnp.float32
                )

            mixed = mix(w_left, v_left) + mix(w_mid, v_mid) + mix(w_right, v_right) + mix(w_far, far_values)
            mixed = mixed / total
            context = jnp.zeros((TOK, WIDE), jnp.float32)
            for h in range(HEADS_LOCAL):
                context = jnp.where(lane_head == h, mixed[h * TOK : (h + 1) * TOK, :], context)
            mine = jnp.where(x == seg, 0, 1)
            out_ref[mine, part * TOK : (part + 1) * TOK, :] = context.astype(jnp.bfloat16)


def output_kernel(index, own_ref, there_ref, *refs):
    blocks, keep_ref, send_ref = refs[:SHARDS], refs[SHARDS], refs[SHARDS + 1]
    z, core, x = index[0], index[1], index[2]
    own, there = own_ref[...], there_ref[...]
    full = jnp.concatenate([jnp.where(x == 0, own, there), jnp.where(x == 0, there, own)], axis=1)
    for j, (way, hops) in enumerate(STEPS):
        zj = z_of(z, core, way, hops)
        out = dot_nt(full, blocks[j][...])
        keep = jnp.where(core == 0, out[:TOK], out[TOK:])
        sent = jnp.where(core == 0, out[TOK:], out[:TOK]).astype(jnp.bfloat16)
        for side in range(X):
            lanes = pl.ds(pl.multiple_of((side * Z + zj) * 128, 128), 128)
            keep_ref[:, lanes] = keep[:, side * 128 : side * 128 + 128]
            send_ref[:, lanes] = sent[:, side * 128 : side * 128 + 128]


def on_chip(kernel, out_shape, flops, exps, args, scratch=()):
    vmem = pl.BlockSpec(memory_space=pltpu.VMEM)
    return pl.pallas_call(
        kernel,
        out_shape=out_shape,
        in_specs=[pl.BlockSpec(memory_space=pltpu.SMEM)] + [vmem] * (len(args) - 1),
        out_specs=jax.tree.map(lambda _: vmem, out_shape),
        scratch_shapes=list(scratch),
        compiler_params=pltpu.CompilerParams(vmem_limit_bytes=VMEM_LIMIT),
        cost_estimate=pl.CostEstimate(flops=flops, bytes_accessed=4 << 20, transcendentals=exps),
    )(*args)


def after(value, *others):
    return lax.optimization_barrier((value, *others))[0]


def per_device(hidden_in, length, attn_gain, global_gain, w_query, w_key, w_value, w_out):
    width = hidden_in.shape[1]
    me = lax.axis_index("seq")
    core = me & 1
    z = (me >> 1) & (Z - 1)
    x = me >> 4
    limit = length[0]
    bf16 = jnp.bfloat16
    index = jnp.stack([z, core, x, limit]).astype(jnp.int32)

    mine = jnp.stack([w_query.T, w_key.T, w_value.T]).reshape(3, 2, 16, width)
    first = mine[:, 0].reshape(48, width)

    normed = rms_norm(hidden_in.astype(jnp.float32), attn_gain).astype(bf16)
    is_valid = (me * TOK + jnp.arange(TOK, dtype=jnp.int32) < limit).astype(jnp.float32)
    block_sums = jnp.sum(
        (normed.astype(jnp.float32) * is_valid[:, None]).reshape(TOK // BLOCK, BLOCK, width), axis=1
    )
    global_mine = rms_norm(block_sums, global_gain).astype(bf16)
    global_there = send(global_mine, OTHER_X)
    second = jnp.concatenate(
        [
            mine[:, 1].reshape(48, width),
            jnp.where(x == 0, global_mine, global_there),
            jnp.where(x == 0, global_there, global_mine),
        ],
        axis=0,
    )

    one, two = {(0, 0): first}, {(0, 0): second}
    a_one, a_two, b_one, b_two = first, second, first, second
    for step in range(1, 5):
        one[0, step] = a_one = send(a_one, AHEAD)
        if step < 4:
            one[1, step] = b_one = send(b_one, BEHIND)
        two[0, step] = a_two = send(a_two, AHEAD)
        if step < 4:
            two[1, step] = b_two = send(b_two, BEHIND)
    firsts = [one[s] for s in STEPS]
    seconds = [two[s] for s in STEPS]

    to_send = after(normed, one[0, 1])
    across = send(to_send, OTHER_X)
    beside = send(to_send, OTHER_CORE)
    beside_across = send(across, OTHER_CORE)

    g_most = send(jnp.concatenate([s[48:] for s in seconds[:-1]], axis=0), OTHER_CORE)
    g_last = send(seconds[-1][48:], OTHER_CORE)

    half = jax.ShapeDtypeStruct((ROWS, 4 * 128), bf16)
    keep, to_swap = on_chip(
        project_kernel,
        (half, half),
        2 * 768 * 768 * width,
        0,
        (index, normed, across, beside, beside_across, *firsts, *seconds, g_most, g_last),
        (pltpu.VMEM((ROWS, width), bf16), pltpu.VMEM((2 * G_ROWS, width), bf16), pltpu.VMEM((768, width), bf16)),
    )
    got = send(to_swap, OTHER_CORE)

    def edge(part):
        tables = [t.reshape(2, 2, TOK, 512)[:, part, :, 128:384].reshape(2 * TOK, 256) for t in (keep, got)]
        return jnp.concatenate(tables, axis=1)

    below = send(edge(1), UP)
    above = send(edge(0), DOWN)

    deltas = jnp.asarray([-h if w == 0 else h for w, h in STEPS], jnp.int32)
    g_core = jnp.arange(C, dtype=jnp.int32)[:, None, None, None]
    g_z = (z + deltas[None, :, None, None] * (1 - 2 * g_core)) & (Z - 1)
    g_x = jnp.arange(X, dtype=jnp.int32)[None, None, :, None]
    g_k = jnp.arange(8, dtype=jnp.int32)[None, None, None, :]
    far_pos = (((g_x * Z + g_z) * C + g_core) * TOK + g_k * BLOCK).reshape(1, 2 * G_ROWS)
    context = on_chip(
        attention_kernel,
        jax.ShapeDtypeStruct((2, 2 * TOK, WIDE), bf16),
        4 * 4 * TOK * 640 * WIDE * 4,
        4 * 4 * TOK * 640,
        (index, far_pos, keep, got, below, above),
    )

    out_t = after(w_out, one[0, 2]).T.reshape(64, X, 2, HEADS_LOCAL, 2, HALF)
    out_t = jnp.transpose(out_t, (0, 2, 1, 4, 3, 5))
    group_0 = out_t[:, 0].reshape(64, 2 * WIDE)
    group_1 = out_t[:, 1, :, ::-1].reshape(64, 2 * WIDE)
    kept = jnp.where(core == 0, group_0, group_1)
    passed = send(jnp.where(core == 0, group_1, group_0), OTHER_CORE)
    chip = jnp.concatenate([jnp.where(core == 0, kept, passed), jnp.where(core == 0, passed, kept)], axis=0)
    chip_there = send(chip, OTHER_X)
    both = jnp.concatenate([jnp.where(x == 0, chip, chip_there), jnp.where(x == 0, chip_there, chip)], axis=0)
    out_blocks = {(0, 0): both}
    ahead = behind = after(both, two[0, 4], two[1, 3])
    for step in range(1, 5):
        out_blocks[0, step] = ahead = send(ahead, AHEAD)
        if step < 4:
            out_blocks[1, step] = behind = send(behind, BEHIND)

    there = send(context[1], OTHER_X)
    kept_part, sent_part = on_chip(
        output_kernel,
        (jax.ShapeDtypeStruct((TOK, width), jnp.float32), jax.ShapeDtypeStruct((TOK, width), bf16)),
        2 * 256 * 512 * width,
        0,
        (index, context[0], there, *[out_blocks[s] for s in STEPS]),
    )
    return (kept_part + send(sent_part, OTHER_CORE).astype(jnp.float32)).astype(bf16)


def solution(mesh):
    placed = (
        P(("doc", "seq"), None),
        P("doc"),
        P(),
        P(),
        P(None, "seq"),
        P(None, "seq"),
        P(None, "seq"),
        P(None, "seq"),
    )
    return jax.shard_map(
        per_device, mesh=mesh, in_specs=placed, out_specs=P(("doc", "seq"), None), check_vma=False
    )
```

```python
import jax
import jax.numpy as jnp
from jax import lax
from jax.experimental import pallas as pl
from jax.experimental.pallas import tpu as pltpu
from jax.sharding import PartitionSpec as P

HEAD_DIM = 64
BLOCK = 16
RADIUS = 127
NEGATIVE = -1e30
EPSILON = 1e-06

X, Z, C = 2, 8, 2
SEQ_SHARDS = X * Z * C
TOK = 128
HALF = 32
HEADS_LOCAL = 4
WIDE = HEADS_LOCAL * HEAD_DIM


def place(x, z, core):
    return (x * Z + z) * C + core


def pairs(move):
    return [
        (place(x, z, c), place(*move(x, z, c))) for x in range(X) for z in range(Z) for c in range(C)
    ]


OTHER_CORE = pairs(lambda x, z, c: (x, z, 1 - c))
OTHER_X = pairs(lambda x, z, c: (1 - x, z, c))
AHEAD = pairs(lambda x, z, c: (x, (z + (1 if c == 0 else -1)) % Z, c))
BEHIND = pairs(lambda x, z, c: (x, (z - (1 if c == 0 else -1)) % Z, c))
UP = pairs(lambda x, z, c: (x, (z + 1) % Z, c))
DOWN = pairs(lambda x, z, c: (x, (z - 1) % Z, c))


def send(value, route):
    return lax.ppermute(value, "seq", route)


def rms_norm(values, gain_row):
    mean_square = jnp.mean(values * values, axis=-1, keepdims=True)
    return values * lax.rsqrt(mean_square + EPSILON) * gain_row


def dot_nt(left, right):
    return lax.dot_general(
        left, right, (((1,), (1,)), ((), ())), preferred_element_type=jnp.float32
    )


STEPS = ((0, 0), (0, 1), (1, 1), (0, 2), (1, 2), (0, 3), (1, 3), (0, 4))
SHARDS = len(STEPS)
ROWS = 4 * TOK
G_ROWS = Z * 16
VMEM_LIMIT = 48 * 1024 * 1024


def z_of(z, core, way, hops):
    delta = -hops if way == 0 else hops
    return (z + delta * (1 - 2 * core)) & (Z - 1)


def project_kernel(index, *refs):
    blocks, firsts, seconds = refs[:4], refs[4 : 4 + SHARDS], refs[4 + SHARDS : 4 + 2 * SHARDS]
    keep_ref, send_ref, g_rows, far_table, rows, table = refs[4 + 2 * SHARDS :]
    z, core, x = index[0], index[1], index[2]
    low_core = core == 0
    for ref, bx, bc in zip(blocks, (x, 1 - x, x, 1 - x), (core, core, 1 - core, 1 - core)):
        rows[pl.ds(pl.multiple_of((bx * 2 + bc) * TOK, TOK), TOK), :] = ref[...]
    for j, (way, hops) in enumerate(STEPS):
        at = z_of(z, core, way, hops) * HALF
        for kind in range(3):
            into = table if kind == 0 else far_table
            base = 0 if kind == 0 else kind * 256 - 256
            here = pl.multiple_of(base + at, 16)
            into[pl.ds(here, 16), :] = firsts[j][kind * 16 : kind * 16 + 16, :]
            there = pl.multiple_of(base + at + 16, 16)
            into[pl.ds(there, 16), :] = seconds[j][kind * 16 : kind * 16 + 16, :]
        g_rows[j * 16 : j * 16 + 16, :] = seconds[j][48:64, :]
    for kind in range(3):
        columns = table[...] if kind == 0 else far_table[kind * 256 - 256 : kind * 256, :]
        out = dot_nt(rows[...], columns).astype(jnp.bfloat16)
        lanes = slice(kind * 128, kind * 128 + 128)
        keep_ref[:, lanes] = jnp.where(low_core, out[:, :128], out[:, 128:])
        send_ref[:, lanes] = jnp.where(low_core, out[:, 128:], out[:, :128])


def far_kernel(index, own_ref, other_ref, table, keep_ref, send_ref):
    low_core = index[1] == 0
    for source in range(2):
        rows = jnp.where(index[1] == source, own_ref[...], other_ref[...])
        at = slice(source * G_ROWS, source * G_ROWS + G_ROWS)
        for kind in range(2):
            out = dot_nt(rows, table[kind * 256 : kind * 256 + 256, :]).astype(jnp.bfloat16)
            lanes = slice(kind * 128, kind * 128 + 128)
            keep_ref[at, lanes] = jnp.where(low_core, out[:, :128], out[:, 128:])
            send_ref[at, lanes] = jnp.where(low_core, out[:, 128:], out[:, :128])


def attention_kernel(index, far_pos, keep_ref, got_ref, g_keep, g_got, below_ref, above_ref, out_ref):
    z, x, limit = index[0], index[2], index[3]
    lane_head = (lax.broadcasted_iota(jnp.int32, (TOK, WIDE), 1) % 128) // HALF
    row = lax.broadcasted_iota(jnp.int32, (HEADS_LOCAL * TOK, TOK), 0) % TOK
    col = lax.broadcasted_iota(jnp.int32, (HEADS_LOCAL * TOK, TOK), 1)
    far_ok = far_pos[...] < limit
    far_keys = jnp.concatenate([g_keep[:, :128], g_got[:, :128]], axis=1)
    far_values = jnp.concatenate([g_keep[:, 128:], g_got[:, 128:]], axis=1)

    def local(kind, at):
        lanes = slice(kind * 128, kind * 128 + 128)
        return jnp.concatenate([keep_ref[at : at + TOK, lanes], got_ref[at : at + TOK, lanes]], axis=1)

    def halo(ref, kind, seg):
        at = pl.ds(pl.multiple_of(seg * TOK, TOK), TOK)
        lanes = kind * 128 - 128
        return jnp.concatenate([ref[at, lanes : lanes + 128], ref[at, lanes + 256 : lanes + 384]], axis=1)

    for seg in range(2):
        below_seg = jnp.where(z == 0, 1 - seg, seg)
        above_seg = jnp.where(z == Z - 1, 1 - seg, seg)
        for part in range(2):
            base = (seg * Z + z) * 2 * TOK + part * TOK
            at = (seg * 2 + part) * TOK
            queries = local(0, at)
            stacked = jnp.concatenate(
                [jnp.where(lane_head == h, queries, jnp.zeros_like(queries)) for h in range(HEADS_LOCAL)],
                axis=0,
            )

            def neighbours(kind):
                if part == 0:
                    return halo(below_ref, kind, below_seg), local(kind, at), local(kind, at + TOK)
                return local(kind, at - TOK), local(kind, at), halo(above_ref, kind, above_seg)

            k_left, k_mid, k_right = neighbours(1)
            v_left, v_mid, v_right = neighbours(2)
            low = base - TOK
            ok_left = (col > row) & (col + low >= 0) & (col + low < limit)
            ok_mid = col + base < limit
            ok_right = (col < row) & (col + (base + TOK) < limit)
            s_left = jnp.where(ok_left, dot_nt(stacked, k_left), NEGATIVE)
            s_mid = jnp.where(ok_mid, dot_nt(stacked, k_mid), NEGATIVE)
            s_right = jnp.where(ok_right, dot_nt(stacked, k_right), NEGATIVE)
            s_far = jnp.where(far_ok, dot_nt(stacked, far_keys), NEGATIVE)
            near_top = jnp.maximum(jnp.maximum(s_left, s_mid), s_right)
            far_top = jnp.maximum(s_far[:, :128], s_far[:, 128:])
            top = jnp.max(jnp.maximum(near_top, far_top), axis=-1, keepdims=True)
            w_left = jnp.exp(s_left - top)
            w_mid = jnp.exp(s_mid - top)
            w_right = jnp.exp(s_right - top)
            w_far = jnp.exp(s_far - top)
            total = jnp.sum(
                w_left + w_mid + w_right + w_far[:, :128] + w_far[:, 128:], axis=-1, keepdims=True
            )

            def mix(weights, values):
                return jnp.dot(
                    weights.astype(jnp.bfloat16), values, preferred_element_type=jnp.float32
                )

            mixed = mix(w_left, v_left) + mix(w_mid, v_mid) + mix(w_right, v_right) + mix(w_far, far_values)
            mixed = mixed / total
            context = jnp.zeros((TOK, WIDE), jnp.float32)
            for h in range(HEADS_LOCAL):
                context = jnp.where(lane_head == h, mixed[h * TOK : (h + 1) * TOK, :], context)
            mine = jnp.where(x == seg, 0, 1)
            out_ref[mine, part * TOK : (part + 1) * TOK, :] = context.astype(jnp.bfloat16)


def output_kernel(index, own_ref, there_ref, weights, keep_ref, send_ref):
    core, x = index[1], index[2]
    own, there = own_ref[...], there_ref[...]
    full = jnp.concatenate([jnp.where(x == 0, own, there), jnp.where(x == 0, there, own)], axis=1)
    for zj in range(Z):
        out = dot_nt(full, weights[zj * 256 : zj * 256 + 256, :])
        keep = jnp.where(core == 0, out[:TOK], out[TOK:])
        sent = jnp.where(core == 0, out[TOK:], out[:TOK]).astype(jnp.bfloat16)
        for side in range(X):
            at = (side * Z + zj) * 128
            keep_ref[:, at : at + 128] = keep[:, side * 128 : side * 128 + 128]
            send_ref[:, at : at + 128] = sent[:, side * 128 : side * 128 + 128]


def on_chip(kernel, out_shape, flops, exps, args, scratch=()):
    vmem = pl.BlockSpec(memory_space=pltpu.VMEM)
    return pl.pallas_call(
        kernel,
        out_shape=out_shape,
        in_specs=[pl.BlockSpec(memory_space=pltpu.SMEM)] + [vmem] * (len(args) - 1),
        out_specs=jax.tree.map(lambda _: vmem, out_shape),
        scratch_shapes=list(scratch),
        compiler_params=pltpu.CompilerParams(vmem_limit_bytes=VMEM_LIMIT),
        cost_estimate=pl.CostEstimate(flops=flops, bytes_accessed=4 << 20, transcendentals=exps),
    )(*args)


def after(value, *others):
    return lax.optimization_barrier((value, *others))[0]


def per_device(hidden_in, length, attn_gain, global_gain, w_query, w_key, w_value, w_out):
    width = hidden_in.shape[1]
    me = lax.axis_index("seq")
    core = me & 1
    z = (me >> 1) & (Z - 1)
    x = me >> 4
    limit = length[0]
    bf16 = jnp.bfloat16
    index = jnp.stack([z, core, x, limit]).astype(jnp.int32)

    mine = jnp.stack([w_query.T, w_key.T, w_value.T]).reshape(3, 2, 16, width)
    first = mine[:, 0].reshape(48, width)

    normed = rms_norm(hidden_in.astype(jnp.float32), attn_gain).astype(bf16)
    is_valid = (me * TOK + jnp.arange(TOK, dtype=jnp.int32) < limit).astype(jnp.float32)
    block_sums = jnp.sum(
        (normed.astype(jnp.float32) * is_valid[:, None]).reshape(TOK // BLOCK, BLOCK, width), axis=1
    )
    global_mine = rms_norm(block_sums, global_gain).astype(bf16)
    global_there = send(global_mine, OTHER_X)
    second = jnp.concatenate(
        [
            mine[:, 1].reshape(48, width),
            jnp.where(x == 0, global_mine, global_there),
            jnp.where(x == 0, global_there, global_mine),
        ],
        axis=0,
    )

    one, two = {(0, 0): first}, {(0, 0): second}
    a_one, a_two, b_one, b_two = first, second, first, second
    for step in range(1, 5):
        if step > 1:
            before = (two[0, step - 2], two[1, step - 2]) if step > 2 else ()
            a_one, b_one = lax.optimization_barrier((a_one, b_one, *before))[:2]
        one[0, step] = a_one = send(a_one, AHEAD)
        if step < 4:
            one[1, step] = b_one = send(b_one, BEHIND)
        if step > 1:
            a_two, b_two = lax.optimization_barrier((a_two, b_two, one[0, step - 1], one[1, step - 1]))[:2]
        two[0, step] = a_two = send(a_two, AHEAD)
        if step < 4:
            two[1, step] = b_two = send(b_two, BEHIND)
    firsts = [one[s] for s in STEPS]
    seconds = [two[s] for s in STEPS]

    to_send = after(normed, one[0, 1])
    across = send(to_send, OTHER_X)
    beside = send(to_send, OTHER_CORE)
    beside_across = send(across, OTHER_CORE)

    half = jax.ShapeDtypeStruct((ROWS, 3 * 128), bf16)
    keep, to_swap, g_own, far_table = on_chip(
        project_kernel,
        (
            half,
            half,
            jax.ShapeDtypeStruct((G_ROWS, width), bf16),
            jax.ShapeDtypeStruct((2 * Z * HALF, width), bf16),
        ),
        2 * ROWS * 768 * width,
        0,
        (index, normed, across, beside, beside_across, *firsts, *seconds),
        (pltpu.VMEM((ROWS, width), bf16), pltpu.VMEM((Z * HALF, width), bf16)),
    )
    got = send(to_swap, OTHER_CORE)
    g_other = send(g_own, OTHER_CORE)

    def edge(part):
        tables = [t.reshape(2, 2, TOK, 384)[:, part, :, 128:384].reshape(2 * TOK, 256) for t in (keep, got)]
        return jnp.concatenate(tables, axis=1)

    below = send(edge(1), UP)
    above = send(edge(0), DOWN)

    far_half = jax.ShapeDtypeStruct((2 * G_ROWS, 256), bf16)
    g_keep, g_swap = on_chip(
        far_kernel, (far_half, far_half), 2 * 256 * 512 * width, 0, (index, g_own, g_other, far_table)
    )
    g_got = send(g_swap, OTHER_CORE)

    deltas = jnp.asarray([-h if w == 0 else h for w, h in STEPS], jnp.int32)
    g_core = jnp.arange(C, dtype=jnp.int32)[:, None, None, None]
    g_z = (z + deltas[None, :, None, None] * (1 - 2 * g_core)) & (Z - 1)
    g_x = jnp.arange(X, dtype=jnp.int32)[None, None, :, None]
    g_k = jnp.arange(8, dtype=jnp.int32)[None, None, None, :]
    far_pos = (((g_x * Z + g_z) * C + g_core) * TOK + g_k * BLOCK).reshape(1, 2 * G_ROWS)
    context = on_chip(
        attention_kernel,
        jax.ShapeDtypeStruct((2, 2 * TOK, WIDE), bf16),
        4 * 4 * TOK * 640 * WIDE * 4,
        4 * 4 * TOK * 640,
        (index, far_pos, keep, got, g_keep, g_got, below, above),
    )

    out_t = after(w_out, one[0, 1]).T.reshape(64, X, 2, HEADS_LOCAL, 2, HALF)
    out_t = jnp.transpose(out_t, (0, 2, 1, 4, 3, 5))
    group_0 = out_t[:, 0].reshape(64, 2 * WIDE)
    group_1 = out_t[:, 1, :, ::-1].reshape(64, 2 * WIDE)
    kept = jnp.where(core == 0, group_0, group_1)
    passed = send(jnp.where(core == 0, group_1, group_0), OTHER_CORE)
    chip = jnp.concatenate([jnp.where(core == 0, kept, passed), jnp.where(core == 0, passed, kept)], axis=0)
    chip_there = send(chip, OTHER_X)
    both = jnp.concatenate([jnp.where(x == 0, chip, chip_there), jnp.where(x == 0, chip_there, chip)], axis=0)
    columns = [[place(i, k, c) for k in range(Z)] for i in range(X) for c in range(C)]
    out_weights = lax.all_gather(both, "seq", axis_index_groups=columns, axis=0, tiled=True)

    there = send(context[1], OTHER_X)
    kept_part, sent_part = on_chip(
        output_kernel,
        (jax.ShapeDtypeStruct((TOK, width), jnp.float32), jax.ShapeDtypeStruct((TOK, width), bf16)),
        2 * 256 * 512 * width,
        0,
        (index, context[0], there, out_weights),
    )
    return (kept_part + send(sent_part, OTHER_CORE).astype(jnp.float32)).astype(bf16)


def solution(mesh):
    placed = (
        P(("doc", "seq"), None),
        P("doc"),
        P(),
        P(),
        P(None, "seq"),
        P(None, "seq"),
        P(None, "seq"),
        P(None, "seq"),
    )
    return jax.shard_map(
        per_device, mesh=mesh, in_specs=placed, out_specs=P(("doc", "seq"), None), check_vma=False
    )
```

```python
import jax
import jax.numpy as jnp
from jax import lax
from jax.experimental import pallas as pl
from jax.experimental.pallas import tpu as pltpu
from jax.sharding import PartitionSpec as P

HEAD_DIM = 64
BLOCK = 16
RADIUS = 127
NEGATIVE = -1e30
EPSILON = 1e-06

X, Z, C = 2, 8, 2
SEQ_SHARDS = X * Z * C
TOK = 128
HALF = 32
HEADS_LOCAL = 4
WIDE = HEADS_LOCAL * HEAD_DIM


def place(x, z, core):
    return (x * Z + z) * C + core


def pairs(move):
    return [
        (place(x, z, c), place(*move(x, z, c))) for x in range(X) for z in range(Z) for c in range(C)
    ]


OTHER_CORE = pairs(lambda x, z, c: (x, z, 1 - c))
OTHER_X = pairs(lambda x, z, c: (1 - x, z, c))
AHEAD = pairs(lambda x, z, c: (x, (z + (1 if c == 0 else -1)) % Z, c))
BEHIND = pairs(lambda x, z, c: (x, (z - (1 if c == 0 else -1)) % Z, c))
UP = pairs(lambda x, z, c: (x, (z + 1) % Z, c))
DOWN = pairs(lambda x, z, c: (x, (z - 1) % Z, c))


def send(value, route):
    return lax.ppermute(value, "seq", route)


def rms_norm(values, gain_row):
    mean_square = jnp.mean(values * values, axis=-1, keepdims=True)
    return values * lax.rsqrt(mean_square + EPSILON) * gain_row


def dot_nt(left, right):
    return lax.dot_general(
        left, right, (((1,), (1,)), ((), ())), preferred_element_type=jnp.float32
    )


STEPS = ((0, 0), (0, 1), (1, 1), (0, 2), (1, 2), (0, 3), (1, 3), (0, 4))
SHARDS = len(STEPS)
ROWS = 4 * TOK
G_ROWS = Z * 16
VMEM_LIMIT = 24 * 1024 * 1024


def z_of(z, core, way, hops):
    delta = -hops if way == 0 else hops
    return (z + delta * (1 - 2 * core)) & (Z - 1)


def project_kernel(index, *refs):
    blocks, firsts, seconds = refs[:4], refs[4 : 4 + SHARDS], refs[4 + SHARDS : 4 + 2 * SHARDS]
    keep_ref, send_ref, g_rows, far_table, rows, table = refs[4 + 2 * SHARDS :]
    z, core, x = index[0], index[1], index[2]
    low_core = core == 0
    for ref, bx, bc in zip(blocks, (x, 1 - x, x, 1 - x), (core, core, 1 - core, 1 - core)):
        rows[pl.ds(pl.multiple_of((bx * 2 + bc) * TOK, TOK), TOK), :] = ref[...]
    for j, (way, hops) in enumerate(STEPS):
        at = z_of(z, core, way, hops) * HALF
        for kind in range(3):
            into = table if kind == 0 else far_table
            base = 0 if kind == 0 else kind * 256 - 256
            here = pl.multiple_of(base + at, 16)
            into[pl.ds(here, 16), :] = firsts[j][kind * 16 : kind * 16 + 16, :]
            there = pl.multiple_of(base + at + 16, 16)
            into[pl.ds(there, 16), :] = seconds[j][kind * 16 : kind * 16 + 16, :]
        g_rows[j * 16 : j * 16 + 16, :] = seconds[j][48:64, :]
    for kind in range(3):
        columns = table[...] if kind == 0 else far_table[kind * 256 - 256 : kind * 256, :]
        out = dot_nt(rows[...], columns).astype(jnp.bfloat16)
        lanes = slice(kind * 128, kind * 128 + 128)
        keep_ref[:, lanes] = jnp.where(low_core, out[:, :128], out[:, 128:])
        send_ref[:, lanes] = jnp.where(low_core, out[:, 128:], out[:, :128])


def far_kernel(index, own_ref, other_ref, table, keep_ref, send_ref):
    low_core = index[1] == 0
    for source in range(2):
        rows = jnp.where(index[1] == source, own_ref[...], other_ref[...])
        at = slice(source * G_ROWS, source * G_ROWS + G_ROWS)
        for kind in range(2):
            out = dot_nt(rows, table[kind * 256 : kind * 256 + 256, :]).astype(jnp.bfloat16)
            lanes = slice(kind * 128, kind * 128 + 128)
            keep_ref[at, lanes] = jnp.where(low_core, out[:, :128], out[:, 128:])
            send_ref[at, lanes] = jnp.where(low_core, out[:, 128:], out[:, :128])


def attention_kernel(index, far_pos, keep_ref, got_ref, g_keep, g_got, below_ref, above_ref, out_ref):
    z, x, limit = index[0], index[2], index[3]
    lane_head = (lax.broadcasted_iota(jnp.int32, (TOK, WIDE), 1) % 128) // HALF
    row = lax.broadcasted_iota(jnp.int32, (HEADS_LOCAL * TOK, TOK), 0) % TOK
    col = lax.broadcasted_iota(jnp.int32, (HEADS_LOCAL * TOK, TOK), 1)
    far_ok = far_pos[...] < limit
    far_keys = jnp.concatenate([g_keep[:, :128], g_got[:, :128]], axis=1)
    far_values = jnp.concatenate([g_keep[:, 128:], g_got[:, 128:]], axis=1)

    def local(kind, at):
        lanes = slice(kind * 128, kind * 128 + 128)
        return jnp.concatenate([keep_ref[at : at + TOK, lanes], got_ref[at : at + TOK, lanes]], axis=1)

    def halo(ref, kind, seg):
        at = pl.ds(pl.multiple_of(seg * TOK, TOK), TOK)
        lanes = kind * 128 - 128
        return jnp.concatenate([ref[at, lanes : lanes + 128], ref[at, lanes + 256 : lanes + 384]], axis=1)

    for seg in range(2):
        below_seg = jnp.where(z == 0, 1 - seg, seg)
        above_seg = jnp.where(z == Z - 1, 1 - seg, seg)
        for part in range(2):
            base = (seg * Z + z) * 2 * TOK + part * TOK
            at = (seg * 2 + part) * TOK
            queries = local(0, at)
            stacked = jnp.concatenate(
                [jnp.where(lane_head == h, queries, jnp.zeros_like(queries)) for h in range(HEADS_LOCAL)],
                axis=0,
            )

            def neighbours(kind):
                if part == 0:
                    return halo(below_ref, kind, below_seg), local(kind, at), local(kind, at + TOK)
                return local(kind, at - TOK), local(kind, at), halo(above_ref, kind, above_seg)

            k_left, k_mid, k_right = neighbours(1)
            v_left, v_mid, v_right = neighbours(2)
            low = base - TOK
            ok_left = (col > row) & (col + low >= 0) & (col + low < limit)
            ok_mid = col + base < limit
            ok_right = (col < row) & (col + (base + TOK) < limit)
            s_left = jnp.where(ok_left, dot_nt(stacked, k_left), NEGATIVE)
            s_mid = jnp.where(ok_mid, dot_nt(stacked, k_mid), NEGATIVE)
            s_right = jnp.where(ok_right, dot_nt(stacked, k_right), NEGATIVE)
            s_far = jnp.where(far_ok, dot_nt(stacked, far_keys), NEGATIVE)
            near_top = jnp.maximum(jnp.maximum(s_left, s_mid), s_right)
            far_top = jnp.maximum(s_far[:, :128], s_far[:, 128:])
            top = jnp.max(jnp.maximum(near_top, far_top), axis=-1, keepdims=True)
            w_left = jnp.exp(s_left - top)
            w_mid = jnp.exp(s_mid - top)
            w_right = jnp.exp(s_right - top)
            w_far = jnp.exp(s_far - top)
            total = jnp.sum(
                w_left + w_mid + w_right + w_far[:, :128] + w_far[:, 128:], axis=-1, keepdims=True
            )

            def mix(weights, values):
                return jnp.dot(
                    weights.astype(jnp.bfloat16), values, preferred_element_type=jnp.float32
                )

            mixed = mix(w_left, v_left) + mix(w_mid, v_mid) + mix(w_right, v_right) + mix(w_far, far_values)
            mixed = mixed / total
            context = jnp.zeros((TOK, WIDE), jnp.float32)
            for h in range(HEADS_LOCAL):
                context = jnp.where(lane_head == h, mixed[h * TOK : (h + 1) * TOK, :], context)
            mine = jnp.where(x == seg, 0, 1)
            out_ref[mine, part * TOK : (part + 1) * TOK, :] = context.astype(jnp.bfloat16)


def output_kernel(index, own_ref, there_ref, *refs):
    blocks, keep_ref, send_ref = refs[:SHARDS], refs[SHARDS], refs[SHARDS + 1]
    z, core, x = index[0], index[1], index[2]
    own, there = own_ref[...], there_ref[...]
    full = jnp.concatenate([jnp.where(x == 0, own, there), jnp.where(x == 0, there, own)], axis=1)
    for j, (way, hops) in enumerate(STEPS):
        zj = z_of(z, core, way, hops)
        out = dot_nt(full, blocks[j][...])
        keep = jnp.where(core == 0, out[:TOK], out[TOK:])
        sent = jnp.where(core == 0, out[TOK:], out[:TOK]).astype(jnp.bfloat16)
        for side in range(X):
            lanes = pl.ds(pl.multiple_of((side * Z + zj) * 128, 128), 128)
            keep_ref[:, lanes] = keep[:, side * 128 : side * 128 + 128]
            send_ref[:, lanes] = sent[:, side * 128 : side * 128 + 128]


def on_chip(kernel, out_shape, flops, exps, args, scratch=()):
    vmem = pl.BlockSpec(memory_space=pltpu.VMEM)
    return pl.pallas_call(
        kernel,
        out_shape=out_shape,
        in_specs=[pl.BlockSpec(memory_space=pltpu.SMEM)] + [vmem] * (len(args) - 1),
        out_specs=jax.tree.map(lambda _: vmem, out_shape),
        scratch_shapes=list(scratch),
        compiler_params=pltpu.CompilerParams(vmem_limit_bytes=VMEM_LIMIT),
        cost_estimate=pl.CostEstimate(flops=flops, bytes_accessed=4 << 20, transcendentals=exps),
    )(*args)


def after(value, *others):
    return lax.optimization_barrier((value, *others))[0]


def per_device(hidden_in, length, attn_gain, global_gain, w_query, w_key, w_value, w_out):
    width = hidden_in.shape[1]
    me = lax.axis_index("seq")
    core = me & 1
    z = (me >> 1) & (Z - 1)
    x = me >> 4
    limit = length[0]
    bf16 = jnp.bfloat16
    index = jnp.stack([z, core, x, limit]).astype(jnp.int32)

    mine = jnp.stack([w_query.T, w_key.T, w_value.T]).reshape(3, 2, 16, width)
    first = mine[:, 0].reshape(48, width)

    normed = rms_norm(hidden_in.astype(jnp.float32), attn_gain).astype(bf16)
    is_valid = (me * TOK + jnp.arange(TOK, dtype=jnp.int32) < limit).astype(jnp.float32)
    block_sums = jnp.sum(
        (normed.astype(jnp.float32) * is_valid[:, None]).reshape(TOK // BLOCK, BLOCK, width), axis=1
    )
    global_mine = rms_norm(block_sums, global_gain).astype(bf16)
    global_there = send(global_mine, OTHER_X)
    second = jnp.concatenate(
        [
            mine[:, 1].reshape(48, width),
            jnp.where(x == 0, global_mine, global_there),
            jnp.where(x == 0, global_there, global_mine),
        ],
        axis=0,
    )

    one, two = {(0, 0): first}, {(0, 0): second}
    a_one, a_two, b_one, b_two = first, second, first, second
    for step in range(1, 5):
        if step > 1:
            before = (two[0, step - 2], two[1, step - 2]) if step > 2 else ()
            a_one, b_one = lax.optimization_barrier((a_one, b_one, *before))[:2]
        one[0, step] = a_one = send(a_one, AHEAD)
        if step < 4:
            one[1, step] = b_one = send(b_one, BEHIND)
        if step > 1:
            a_two, b_two = lax.optimization_barrier((a_two, b_two, one[0, step - 1], one[1, step - 1]))[:2]
        two[0, step] = a_two = send(a_two, AHEAD)
        if step < 4:
            two[1, step] = b_two = send(b_two, BEHIND)
    firsts = [one[s] for s in STEPS]
    seconds = [two[s] for s in STEPS]

    to_send = after(normed, one[0, 1])
    across = send(to_send, OTHER_X)
    beside = send(to_send, OTHER_CORE)
    beside_across = send(across, OTHER_CORE)

    half = jax.ShapeDtypeStruct((ROWS, 3 * 128), bf16)
    keep, to_swap, g_own, far_table = on_chip(
        project_kernel,
        (
            half,
            half,
            jax.ShapeDtypeStruct((G_ROWS, width), bf16),
            jax.ShapeDtypeStruct((2 * Z * HALF, width), bf16),
        ),
        2 * ROWS * 768 * width,
        0,
        (index, normed, across, beside, beside_across, *firsts, *seconds),
        (pltpu.VMEM((ROWS, width), bf16), pltpu.VMEM((Z * HALF, width), bf16)),
    )
    got = send(to_swap, OTHER_CORE)
    g_other = send(g_own, OTHER_CORE)

    def edge(part):
        tables = [t.reshape(2, 2, TOK, 384)[:, part, :, 128:384].reshape(2 * TOK, 256) for t in (keep, got)]
        return jnp.concatenate(tables, axis=1)

    low_edge, high_edge = edge(0), edge(1)
    below = send(high_edge, UP)
    above = send(low_edge, DOWN)

    far_half = jax.ShapeDtypeStruct((2 * G_ROWS, 256), bf16)
    g_keep, g_swap = on_chip(
        far_kernel, (far_half, far_half), 2 * 256 * 512 * width, 0, (index, g_own, g_other, far_table)
    )
    g_got = send(g_swap, OTHER_CORE)

    deltas = jnp.asarray([-h if w == 0 else h for w, h in STEPS], jnp.int32)
    g_core = jnp.arange(C, dtype=jnp.int32)[:, None, None, None]
    g_z = (z + deltas[None, :, None, None] * (1 - 2 * g_core)) & (Z - 1)
    g_x = jnp.arange(X, dtype=jnp.int32)[None, None, :, None]
    g_k = jnp.arange(8, dtype=jnp.int32)[None, None, None, :]
    far_pos = (((g_x * Z + g_z) * C + g_core) * TOK + g_k * BLOCK).reshape(1, 2 * G_ROWS)
    context = on_chip(
        attention_kernel,
        jax.ShapeDtypeStruct((2, 2 * TOK, WIDE), bf16),
        4 * 4 * TOK * 640 * WIDE * 4,
        4 * 4 * TOK * 640,
        (index, far_pos, keep, got, g_keep, g_got, below, above),
    )

    out_t = after(w_out, two[0, 1], two[1, 1]).T.reshape(64, X, 2, HEADS_LOCAL, 2, HALF)
    out_t = jnp.transpose(out_t, (0, 2, 1, 4, 3, 5))
    group_0 = out_t[:, 0].reshape(64, 2 * WIDE)
    group_1 = out_t[:, 1, :, ::-1].reshape(64, 2 * WIDE)
    kept = jnp.where(core == 0, group_0, group_1)
    passed = send(jnp.where(core == 0, group_1, group_0), OTHER_CORE)
    chip = jnp.concatenate([jnp.where(core == 0, kept, passed), jnp.where(core == 0, passed, kept)], axis=0)
    chip_there = send(chip, OTHER_X)
    both = jnp.concatenate([jnp.where(x == 0, chip, chip_there), jnp.where(x == 0, chip_there, chip)], axis=0)
    out_blocks = {(0, 0): both}
    ahead = behind = after(both, one[0, 4], two[0, 4])
    for step in range(1, 5):
        if step == 2:
            ahead, behind = lax.optimization_barrier((ahead, behind, low_edge, high_edge))[:2]
        out_blocks[0, step] = ahead = send(ahead, AHEAD)
        if step < 4:
            out_blocks[1, step] = behind = send(behind, BEHIND)

    there = send(context[1], OTHER_X)
    kept_part, sent_part = on_chip(
        output_kernel,
        (jax.ShapeDtypeStruct((TOK, width), jnp.float32), jax.ShapeDtypeStruct((TOK, width), bf16)),
        2 * 256 * 512 * width,
        0,
        (index, context[0], there, *[out_blocks[s] for s in STEPS]),
    )
    return (kept_part + send(sent_part, OTHER_CORE).astype(jnp.float32)).astype(bf16)


def solution(mesh):
    placed = (
        P(("doc", "seq"), None),
        P("doc"),
        P(),
        P(),
        P(None, "seq"),
        P(None, "seq"),
        P(None, "seq"),
        P(None, "seq"),
    )
    return jax.shard_map(
        per_device, mesh=mesh, in_specs=placed, out_specs=P(("doc", "seq"), None), check_vma=False
    )
```

```python
import jax
import jax.numpy as jnp
from jax import lax
from jax.experimental import pallas as pl
from jax.experimental.pallas import tpu as pltpu
from jax.sharding import PartitionSpec as P

HEAD_DIM = 64
BLOCK = 16
RADIUS = 127
NEGATIVE = -1e30
EPSILON = 1e-06

X, Z, C = 2, 8, 2
SEQ_SHARDS = X * Z * C
TOK = 128
HALF = 32
HEADS_LOCAL = 4
WIDE = HEADS_LOCAL * HEAD_DIM


def place(x, z, core):
    return (x * Z + z) * C + core


def pairs(move):
    return [
        (place(x, z, c), place(*move(x, z, c))) for x in range(X) for z in range(Z) for c in range(C)
    ]


OTHER_CORE = pairs(lambda x, z, c: (x, z, 1 - c))
OTHER_X = pairs(lambda x, z, c: (1 - x, z, c))
AHEAD = pairs(lambda x, z, c: (x, (z + (1 if c == 0 else -1)) % Z, c))
BEHIND = pairs(lambda x, z, c: (x, (z - (1 if c == 0 else -1)) % Z, c))
UP = pairs(lambda x, z, c: (x, (z + 1) % Z, c))
DOWN = pairs(lambda x, z, c: (x, (z - 1) % Z, c))


Y = 4
Y_UP = [(d, (d & 4) | ((d + 1) & 3)) for d in range(2 * Y)]
Y_DOWN = [(d, (d & 4) | ((d - 1) & 3)) for d in range(2 * Y)]


def send(value, route, axis="seq"):
    return lax.ppermute(value, axis, route)


def rms_norm(values, gain_row):
    mean_square = jnp.mean(values * values, axis=-1, keepdims=True)
    return values * lax.rsqrt(mean_square + EPSILON) * gain_row


def norm_kernel(index, hidden, gain, global_gain, normed_ref, blocks_ref):
    normed = rms_norm(hidden[...].astype(jnp.float32), gain[...]).astype(jnp.bfloat16)
    normed_ref[...] = normed
    at = index[4] + lax.broadcasted_iota(jnp.int32, (TOK, 1), 0)
    valid = (at < index[3]).astype(jnp.float32)
    kept = (normed.astype(jnp.float32) * valid).reshape(TOK // BLOCK, BLOCK, normed.shape[1])
    blocks_ref[...] = rms_norm(jnp.sum(kept, axis=1), global_gain[...]).astype(jnp.bfloat16)


def dot_nt(left, right):
    return lax.dot_general(
        left, right, (((1,), (1,)), ((), ())), preferred_element_type=jnp.float32
    )


STEPS = ((0, 0), (0, 1), (1, 1), (0, 2), (1, 2), (0, 3), (1, 3), (0, 4))
SHARDS = len(STEPS)
ROWS = 4 * TOK
G_ROWS = Z * 16
VMEM_LIMIT = 32 * 1024 * 1024


def z_of(z, core, way, hops):
    delta = -hops if way == 0 else hops
    return (z + delta * (1 - 2 * core)) & (Z - 1)


def project_kernel(index, *refs):
    blocks, firsts, seconds = refs[:4], refs[4 : 4 + SHARDS], refs[4 + SHARDS : 4 + 2 * SHARDS]
    keep_ref, send_ref, g_rows, far_table, out_rows, rows, table, sems = refs[4 + 2 * SHARDS :]
    z, core, x = index[0], index[1], index[2]
    low_core = core == 0
    copies = []
    for i, (ref, bx, bc) in enumerate(zip(blocks, (x, 1 - x, x, 1 - x), (core, core, 1 - core, 1 - core))):
        into = rows.at[pl.ds(pl.multiple_of((bx * 2 + bc) * TOK, TOK), TOK), :]
        copies.append(pltpu.make_async_copy(ref, into, sems.at[i]))
        copies[-1].start()
    for j, (way, hops) in enumerate(STEPS):
        at = z_of(z, core, way, hops) * HALF
        for kind in range(3):
            into = table if kind == 0 else far_table
            base = 0 if kind == 0 else kind * 256 - 256
            here = pl.multiple_of(base + at, 16)
            into[pl.ds(here, 16), :] = firsts[j][kind * 16 : kind * 16 + 16, :]
            there = pl.multiple_of(base + at + 16, 16)
            into[pl.ds(there, 16), :] = seconds[j][kind * 16 : kind * 16 + 16, :]
        g_rows[j * 16 : j * 16 + 16, :] = seconds[j][48:64, :]
        out_rows[j * 16 : j * 16 + 16, :] = seconds[j][64:80, :]
    for copy in copies:
        copy.wait()
    for kind in range(3):
        columns = table[...] if kind == 0 else far_table[kind * 256 - 256 : kind * 256, :]
        out = dot_nt(rows[...], columns).astype(jnp.bfloat16)
        lanes = slice(kind * 128, kind * 128 + 128)
        keep_ref[:, lanes] = jnp.where(low_core, out[:, :128], out[:, 128:])
        send_ref[:, lanes] = jnp.where(low_core, out[:, 128:], out[:, :128])


def far_kernel(index, own_ref, other_ref, table, keep_ref, send_ref):
    low_core = index[1] == 0
    for source in range(2):
        rows = jnp.where(index[1] == source, own_ref[...], other_ref[...])
        at = slice(source * G_ROWS, source * G_ROWS + G_ROWS)
        for kind in range(2):
            out = dot_nt(rows, table[kind * 256 : kind * 256 + 256, :]).astype(jnp.bfloat16)
            lanes = slice(kind * 128, kind * 128 + 128)
            keep_ref[at, lanes] = jnp.where(low_core, out[:, :128], out[:, 128:])
            send_ref[at, lanes] = jnp.where(low_core, out[:, 128:], out[:, :128])


def edge_kernel(keep_ref, got_ref, low_ref, high_ref):
    for seg in range(2):
        into = slice(seg * TOK, seg * TOK + TOK)
        for part, out in ((0, low_ref), (1, high_ref)):
            at = slice((seg * 2 + part) * TOK, (seg * 2 + part + 1) * TOK)
            out[into, :256] = keep_ref[at, 128:]
            out[into, 256:] = got_ref[at, 128:]


def attention_kernel(index, keep_ref, got_ref, g_keep, g_got, below_ref, above_ref, out_ref):
    z, x, limit = index[0], index[2], index[3]
    lane_head = (lax.broadcasted_iota(jnp.int32, (TOK, WIDE), 1) % 128) // HALF
    row = lax.broadcasted_iota(jnp.int32, (HEADS_LOCAL * TOK, TOK), 0) % TOK
    col = lax.broadcasted_iota(jnp.int32, (HEADS_LOCAL * TOK, TOK), 1)
    far = lax.broadcasted_iota(jnp.int32, (1, 2 * G_ROWS), 1)
    far_core, j, far_x, far_k = far >> 7, (far >> 4) & 7, (far >> 3) & 1, far & 7
    delta = jnp.where((j & 1) == 1, -((j + 1) >> 1), j >> 1)
    far_z = (z + delta * (1 - 2 * far_core)) & (Z - 1)
    far_ok = ((far_x * Z + far_z) * C + far_core) * TOK + far_k * BLOCK < limit
    far_keys = jnp.concatenate([g_keep[:, :128], g_got[:, :128]], axis=1)
    far_values = jnp.concatenate([g_keep[:, 128:], g_got[:, 128:]], axis=1)

    def local(kind, at):
        lanes = slice(kind * 128, kind * 128 + 128)
        return jnp.concatenate([keep_ref[at : at + TOK, lanes], got_ref[at : at + TOK, lanes]], axis=1)

    def halo(ref, kind, seg):
        at = pl.ds(pl.multiple_of(seg * TOK, TOK), TOK)
        lanes = kind * 128 - 128
        return jnp.concatenate([ref[at, lanes : lanes + 128], ref[at, lanes + 256 : lanes + 384]], axis=1)

    for seg in range(2):
        below_seg = jnp.where(z == 0, 1 - seg, seg)
        above_seg = jnp.where(z == Z - 1, 1 - seg, seg)
        for part in range(2):
            base = (seg * Z + z) * 2 * TOK + part * TOK
            at = (seg * 2 + part) * TOK
            queries = local(0, at)
            stacked = jnp.concatenate(
                [jnp.where(lane_head == h, queries, jnp.zeros_like(queries)) for h in range(HEADS_LOCAL)],
                axis=0,
            )

            def neighbours(kind):
                if part == 0:
                    return halo(below_ref, kind, below_seg), local(kind, at), local(kind, at + TOK)
                return local(kind, at - TOK), local(kind, at), halo(above_ref, kind, above_seg)

            k_left, k_mid, k_right = neighbours(1)
            v_left, v_mid, v_right = neighbours(2)
            low = base - TOK
            ok_left = (col > row) & (col + low >= 0) & (col + low < limit)
            ok_mid = col + base < limit
            ok_right = (col < row) & (col + (base + TOK) < limit)
            s_left = jnp.where(ok_left, dot_nt(stacked, k_left), NEGATIVE)
            s_mid = jnp.where(ok_mid, dot_nt(stacked, k_mid), NEGATIVE)
            s_right = jnp.where(ok_right, dot_nt(stacked, k_right), NEGATIVE)
            s_far = jnp.where(far_ok, dot_nt(stacked, far_keys), NEGATIVE)
            near_top = jnp.maximum(jnp.maximum(s_left, s_mid), s_right)
            far_top = jnp.maximum(s_far[:, :128], s_far[:, 128:])
            top = jnp.max(jnp.maximum(near_top, far_top), axis=-1, keepdims=True)
            w_left = jnp.exp(s_left - top)
            w_mid = jnp.exp(s_mid - top)
            w_right = jnp.exp(s_right - top)
            w_far = jnp.exp(s_far - top)
            total = jnp.sum(
                w_left + w_mid + w_right + w_far[:, :128] + w_far[:, 128:], axis=-1, keepdims=True
            )

            def mix(weights, values):
                return jnp.dot(
                    weights.astype(jnp.bfloat16), values, preferred_element_type=jnp.float32
                )

            mixed = mix(w_left, v_left) + mix(w_mid, v_mid) + mix(w_right, v_right) + mix(w_far, far_values)
            mixed = mixed / total
            context = jnp.zeros((TOK, WIDE), jnp.float32)
            for h in range(HEADS_LOCAL):
                context = jnp.where(lane_head == h, mixed[h * TOK : (h + 1) * TOK, :], context)
            mine = jnp.where(x == seg, 0, 1)
            out_ref[mine, part * TOK : (part + 1) * TOK, :] = context.astype(jnp.bfloat16)


def output_kernel(index, own_ref, there_ref, mine, prev, nxt, far_a, far_b, keep_ref, send_ref, table):
    z, core, x, y = index[0], index[1], index[2], index[5]
    own, there = own_ref[...], there_ref[...]
    for side in range(X):
        mixed = jnp.where(x == side, own, there)
        table[2 * side] = mixed[:, :128]
        table[2 * side + 1] = mixed[:, 128:]
    full = jnp.concatenate([table[(y + turn) & 3] for turn in (0, 3, 1, 2)], axis=1)
    for j, (way, hops) in enumerate(STEPS):
        zj = z_of(z, core, way, hops)
        here = j * 16
        far = (far_a, here) if j < 4 else (far_b, here - 64)
        weights = [
            ref[at : at + 16, i * 256 : i * 256 + 256]
            for ref, at in ((mine, here), (prev, here), (nxt, here), far)
            for i in range(8)
        ]
        out = jnp.dot(full, jnp.concatenate(weights, axis=0), preferred_element_type=jnp.float32)
        keep = jnp.where(core == 0, out[:TOK], out[TOK:])
        sent = jnp.where(core == 0, out[TOK:], out[:TOK]).astype(jnp.bfloat16)
        for side in range(X):
            lanes = pl.ds(pl.multiple_of((side * Z + zj) * 128, 128), 128)
            keep_ref[:, lanes] = keep[:, side * 128 : side * 128 + 128]
            send_ref[:, lanes] = sent[:, side * 128 : side * 128 + 128]


def on_chip(kernel, out_shape, flops, exps, args, scratch=(), in_hbm=0):
    vmem = pl.BlockSpec(memory_space=pltpu.VMEM)
    specs = [pl.BlockSpec(memory_space=pltpu.SMEM)] + [pl.BlockSpec(memory_space=pltpu.HBM)] * in_hbm
    specs += [vmem] * (len(args) - len(specs))
    return pl.pallas_call(
        kernel,
        out_shape=out_shape,
        in_specs=specs,
        out_specs=jax.tree.map(lambda _: vmem, out_shape),
        scratch_shapes=list(scratch),
        compiler_params=pltpu.CompilerParams(vmem_limit_bytes=VMEM_LIMIT),
        cost_estimate=pl.CostEstimate(flops=flops, bytes_accessed=4 << 20, transcendentals=exps),
    )(*args)


def after(value, *others):
    return lax.optimization_barrier((value, *others))[0]


def per_device(hidden_in, length, attn_gain, global_gain, w_query, w_key, w_value, w_out):
    width = hidden_in.shape[1]
    me = lax.axis_index("seq")
    core = me & 1
    z = (me >> 1) & (Z - 1)
    x = me >> 4
    limit = length[0]
    bf16 = jnp.bfloat16
    y = lax.axis_index("doc") & (Y - 1)
    index = jnp.stack([z, core, x, limit, me * TOK, y]).astype(jnp.int32)

    mine = jnp.stack([w_query.T, w_key.T, w_value.T]).reshape(3, 2, 16, width)
    first = mine[:, 0].reshape(48, width)

    normed, global_mine = on_chip(
        norm_kernel,
        (jax.ShapeDtypeStruct((TOK, width), bf16), jax.ShapeDtypeStruct((TOK // BLOCK, width), bf16)),
        8 * TOK * width,
        0,
        (index, hidden_in, attn_gain[None], global_gain[None]),
    )
    global_there = send(global_mine, OTHER_X)

    split = w_out.reshape(X, 2, HEADS_LOCAL, 2, HALF, 64)

    def slab(group):
        at = (y >> 1, group, 0, (y & 1) ^ group, 0, 0)
        return lax.dynamic_slice(split, at, (1, 1, HEADS_LOCAL, 1, HALF, 64)).reshape(128, 64)

    kept = slab(core)
    passed = send(slab(1 - core), OTHER_CORE)
    chip = jnp.concatenate([jnp.where(core == 0, kept, passed), jnp.where(core == 0, passed, kept)], axis=1)
    chip_there = send(chip, OTHER_X)
    both = jnp.concatenate([jnp.where(x == 0, chip, chip_there), jnp.where(x == 0, chip_there, chip)], axis=1)

    second = jnp.concatenate(
        [
            mine[:, 1].reshape(48, width),
            jnp.where(x == 0, global_mine, global_there),
            jnp.where(x == 0, global_there, global_mine),
            jnp.concatenate([both[i * 16 : i * 16 + 16] for i in range(8)], axis=1),
        ],
        axis=0,
    )

    one, two = {(0, 0): first}, {(0, 0): second}
    a_one, a_two, b_one, b_two = first, second, first, second
    for step in range(1, 5):
        if step > 1:
            before = (two[0, step - 2], two[1, step - 2]) if step > 2 else ()
            a_one, b_one = lax.optimization_barrier((a_one, b_one, *before))[:2]
        one[0, step] = a_one = send(a_one, AHEAD)
        if step < 4:
            one[1, step] = b_one = send(b_one, BEHIND)
        if step > 1:
            a_two, b_two = lax.optimization_barrier((a_two, b_two, one[0, step - 1], one[1, step - 1]))[:2]
        two[0, step] = a_two = send(a_two, AHEAD)
        if step < 4:
            two[1, step] = b_two = send(b_two, BEHIND)
    firsts = [one[s] for s in STEPS]
    seconds = [two[s] for s in STEPS]

    to_send = after(normed, one[0, 1])
    across = send(to_send, OTHER_X)
    beside = send(to_send, OTHER_CORE)
    beside_across = send(across, OTHER_CORE)

    half = jax.ShapeDtypeStruct((ROWS, 3 * 128), bf16)
    keep, to_swap, g_own, far_table, out_own = on_chip(
        project_kernel,
        (
            half,
            half,
            jax.ShapeDtypeStruct((G_ROWS, width), bf16),
            jax.ShapeDtypeStruct((2 * Z * HALF, width), bf16),
            jax.ShapeDtypeStruct((128, width), bf16),
        ),
        2 * ROWS * 768 * width,
        0,
        (index, normed, across, beside, beside_across, *firsts, *seconds),
        (pltpu.VMEM((ROWS, width), bf16), pltpu.VMEM((Z * HALF, width), bf16), pltpu.SemaphoreType.DMA((4,))),
        in_hbm=4,
    )
    got = send(to_swap, OTHER_CORE)
    g_other = send(g_own, OTHER_CORE)

    vmem = pl.BlockSpec(memory_space=pltpu.VMEM)
    edge_shape = jax.ShapeDtypeStruct((2 * TOK, 512), bf16)
    low_edge, high_edge = pl.pallas_call(
        edge_kernel, out_shape=(edge_shape, edge_shape), in_specs=[vmem] * 2, out_specs=(vmem, vmem)
    )(keep, got)
    below = send(high_edge, UP)
    above = send(low_edge, DOWN)

    far_half = jax.ShapeDtypeStruct((2 * G_ROWS, 256), bf16)
    g_keep, g_swap = on_chip(
        far_kernel, (far_half, far_half), 2 * 256 * 512 * width, 0, (index, g_own, g_other, far_table)
    )
    g_got = send(g_swap, OTHER_CORE)

    to_pass = after(out_own, low_edge, high_edge)
    out_prev = send(to_pass, Y_UP, "doc")
    out_next = send(to_pass, Y_DOWN, "doc")
    out_far_a = send(out_prev[:64], Y_UP, "doc")
    out_far_b = send(out_next[64:], Y_DOWN, "doc")

    context = on_chip(
        attention_kernel,
        jax.ShapeDtypeStruct((2, 2 * TOK, WIDE), bf16),
        4 * 4 * TOK * 640 * WIDE * 4,
        4 * 4 * TOK * 640,
        (index, keep, got, g_keep, g_got, below, above),
    )

    there = send(context[1], OTHER_X)
    kept_part, sent_part = on_chip(
        output_kernel,
        (jax.ShapeDtypeStruct((TOK, width), jnp.float32), jax.ShapeDtypeStruct((TOK, width), bf16)),
        2 * 256 * 512 * width,
        0,
        (index, context[0], there, out_own, out_prev, out_next, out_far_a, out_far_b),
        (pltpu.VMEM((4, 2 * TOK, 128), bf16),),
    )
    return (kept_part + send(sent_part, OTHER_CORE).astype(jnp.float32)).astype(bf16)


def solution(mesh):
    placed = (
        P(("doc", "seq"), None),
        P("doc"),
        P(),
        P(),
        P(None, "seq"),
        P(None, "seq"),
        P(None, "seq"),
        P(None, "seq"),
    )
    return jax.shard_map(
        per_device, mesh=mesh, in_specs=placed, out_specs=P(("doc", "seq"), None), check_vma=False
    )
```

```python
import jax
import jax.numpy as jnp
from jax import lax
from jax.experimental import pallas as pl
from jax.experimental.pallas import tpu as pltpu
from jax.sharding import PartitionSpec as P

HEAD_DIM = 64
BLOCK = 16
RADIUS = 127
NEGATIVE = -1e30
EPSILON = 1e-06

X, Z, C = 2, 8, 2
SEQ_SHARDS = X * Z * C
TOK = 128
HALF = 32
HEADS_LOCAL = 4
WIDE = HEADS_LOCAL * HEAD_DIM


def place(x, z, core):
    return (x * Z + z) * C + core


def pairs(move):
    return [
        (place(x, z, c), place(*move(x, z, c))) for x in range(X) for z in range(Z) for c in range(C)
    ]


OTHER_CORE = pairs(lambda x, z, c: (x, z, 1 - c))
OTHER_X = pairs(lambda x, z, c: (1 - x, z, c))
AHEAD = pairs(lambda x, z, c: (x, (z + (1 if c == 0 else -1)) % Z, c))
BEHIND = pairs(lambda x, z, c: (x, (z - (1 if c == 0 else -1)) % Z, c))
UP = pairs(lambda x, z, c: (x, (z + 1) % Z, c))
DOWN = pairs(lambda x, z, c: (x, (z - 1) % Z, c))


Y = 4
Y_UP = [(d, (d & 4) | ((d + 1) & 3)) for d in range(2 * Y)]
Y_DOWN = [(d, (d & 4) | ((d - 1) & 3)) for d in range(2 * Y)]


UP_CROSS = pairs(lambda x, z, c: (x, (z + 1) % Z, 1 - c))
DOWN_CROSS = pairs(lambda x, z, c: (x, (z - 1) % Z, 1 - c))


def send(value, route, axis="seq"):
    return lax.ppermute(value, axis, route)


def rms_norm(values, gain_row):
    mean_square = jnp.mean(values * values, axis=-1, keepdims=True)
    return values * lax.rsqrt(mean_square + EPSILON) * gain_row


def norm_kernel(index, hidden_in, gain_in, global_in, normed_ref, blocks_ref, hidden, gain, global_gain, sems):
    copies = [
        pltpu.make_async_copy(source, into, sems.at[i])
        for i, (source, into) in enumerate(((hidden_in, hidden), (gain_in, gain), (global_in, global_gain)))
    ]
    for copy in copies:
        copy.start()
    for copy in copies:
        copy.wait()
    normed = rms_norm(hidden[...].astype(jnp.float32), gain[...]).astype(jnp.bfloat16)
    normed_ref[...] = normed
    at = index[4] + lax.broadcasted_iota(jnp.int32, (TOK, 1), 0)
    valid = (at < index[3]).astype(jnp.float32)
    kept = (normed.astype(jnp.float32) * valid).reshape(TOK // BLOCK, BLOCK, normed.shape[1])
    blocks_ref[...] = rms_norm(jnp.sum(kept, axis=1), global_gain[...]).astype(jnp.bfloat16)


def dot_nt(left, right):
    return lax.dot_general(
        left, right, (((1,), (1,)), ((), ())), preferred_element_type=jnp.float32
    )


STEPS = ((0, 0), (0, 1), (1, 1), (0, 2), (1, 2), (0, 3), (1, 3), (0, 4))
SHARDS = len(STEPS)
ROWS = 4 * TOK
G_ROWS = Z * 16
VMEM_LIMIT = 32 * 1024 * 1024


def z_of(z, core, way, hops):
    delta = -hops if way == 0 else hops
    return (z + delta * (1 - 2 * core)) & (Z - 1)


def project_kernel(index, *refs):
    blocks, firsts, seconds = refs[:4], refs[4 : 4 + SHARDS], refs[4 + SHARDS : 4 + 2 * SHARDS]
    keep_ref, send_ref, g_rows, far_table, out_rows, *edges, rows, table, sems = refs[4 + 2 * SHARDS :]
    z, core, x = index[0], index[1], index[2]
    low_core = core == 0
    copies = []
    for i, (ref, bx, bc) in enumerate(zip(blocks, (x, 1 - x, x, 1 - x), (core, core, 1 - core, 1 - core))):
        into = rows.at[pl.ds(pl.multiple_of((bx * 2 + bc) * TOK, TOK), TOK), :]
        copies.append(pltpu.make_async_copy(ref, into, sems.at[i]))
        copies[-1].start()
    for j, (way, hops) in enumerate(STEPS):
        at = z_of(z, core, way, hops) * HALF
        for kind in range(3):
            into = table if kind == 0 else far_table
            base = 0 if kind == 0 else kind * 256 - 256
            here = pl.multiple_of(base + at, 16)
            into[pl.ds(here, 16), :] = firsts[j][kind * 16 : kind * 16 + 16, :]
            there = pl.multiple_of(base + at + 16, 16)
            into[pl.ds(there, 16), :] = seconds[j][kind * 16 : kind * 16 + 16, :]
        g_rows[j * 16 : j * 16 + 16, :] = seconds[j][48:64, :]
        out_rows[j * 16 : j * 16 + 16, :] = seconds[j][64:80, :]
    for copy in copies:
        copy.wait()
    for kind in range(3):
        columns = table[...] if kind == 0 else far_table[kind * 256 - 256 : kind * 256, :]
        out = dot_nt(rows[...], columns).astype(jnp.bfloat16)
        lanes = slice(kind * 128, kind * 128 + 128)
        keep_ref[:, lanes] = jnp.where(low_core, out[:, :128], out[:, 128:])
        send_ref[:, lanes] = jnp.where(low_core, out[:, 128:], out[:, :128])
        if kind:
            lanes_out = slice(kind * 128 - 128, kind * 128)
            for part in range(2):
                for seg in range(2):
                    at = slice((seg * 2 + part) * TOK, (seg * 2 + part + 1) * TOK)
                    into = slice(seg * TOK, seg * TOK + TOK)
                    edges[2 * part][into, lanes_out] = keep_ref[at, lanes]
                    edges[2 * part + 1][into, lanes_out] = send_ref[at, lanes]


def far_kernel(index, own_ref, other_ref, table, keep_ref, send_ref):
    low_core = index[1] == 0
    for source in range(2):
        rows = jnp.where(index[1] == source, own_ref[...], other_ref[...])
        at = slice(source * G_ROWS, source * G_ROWS + G_ROWS)
        for kind in range(2):
            out = dot_nt(rows, table[kind * 256 : kind * 256 + 256, :]).astype(jnp.bfloat16)
            lanes = slice(kind * 128, kind * 128 + 128)
            keep_ref[at, lanes] = jnp.where(low_core, out[:, :128], out[:, 128:])
            send_ref[at, lanes] = jnp.where(low_core, out[:, 128:], out[:, :128])


def attention_kernel(index, keep_ref, got_ref, g_keep, g_got, below_ref, below_got, above_ref, above_got, out_ref):
    z, x, limit = index[0], index[2], index[3]
    lane_head = (lax.broadcasted_iota(jnp.int32, (TOK, WIDE), 1) % 128) // HALF
    row = lax.broadcasted_iota(jnp.int32, (HEADS_LOCAL * TOK, TOK), 0) % TOK
    col = lax.broadcasted_iota(jnp.int32, (HEADS_LOCAL * TOK, TOK), 1)
    far = lax.broadcasted_iota(jnp.int32, (1, 2 * G_ROWS), 1)
    far_core, j, far_x, far_k = far >> 7, (far >> 4) & 7, (far >> 3) & 1, far & 7
    delta = jnp.where((j & 1) == 1, -((j + 1) >> 1), j >> 1)
    far_z = (z + delta * (1 - 2 * far_core)) & (Z - 1)
    far_ok = ((far_x * Z + far_z) * C + far_core) * TOK + far_k * BLOCK < limit
    far_keys = jnp.concatenate([g_keep[:, :128], g_got[:, :128]], axis=1)
    far_values = jnp.concatenate([g_keep[:, 128:], g_got[:, 128:]], axis=1)

    def local(kind, at):
        lanes = slice(kind * 128, kind * 128 + 128)
        return jnp.concatenate([keep_ref[at : at + TOK, lanes], got_ref[at : at + TOK, lanes]], axis=1)

    def halo(ref, got, kind, seg):
        at = pl.ds(pl.multiple_of(seg * TOK, TOK), TOK)
        lanes = slice(kind * 128 - 128, kind * 128)
        return jnp.concatenate([ref[at, lanes], got[at, lanes]], axis=1)

    for seg in range(2):
        below_seg = jnp.where(z == 0, 1 - seg, seg)
        above_seg = jnp.where(z == Z - 1, 1 - seg, seg)
        for part in range(2):
            base = (seg * Z + z) * 2 * TOK + part * TOK
            at = (seg * 2 + part) * TOK
            queries = local(0, at)
            stacked = jnp.concatenate(
                [jnp.where(lane_head == h, queries, jnp.zeros_like(queries)) for h in range(HEADS_LOCAL)],
                axis=0,
            )

            def neighbours(kind):
                if part == 0:
                    return halo(below_ref, below_got, kind, below_seg), local(kind, at), local(kind, at + TOK)
                return local(kind, at - TOK), local(kind, at), halo(above_ref, above_got, kind, above_seg)

            k_left, k_mid, k_right = neighbours(1)
            v_left, v_mid, v_right = neighbours(2)
            low = base - TOK
            ok_left = (col > row) & (col + low >= 0) & (col + low < limit)
            ok_mid = col + base < limit
            ok_right = (col < row) & (col + (base + TOK) < limit)
            s_left = jnp.where(ok_left, dot_nt(stacked, k_left), NEGATIVE)
            s_mid = jnp.where(ok_mid, dot_nt(stacked, k_mid), NEGATIVE)
            s_right = jnp.where(ok_right, dot_nt(stacked, k_right), NEGATIVE)
            s_far = jnp.where(far_ok, dot_nt(stacked, far_keys), NEGATIVE)
            near_top = jnp.maximum(jnp.maximum(s_left, s_mid), s_right)
            far_top = jnp.maximum(s_far[:, :128], s_far[:, 128:])
            top = jnp.max(jnp.maximum(near_top, far_top), axis=-1, keepdims=True)
            w_left = jnp.exp(s_left - top)
            w_mid = jnp.exp(s_mid - top)
            w_right = jnp.exp(s_right - top)
            w_far = jnp.exp(s_far - top)
            total = jnp.sum(
                w_left + w_mid + w_right + w_far[:, :128] + w_far[:, 128:], axis=-1, keepdims=True
            )

            def mix(weights, values):
                return jnp.dot(
                    weights.astype(jnp.bfloat16), values, preferred_element_type=jnp.float32
                )

            mixed = mix(w_left, v_left) + mix(w_mid, v_mid) + mix(w_right, v_right) + mix(w_far, far_values)
            mixed = mixed / total
            context = jnp.zeros((TOK, WIDE), jnp.float32)
            for h in range(HEADS_LOCAL):
                context = jnp.where(lane_head == h, mixed[h * TOK : (h + 1) * TOK, :], context)
            mine = jnp.where(x == seg, 0, 1)
            out_ref[mine, part * TOK : (part + 1) * TOK, :] = context.astype(jnp.bfloat16)


def output_kernel(index, own_ref, there_ref, mine, prev, nxt, far_a, far_b, keep_ref, send_ref, table):
    z, core, x, y = index[0], index[1], index[2], index[5]
    own, there = own_ref[...], there_ref[...]
    for side in range(X):
        mixed = jnp.where(x == side, own, there)
        table[2 * side] = mixed[:, :128]
        table[2 * side + 1] = mixed[:, 128:]
    full = jnp.concatenate([table[(y + turn) & 3] for turn in (0, 3, 1, 2)], axis=1)
    for j, (way, hops) in enumerate(STEPS):
        zj = z_of(z, core, way, hops)
        here = j * 16
        far = (far_a, here) if j < 4 else (far_b, here - 64)
        weights = [
            ref[at : at + 16, i * 256 : i * 256 + 256]
            for ref, at in ((mine, here), (prev, here), (nxt, here), far)
            for i in range(8)
        ]
        out = jnp.dot(full, jnp.concatenate(weights, axis=0), preferred_element_type=jnp.float32)
        keep = jnp.where(core == 0, out[:TOK], out[TOK:])
        sent = jnp.where(core == 0, out[TOK:], out[:TOK]).astype(jnp.bfloat16)
        for side in range(X):
            lanes = pl.ds(pl.multiple_of((side * Z + zj) * 128, 128), 128)
            keep_ref[:, lanes] = keep[:, side * 128 : side * 128 + 128]
            send_ref[:, lanes] = sent[:, side * 128 : side * 128 + 128]


def on_chip(kernel, out_shape, flops, exps, args, scratch=(), in_hbm=0):
    vmem = pl.BlockSpec(memory_space=pltpu.VMEM)
    specs = [pl.BlockSpec(memory_space=pltpu.SMEM)] + [pl.BlockSpec(memory_space=pltpu.HBM)] * in_hbm
    specs += [vmem] * (len(args) - len(specs))
    return pl.pallas_call(
        kernel,
        out_shape=out_shape,
        in_specs=specs,
        out_specs=jax.tree.map(lambda _: vmem, out_shape),
        scratch_shapes=list(scratch),
        compiler_params=pltpu.CompilerParams(vmem_limit_bytes=VMEM_LIMIT),
        cost_estimate=pl.CostEstimate(flops=flops, bytes_accessed=4 << 20, transcendentals=exps),
    )(*args)


def after(value, *others):
    return lax.optimization_barrier((value, *others))[0]


def per_device(hidden_in, length, attn_gain, global_gain, w_query, w_key, w_value, w_out):
    width = hidden_in.shape[1]
    me = lax.axis_index("seq")
    core = me & 1
    z = (me >> 1) & (Z - 1)
    x = me >> 4
    limit = length[0]
    bf16 = jnp.bfloat16
    y = lax.axis_index("doc") & (Y - 1)
    index = jnp.stack([z, core, x, limit, me * TOK, y]).astype(jnp.int32)

    mine = jnp.stack([w_query.T, w_key.T, w_value.T]).reshape(3, 2, 16, width)
    first = mine[:, 0].reshape(48, width)

    normed, global_mine = on_chip(
        norm_kernel,
        (jax.ShapeDtypeStruct((TOK, width), bf16), jax.ShapeDtypeStruct((TOK // BLOCK, width), bf16)),
        8 * TOK * width,
        0,
        (index, after(hidden_in, first), attn_gain[None], global_gain[None]),
        (
            pltpu.VMEM((TOK, width), bf16),
            pltpu.VMEM((1, width), jnp.float32),
            pltpu.VMEM((1, width), jnp.float32),
            pltpu.SemaphoreType.DMA((3,)),
        ),
        in_hbm=3,
    )
    global_there = send(global_mine, OTHER_X)

    split = after(w_out, first).reshape(X, 2, HEADS_LOCAL, 2, HALF, 64)

    def slab(group):
        at = (y >> 1, group, 0, (y & 1) ^ group, 0, 0)
        return lax.dynamic_slice(split, at, (1, 1, HEADS_LOCAL, 1, HALF, 64)).reshape(128, 64)

    kept = slab(core)
    passed = send(slab(1 - core), OTHER_CORE)
    chip = jnp.concatenate([jnp.where(core == 0, kept, passed), jnp.where(core == 0, passed, kept)], axis=1)
    chip_there = send(chip, OTHER_X)
    both = jnp.concatenate([jnp.where(x == 0, chip, chip_there), jnp.where(x == 0, chip_there, chip)], axis=1)

    second = jnp.concatenate(
        [
            mine[:, 1].reshape(48, width),
            jnp.where(x == 0, global_mine, global_there),
            jnp.where(x == 0, global_there, global_mine),
            jnp.concatenate([both[i * 16 : i * 16 + 16] for i in range(8)], axis=1),
        ],
        axis=0,
    )

    one, two = {(0, 0): first}, {(0, 0): second}
    a_one, a_two, b_one, b_two = first, second, first, second
    for step in range(1, 5):
        if step > 1:
            before = (two[0, step - 2], two[1, step - 2]) if step > 2 else ()
            a_one, b_one = lax.optimization_barrier((a_one, b_one, *before))[:2]
        one[0, step] = a_one = send(a_one, AHEAD)
        if step < 4:
            one[1, step] = b_one = send(b_one, BEHIND)
        if step == 1:
            a_two = b_two = after(second, a_one, b_one)
        else:
            a_two, b_two = lax.optimization_barrier((a_two, b_two, one[0, step - 1], one[1, step - 1]))[:2]
        two[0, step] = a_two = send(a_two, AHEAD)
        if step < 4:
            two[1, step] = b_two = send(b_two, BEHIND)
    firsts = [one[s] for s in STEPS]
    seconds = [two[s] for s in STEPS]

    to_send = after(normed, one[0, 1])
    across = send(to_send, OTHER_X)
    beside = send(to_send, OTHER_CORE)
    beside_across = send(across, OTHER_CORE)

    half = jax.ShapeDtypeStruct((ROWS, 3 * 128), bf16)
    keep, to_swap, g_own, far_table, out_own, *edges = on_chip(
        project_kernel,
        (
            half,
            half,
            jax.ShapeDtypeStruct((G_ROWS, width), bf16),
            jax.ShapeDtypeStruct((2 * Z * HALF, width), bf16),
            jax.ShapeDtypeStruct((128, width), bf16),
            *[jax.ShapeDtypeStruct((2 * TOK, 256), bf16)] * 4,
        ),
        2 * ROWS * 768 * width,
        0,
        (index, normed, across, beside, beside_across, *firsts, *seconds),
        (pltpu.VMEM((ROWS, width), bf16), pltpu.VMEM((Z * HALF, width), bf16), pltpu.SemaphoreType.DMA((4,))),
        in_hbm=4,
    )
    got = send(to_swap, OTHER_CORE)
    g_other = send(g_own, OTHER_CORE)

    below = send(edges[2], UP), send(edges[3], UP_CROSS)
    above = send(edges[0], DOWN), send(edges[1], DOWN_CROSS)
    far_half = jax.ShapeDtypeStruct((2 * G_ROWS, 256), bf16)
    g_keep, g_swap = on_chip(
        far_kernel, (far_half, far_half), 2 * 256 * 512 * width, 0, (index, g_own, g_other, far_table)
    )
    g_got = send(g_swap, OTHER_CORE)

    to_pass = after(out_own, got, g_other)
    out_prev = send(to_pass, Y_UP, "doc")
    out_next = send(to_pass, Y_DOWN, "doc")
    out_far_a = send(out_prev[:64], Y_UP, "doc")
    out_far_b = send(out_next[64:], Y_DOWN, "doc")

    context = on_chip(
        attention_kernel,
        jax.ShapeDtypeStruct((2, 2 * TOK, WIDE), bf16),
        4 * 4 * TOK * 640 * WIDE * 4,
        4 * 4 * TOK * 640,
        (index, keep, got, g_keep, g_got, *below, *above),
    )

    there = send(context[1], OTHER_X)
    kept_part, sent_part = on_chip(
        output_kernel,
        (jax.ShapeDtypeStruct((TOK, width), jnp.float32), jax.ShapeDtypeStruct((TOK, width), bf16)),
        2 * 256 * 512 * width,
        0,
        (index, context[0], there, out_own, out_prev, out_next, out_far_a, out_far_b),
        (pltpu.VMEM((4, 2 * TOK, 128), bf16),),
    )
    return (kept_part + send(sent_part, OTHER_CORE).astype(jnp.float32)).astype(bf16)


def solution(mesh):
    placed = (
        P(("doc", "seq"), None),
        P("doc"),
        P(),
        P(),
        P(None, "seq"),
        P(None, "seq"),
        P(None, "seq"),
        P(None, "seq"),
    )
    return jax.shard_map(
        per_device, mesh=mesh, in_specs=placed, out_specs=P(("doc", "seq"), None), check_vma=False
    )
```

```python
import jax
import jax.numpy as jnp
from jax import lax
from jax.experimental import pallas as pl
from jax.experimental.pallas import tpu as pltpu
from jax.sharding import PartitionSpec as P

HEAD_DIM = 64
BLOCK = 16
RADIUS = 127
NEGATIVE = -1e30
EPSILON = 1e-06

X, Z, C = 2, 8, 2
SEQ_SHARDS = X * Z * C
TOK = 128
HALF = 32
HEADS_LOCAL = 4
WIDE = HEADS_LOCAL * HEAD_DIM


def place(x, z, core):
    return (x * Z + z) * C + core


def pairs(move):
    return [
        (place(x, z, c), place(*move(x, z, c))) for x in range(X) for z in range(Z) for c in range(C)
    ]


OTHER_CORE = pairs(lambda x, z, c: (x, z, 1 - c))
OTHER_X = pairs(lambda x, z, c: (1 - x, z, c))
AHEAD = pairs(lambda x, z, c: (x, (z + (1 if c == 0 else -1)) % Z, c))
BEHIND = pairs(lambda x, z, c: (x, (z - (1 if c == 0 else -1)) % Z, c))
UP = pairs(lambda x, z, c: (x, (z + 1) % Z, c))
DOWN = pairs(lambda x, z, c: (x, (z - 1) % Z, c))


Y = 4
Y_UP = [(d, (d & 4) | ((d + 1) & 3)) for d in range(2 * Y)]
Y_DOWN = [(d, (d & 4) | ((d - 1) & 3)) for d in range(2 * Y)]


UP_CROSS = pairs(lambda x, z, c: (x, (z + 1) % Z, 1 - c))
DOWN_CROSS = pairs(lambda x, z, c: (x, (z - 1) % Z, 1 - c))


def send(value, route, axis="seq"):
    return lax.ppermute(value, axis, route)


def rms_norm(values, gain_row):
    mean_square = jnp.mean(values * values, axis=-1, keepdims=True)
    return values * lax.rsqrt(mean_square + EPSILON) * gain_row


def norm_kernel(index, hidden_in, gain_in, global_in, normed_ref, blocks_ref, hidden, gain, global_gain, sems):
    copies = [
        pltpu.make_async_copy(source, into, sems.at[i])
        for i, (source, into) in enumerate(((hidden_in, hidden), (gain_in, gain), (global_in, global_gain)))
    ]
    for copy in copies:
        copy.start()
    for copy in copies:
        copy.wait()
    normed = rms_norm(hidden[...].astype(jnp.float32), gain[...]).astype(jnp.bfloat16)
    normed_ref[...] = normed
    at = index[4] + lax.broadcasted_iota(jnp.int32, (TOK, 1), 0)
    valid = (at < index[3]).astype(jnp.float32)
    kept = (normed.astype(jnp.float32) * valid).reshape(TOK // BLOCK, BLOCK, normed.shape[1])
    blocks_ref[...] = rms_norm(jnp.sum(kept, axis=1), global_gain[...]).astype(jnp.bfloat16)


def dot_nt(left, right):
    return lax.dot_general(
        left, right, (((1,), (1,)), ((), ())), preferred_element_type=jnp.float32
    )


STEPS = ((0, 0), (0, 1), (1, 1), (0, 2), (1, 2), (0, 3), (1, 3), (0, 4))
SHARDS = len(STEPS)
ROWS = 4 * TOK
G_ROWS = Z * 16
VMEM_LIMIT = 32 * 1024 * 1024


def z_of(z, core, way, hops):
    delta = -hops if way == 0 else hops
    return (z + delta * (1 - 2 * core)) & (Z - 1)


def project_kernel(index, *refs):
    blocks, shards = refs[:4], refs[4 : 4 + SHARDS]
    keep_ref, send_ref, far_table, *edges, rows, table, sems = refs[4 + SHARDS :]
    z, core, x = index[0], index[1], index[2]
    low_core = core == 0
    copies = []
    for i, (ref, bx, bc) in enumerate(zip(blocks, (x, 1 - x, x, 1 - x), (core, core, 1 - core, 1 - core))):
        into = rows.at[pl.ds(pl.multiple_of((bx * 2 + bc) * TOK, TOK), TOK), :]
        copies.append(pltpu.make_async_copy(ref, into, sems.at[i]))
        copies[-1].start()
    for j, (way, hops) in enumerate(STEPS):
        at = z_of(z, core, way, hops) * HALF
        for kind in range(3):
            into = table if kind == 0 else far_table
            base = 0 if kind == 0 else kind * 256 - 256
            here = pl.multiple_of(base + at, HALF)
            into[pl.ds(here, HALF), :] = shards[j][kind * HALF : kind * HALF + HALF, :]
    for copy in copies:
        copy.wait()
    for kind in range(3):
        columns = table[...] if kind == 0 else far_table[kind * 256 - 256 : kind * 256, :]
        out = dot_nt(rows[...], columns).astype(jnp.bfloat16)
        lanes = slice(kind * 128, kind * 128 + 128)
        keep_ref[:, lanes] = jnp.where(low_core, out[:, :128], out[:, 128:])
        send_ref[:, lanes] = jnp.where(low_core, out[:, 128:], out[:, :128])
        if kind:
            lanes_out = slice(kind * 128 - 128, kind * 128)
            for part in range(2):
                for seg in range(2):
                    at = slice((seg * 2 + part) * TOK, (seg * 2 + part + 1) * TOK)
                    into = slice(seg * TOK, seg * TOK + TOK)
                    edges[2 * part][into, lanes_out] = keep_ref[at, lanes]
                    edges[2 * part + 1][into, lanes_out] = send_ref[at, lanes]


def collect_kernel(*refs):
    riders, g_rows, out_rows = refs[1 : 1 + SHARDS], refs[1 + SHARDS], refs[2 + SHARDS]
    for j in range(SHARDS):
        g_rows[j * 16 : j * 16 + 16, :] = riders[j][:16, :]
        out_rows[j * 16 : j * 16 + 16, :] = riders[j][16:, :]


def far_kernel(index, own_ref, other_ref, table, keep_ref, send_ref):
    low_core = index[1] == 0
    for source in range(2):
        rows = jnp.where(index[1] == source, own_ref[...], other_ref[...])
        at = slice(source * G_ROWS, source * G_ROWS + G_ROWS)
        for kind in range(2):
            out = dot_nt(rows, table[kind * 256 : kind * 256 + 256, :]).astype(jnp.bfloat16)
            lanes = slice(kind * 128, kind * 128 + 128)
            keep_ref[at, lanes] = jnp.where(low_core, out[:, :128], out[:, 128:])
            send_ref[at, lanes] = jnp.where(low_core, out[:, 128:], out[:, :128])


def attention_kernel(index, keep_ref, got_ref, g_keep, g_got, below_ref, below_got, above_ref, above_got, out_ref):
    z, x, limit = index[0], index[2], index[3]
    lane_head = (lax.broadcasted_iota(jnp.int32, (TOK, WIDE), 1) % 128) // HALF
    row = lax.broadcasted_iota(jnp.int32, (HEADS_LOCAL * TOK, TOK), 0) % TOK
    col = lax.broadcasted_iota(jnp.int32, (HEADS_LOCAL * TOK, TOK), 1)
    far = lax.broadcasted_iota(jnp.int32, (1, 2 * G_ROWS), 1)
    far_core, j, far_x, far_k = far >> 7, (far >> 4) & 7, (far >> 3) & 1, far & 7
    delta = jnp.where((j & 1) == 1, -((j + 1) >> 1), j >> 1)
    far_z = (z + delta * (1 - 2 * far_core)) & (Z - 1)
    far_ok = ((far_x * Z + far_z) * C + far_core) * TOK + far_k * BLOCK < limit
    far_keys = jnp.concatenate([g_keep[:, :128], g_got[:, :128]], axis=1)
    far_values = jnp.concatenate([g_keep[:, 128:], g_got[:, 128:]], axis=1)

    def local(kind, at):
        lanes = slice(kind * 128, kind * 128 + 128)
        return jnp.concatenate([keep_ref[at : at + TOK, lanes], got_ref[at : at + TOK, lanes]], axis=1)

    def halo(ref, got, kind, seg):
        at = pl.ds(pl.multiple_of(seg * TOK, TOK), TOK)
        lanes = slice(kind * 128 - 128, kind * 128)
        return jnp.concatenate([ref[at, lanes], got[at, lanes]], axis=1)

    for seg in range(2):
        below_seg = jnp.where(z == 0, 1 - seg, seg)
        above_seg = jnp.where(z == Z - 1, 1 - seg, seg)
        for part in range(2):
            base = (seg * Z + z) * 2 * TOK + part * TOK
            at = (seg * 2 + part) * TOK
            queries = local(0, at)
            stacked = jnp.concatenate(
                [jnp.where(lane_head == h, queries, jnp.zeros_like(queries)) for h in range(HEADS_LOCAL)],
                axis=0,
            )

            def neighbours(kind):
                if part == 0:
                    return halo(below_ref, below_got, kind, below_seg), local(kind, at), local(kind, at + TOK)
                return local(kind, at - TOK), local(kind, at), halo(above_ref, above_got, kind, above_seg)

            k_left, k_mid, k_right = neighbours(1)
            v_left, v_mid, v_right = neighbours(2)
            low = base - TOK
            ok_left = (col > row) & (col + low >= 0) & (col + low < limit)
            ok_mid = col + base < limit
            ok_right = (col < row) & (col + (base + TOK) < limit)
            s_left = jnp.where(ok_left, dot_nt(stacked, k_left), NEGATIVE)
            s_mid = jnp.where(ok_mid, dot_nt(stacked, k_mid), NEGATIVE)
            s_right = jnp.where(ok_right, dot_nt(stacked, k_right), NEGATIVE)
            s_far = jnp.where(far_ok, dot_nt(stacked, far_keys), NEGATIVE)
            near_top = jnp.maximum(jnp.maximum(s_left, s_mid), s_right)
            far_top = jnp.maximum(s_far[:, :128], s_far[:, 128:])
            top = jnp.max(jnp.maximum(near_top, far_top), axis=-1, keepdims=True)
            w_left = jnp.exp(s_left - top)
            w_mid = jnp.exp(s_mid - top)
            w_right = jnp.exp(s_right - top)
            w_far = jnp.exp(s_far - top)
            total = jnp.sum(
                w_left + w_mid + w_right + w_far[:, :128] + w_far[:, 128:], axis=-1, keepdims=True
            )

            def mix(weights, values):
                return jnp.dot(
                    weights.astype(jnp.bfloat16), values, preferred_element_type=jnp.float32
                )

            mixed = mix(w_left, v_left) + mix(w_mid, v_mid) + mix(w_right, v_right) + mix(w_far, far_values)
            mixed = mixed / total
            context = jnp.zeros((TOK, WIDE), jnp.float32)
            for h in range(HEADS_LOCAL):
                context = jnp.where(lane_head == h, mixed[h * TOK : (h + 1) * TOK, :], context)
            mine = jnp.where(x == seg, 0, 1)
            out_ref[mine, part * TOK : (part + 1) * TOK, :] = context.astype(jnp.bfloat16)


def output_kernel(index, own_ref, there_ref, mine, prev, nxt, far_a, far_b, keep_ref, send_ref, table):
    z, core, x, y = index[0], index[1], index[2], index[5]
    own, there = own_ref[...], there_ref[...]
    for side in range(X):
        mixed = jnp.where(x == side, own, there)
        table[2 * side] = mixed[:, :128]
        table[2 * side + 1] = mixed[:, 128:]
    full = jnp.concatenate([table[(y + turn) & 3] for turn in (0, 3, 1, 2)], axis=1)
    for j, (way, hops) in enumerate(STEPS):
        zj = z_of(z, core, way, hops)
        here = j * 16
        far = (far_a, here) if j < 4 else (far_b, here - 64)
        weights = [
            ref[at : at + 16, i * 256 : i * 256 + 256]
            for ref, at in ((mine, here), (prev, here), (nxt, here), far)
            for i in range(8)
        ]
        out = jnp.dot(full, jnp.concatenate(weights, axis=0), preferred_element_type=jnp.float32)
        keep = jnp.where(core == 0, out[:TOK], out[TOK:])
        sent = jnp.where(core == 0, out[TOK:], out[:TOK]).astype(jnp.bfloat16)
        for side in range(X):
            lanes = pl.ds(pl.multiple_of((side * Z + zj) * 128, 128), 128)
            keep_ref[:, lanes] = keep[:, side * 128 : side * 128 + 128]
            send_ref[:, lanes] = sent[:, side * 128 : side * 128 + 128]


def on_chip(kernel, out_shape, flops, exps, args, scratch=(), in_hbm=0):
    vmem = pl.BlockSpec(memory_space=pltpu.VMEM)
    specs = [pl.BlockSpec(memory_space=pltpu.SMEM)] + [pl.BlockSpec(memory_space=pltpu.HBM)] * in_hbm
    specs += [vmem] * (len(args) - len(specs))
    return pl.pallas_call(
        kernel,
        out_shape=out_shape,
        in_specs=specs,
        out_specs=jax.tree.map(lambda _: vmem, out_shape),
        scratch_shapes=list(scratch),
        compiler_params=pltpu.CompilerParams(vmem_limit_bytes=VMEM_LIMIT),
        cost_estimate=pl.CostEstimate(flops=flops, bytes_accessed=4 << 20, transcendentals=exps),
    )(*args)


def after(value, *others):
    return lax.optimization_barrier((value, *others))[0]


def per_device(hidden_in, length, attn_gain, global_gain, w_query, w_key, w_value, w_out):
    width = hidden_in.shape[1]
    me = lax.axis_index("seq")
    core = me & 1
    z = (me >> 1) & (Z - 1)
    x = me >> 4
    limit = length[0]
    bf16 = jnp.bfloat16
    y = lax.axis_index("doc") & (Y - 1)
    index = jnp.stack([z, core, x, limit, me * TOK, y]).astype(jnp.int32)

    first = jnp.concatenate([w_query.T, w_key.T, w_value.T], axis=0)

    normed, global_mine = on_chip(
        norm_kernel,
        (jax.ShapeDtypeStruct((TOK, width), bf16), jax.ShapeDtypeStruct((TOK // BLOCK, width), bf16)),
        8 * TOK * width,
        0,
        (index, after(hidden_in, first), attn_gain[None], global_gain[None]),
        (
            pltpu.VMEM((TOK, width), bf16),
            pltpu.VMEM((1, width), jnp.float32),
            pltpu.VMEM((1, width), jnp.float32),
            pltpu.SemaphoreType.DMA((3,)),
        ),
        in_hbm=3,
    )
    global_there = send(global_mine, OTHER_X)

    split = after(w_out, first).reshape(X, 2, HEADS_LOCAL, 2, HALF, 64)

    def slab(group):
        at = (y >> 1, group, 0, (y & 1) ^ group, 0, 0)
        return lax.dynamic_slice(split, at, (1, 1, HEADS_LOCAL, 1, HALF, 64)).reshape(128, 64)

    kept = slab(core)
    passed = send(slab(1 - core), OTHER_CORE)
    chip = jnp.concatenate([jnp.where(core == 0, kept, passed), jnp.where(core == 0, passed, kept)], axis=1)
    chip_there = send(chip, OTHER_X)
    both = jnp.concatenate([jnp.where(x == 0, chip, chip_there), jnp.where(x == 0, chip_there, chip)], axis=1)

    second = jnp.concatenate(
        [
            jnp.where(x == 0, global_mine, global_there),
            jnp.where(x == 0, global_there, global_mine),
            jnp.concatenate([both[i * 16 : i * 16 + 16] for i in range(8)], axis=1),
        ],
        axis=0,
    )

    one, two = {(0, 0): first}, {(0, 0): second}
    a_one, a_two, b_one, b_two = first, second, first, second
    for step in range(1, 5):
        if step > 2:
            before = two[0, step - 2], two[1, step - 2]
            a_one, b_one = lax.optimization_barrier((a_one, b_one, *before))[:2]
        one[0, step] = a_one = send(a_one, AHEAD)
        if step < 4:
            one[1, step] = b_one = send(b_one, BEHIND)
        before = one[0, max(step - 1, 1)], one[1, max(step - 1, 1)]
        a_two, b_two = lax.optimization_barrier((a_two, b_two, *before))[:2]
        two[0, step] = a_two = send(a_two, AHEAD)
        if step < 4:
            two[1, step] = b_two = send(b_two, BEHIND)
    shards = [one[s] for s in STEPS]
    riders = [two[s] for s in STEPS]

    to_send = after(normed, one[0, 1])
    across = send(to_send, OTHER_X)
    beside = send(to_send, OTHER_CORE)
    beside_across = send(across, OTHER_CORE)

    half = jax.ShapeDtypeStruct((ROWS, 3 * 128), bf16)
    keep, to_swap, far_table, *edges = on_chip(
        project_kernel,
        (
            half,
            half,
            jax.ShapeDtypeStruct((2 * Z * HALF, width), bf16),
            *[jax.ShapeDtypeStruct((2 * TOK, 256), bf16)] * 4,
        ),
        2 * ROWS * 768 * width,
        0,
        (index, normed, across, beside, beside_across, *shards),
        (pltpu.VMEM((ROWS, width), bf16), pltpu.VMEM((Z * HALF, width), bf16), pltpu.SemaphoreType.DMA((4,))),
        in_hbm=4,
    )
    got = send(to_swap, OTHER_CORE)
    block = jax.ShapeDtypeStruct((G_ROWS, width), bf16)
    g_own, out_own = on_chip(collect_kernel, (block, block), 0, 0, (index, *riders))
    g_other = send(g_own, OTHER_CORE)

    below = send(edges[2], UP), send(edges[3], UP_CROSS)
    above = send(edges[0], DOWN), send(edges[1], DOWN_CROSS)
    far_half = jax.ShapeDtypeStruct((2 * G_ROWS, 256), bf16)
    g_keep, g_swap = on_chip(
        far_kernel, (far_half, far_half), 2 * 256 * 512 * width, 0, (index, g_own, g_other, far_table)
    )
    g_got = send(g_swap, OTHER_CORE)

    to_pass = after(out_own, below[0], above[0])
    out_prev = send(to_pass, Y_UP, "doc")
    out_next = send(to_pass, Y_DOWN, "doc")
    out_far_a = send(out_prev[:64], Y_UP, "doc")
    out_far_b = send(out_next[64:], Y_DOWN, "doc")

    context = on_chip(
        attention_kernel,
        jax.ShapeDtypeStruct((2, 2 * TOK, WIDE), bf16),
        4 * 4 * TOK * 640 * WIDE * 4,
        4 * 4 * TOK * 640,
        (index, keep, got, g_keep, g_got, *below, *above),
    )

    there = send(context[1], OTHER_X)
    kept_part, sent_part = on_chip(
        output_kernel,
        (jax.ShapeDtypeStruct((TOK, width), jnp.float32), jax.ShapeDtypeStruct((TOK, width), bf16)),
        2 * 256 * 512 * width,
        0,
        (index, context[0], there, out_own, out_prev, out_next, out_far_a, out_far_b),
        (pltpu.VMEM((4, 2 * TOK, 128), bf16),),
    )
    return (kept_part + send(sent_part, OTHER_CORE).astype(jnp.float32)).astype(bf16)


def solution(mesh):
    placed = (
        P(("doc", "seq"), None),
        P("doc"),
        P(),
        P(),
        P(None, "seq"),
        P(None, "seq"),
        P(None, "seq"),
        P(None, "seq"),
    )
    return jax.shard_map(
        per_device, mesh=mesh, in_specs=placed, out_specs=P(("doc", "seq"), None), check_vma=False
    )
```

```python
import jax
import jax.numpy as jnp
from jax import lax
from jax.experimental import pallas as pl
from jax.experimental.pallas import tpu as pltpu
from jax.sharding import PartitionSpec as P

HEAD_DIM = 64
BLOCK = 16
RADIUS = 127
NEGATIVE = -1e30
EPSILON = 1e-06

X, Z, C = 2, 8, 2
SEQ_SHARDS = X * Z * C
TOK = 128
HALF = 32
HEADS_LOCAL = 4
WIDE = HEADS_LOCAL * HEAD_DIM


def place(x, z, core):
    return (x * Z + z) * C + core


def pairs(move):
    return [
        (place(x, z, c), place(*move(x, z, c))) for x in range(X) for z in range(Z) for c in range(C)
    ]


OTHER_CORE = pairs(lambda x, z, c: (x, z, 1 - c))
OTHER_X = pairs(lambda x, z, c: (1 - x, z, c))
AHEAD = pairs(lambda x, z, c: (x, (z + (1 if c == 0 else -1)) % Z, c))
BEHIND = pairs(lambda x, z, c: (x, (z - (1 if c == 0 else -1)) % Z, c))
UP = pairs(lambda x, z, c: (x, (z + 1) % Z, c))
DOWN = pairs(lambda x, z, c: (x, (z - 1) % Z, c))


Y = 4
Y_UP = [(d, (d & 4) | ((d + 1) & 3)) for d in range(2 * Y)]
Y_DOWN = [(d, (d & 4) | ((d - 1) & 3)) for d in range(2 * Y)]


UP_CROSS = pairs(lambda x, z, c: (x, (z + 1) % Z, 1 - c))
DOWN_CROSS = pairs(lambda x, z, c: (x, (z - 1) % Z, 1 - c))


def send(value, route, axis="seq"):
    return lax.ppermute(value, axis, route)


def rms_norm(values, gain_row):
    mean_square = jnp.mean(values * values, axis=-1, keepdims=True)
    return values * lax.rsqrt(mean_square + EPSILON) * gain_row


def norm_kernel(index, hidden_in, gain_in, global_in, normed_ref, blocks_ref, hidden, gain, global_gain, sems):
    copies = [
        pltpu.make_async_copy(source, into, sems.at[i])
        for i, (source, into) in enumerate(((hidden_in, hidden), (gain_in, gain), (global_in, global_gain)))
    ]
    for copy in copies:
        copy.start()
    for copy in copies:
        copy.wait()
    normed = rms_norm(hidden[...].astype(jnp.float32), gain[...]).astype(jnp.bfloat16)
    normed_ref[...] = normed
    at = index[4] + lax.broadcasted_iota(jnp.int32, (TOK, 1), 0)
    valid = (at < index[3]).astype(jnp.float32)
    kept = (normed.astype(jnp.float32) * valid).reshape(TOK // BLOCK, BLOCK, normed.shape[1])
    blocks_ref[...] = rms_norm(jnp.sum(kept, axis=1), global_gain[...]).astype(jnp.bfloat16)


def dot_nt(left, right):
    return lax.dot_general(
        left, right, (((1,), (1,)), ((), ())), preferred_element_type=jnp.float32
    )


STEPS = ((0, 0), (0, 1), (1, 1), (0, 2), (1, 2), (0, 3), (1, 3), (0, 4))
SHARDS = len(STEPS)
ROWS = 4 * TOK
G_ROWS = Z * 16
VMEM_LIMIT = 32 * 1024 * 1024


def z_of(z, core, way, hops):
    delta = -hops if way == 0 else hops
    return (z + delta * (1 - 2 * core)) & (Z - 1)


def project_kernel(index, *refs):
    blocks, firsts, seconds = refs[:4], refs[4 : 4 + SHARDS], refs[4 + SHARDS : 4 + 2 * SHARDS]
    keep_ref, send_ref, g_rows, far_table, *edges, rows, table, sems = refs[4 + 2 * SHARDS :]
    z, core, x = index[0], index[1], index[2]
    low_core = core == 0
    copies = []
    for i, (ref, bx, bc) in enumerate(zip(blocks, (x, 1 - x, x, 1 - x), (core, core, 1 - core, 1 - core))):
        into = rows.at[pl.ds(pl.multiple_of((bx * 2 + bc) * TOK, TOK), TOK), :]
        copies.append(pltpu.make_async_copy(ref, into, sems.at[i]))
        copies[-1].start()
    for j, (way, hops) in enumerate(STEPS):
        at = z_of(z, core, way, hops) * HALF
        for kind in range(3):
            into = table if kind == 0 else far_table
            base = 0 if kind == 0 else kind * 256 - 256
            here = pl.multiple_of(base + at, 16)
            into[pl.ds(here, 16), :] = firsts[j][kind * 16 : kind * 16 + 16, :]
            there = pl.multiple_of(base + at + 16, 16)
            into[pl.ds(there, 16), :] = seconds[j][kind * 16 : kind * 16 + 16, :]
        g_rows[j * 16 : j * 16 + 16, :] = seconds[j][48:64, :]
    for copy in copies:
        copy.wait()
    for kind in range(3):
        columns = table[...] if kind == 0 else far_table[kind * 256 - 256 : kind * 256, :]
        out = dot_nt(rows[...], columns).astype(jnp.bfloat16)
        lanes = slice(kind * 128, kind * 128 + 128)
        keep_ref[:, lanes] = jnp.where(low_core, out[:, :128], out[:, 128:])
        send_ref[:, lanes] = jnp.where(low_core, out[:, 128:], out[:, :128])
        if kind:
            lanes_out = slice(kind * 128 - 128, kind * 128)
            for part in range(2):
                for seg in range(2):
                    at = slice((seg * 2 + part) * TOK, (seg * 2 + part + 1) * TOK)
                    into = slice(seg * TOK, seg * TOK + TOK)
                    edges[2 * part][into, lanes_out] = keep_ref[at, lanes]
                    edges[2 * part + 1][into, lanes_out] = send_ref[at, lanes]


def collect_kernel(*refs):
    for j, ref in enumerate(refs[1 : 1 + SHARDS]):
        refs[1 + SHARDS][j * 16 : j * 16 + 16, :] = ref[ref.shape[0] - 16 :, :]


def far_kernel(index, own_ref, other_ref, table, keep_ref, send_ref):
    low_core = index[1] == 0
    for source in range(2):
        rows = jnp.where(index[1] == source, own_ref[...], other_ref[...])
        at = slice(source * G_ROWS, source * G_ROWS + G_ROWS)
        for kind in range(2):
            out = dot_nt(rows, table[kind * 256 : kind * 256 + 256, :]).astype(jnp.bfloat16)
            lanes = slice(kind * 128, kind * 128 + 128)
            keep_ref[at, lanes] = jnp.where(low_core, out[:, :128], out[:, 128:])
            send_ref[at, lanes] = jnp.where(low_core, out[:, 128:], out[:, :128])


def attention_kernel(index, keep_ref, got_ref, g_keep, g_got, below_ref, below_got, above_ref, above_got, out_ref):
    z, x, limit = index[0], index[2], index[3]
    lane_head = (lax.broadcasted_iota(jnp.int32, (TOK, WIDE), 1) % 128) // HALF
    row = lax.broadcasted_iota(jnp.int32, (HEADS_LOCAL * TOK, TOK), 0) % TOK
    col = lax.broadcasted_iota(jnp.int32, (HEADS_LOCAL * TOK, TOK), 1)
    far = lax.broadcasted_iota(jnp.int32, (1, 2 * G_ROWS), 1)
    far_core, j, far_x, far_k = far >> 7, (far >> 4) & 7, (far >> 3) & 1, far & 7
    delta = jnp.where((j & 1) == 1, -((j + 1) >> 1), j >> 1)
    far_z = (z + delta * (1 - 2 * far_core)) & (Z - 1)
    far_ok = ((far_x * Z + far_z) * C + far_core) * TOK + far_k * BLOCK < limit
    far_keys = jnp.concatenate([g_keep[:, :128], g_got[:, :128]], axis=1)
    far_values = jnp.concatenate([g_keep[:, 128:], g_got[:, 128:]], axis=1)

    def local(kind, at):
        lanes = slice(kind * 128, kind * 128 + 128)
        return jnp.concatenate([keep_ref[at : at + TOK, lanes], got_ref[at : at + TOK, lanes]], axis=1)

    def halo(ref, got, kind, seg):
        at = pl.ds(pl.multiple_of(seg * TOK, TOK), TOK)
        lanes = slice(kind * 128 - 128, kind * 128)
        return jnp.concatenate([ref[at, lanes], got[at, lanes]], axis=1)

    for seg in range(2):
        below_seg = jnp.where(z == 0, 1 - seg, seg)
        above_seg = jnp.where(z == Z - 1, 1 - seg, seg)
        for part in range(2):
            base = (seg * Z + z) * 2 * TOK + part * TOK
            at = (seg * 2 + part) * TOK
            queries = local(0, at)
            stacked = jnp.concatenate(
                [jnp.where(lane_head == h, queries, jnp.zeros_like(queries)) for h in range(HEADS_LOCAL)],
                axis=0,
            )

            def neighbours(kind):
                if part == 0:
                    return halo(below_ref, below_got, kind, below_seg), local(kind, at), local(kind, at + TOK)
                return local(kind, at - TOK), local(kind, at), halo(above_ref, above_got, kind, above_seg)

            k_left, k_mid, k_right = neighbours(1)
            v_left, v_mid, v_right = neighbours(2)
            low = base - TOK
            ok_left = (col > row) & (col + low >= 0) & (col + low < limit)
            ok_mid = col + base < limit
            ok_right = (col < row) & (col + (base + TOK) < limit)
            s_left = jnp.where(ok_left, dot_nt(stacked, k_left), NEGATIVE)
            s_mid = jnp.where(ok_mid, dot_nt(stacked, k_mid), NEGATIVE)
            s_right = jnp.where(ok_right, dot_nt(stacked, k_right), NEGATIVE)
            s_far = jnp.where(far_ok, dot_nt(stacked, far_keys), NEGATIVE)
            near_top = jnp.maximum(jnp.maximum(s_left, s_mid), s_right)
            far_top = jnp.maximum(s_far[:, :128], s_far[:, 128:])
            top = jnp.max(jnp.maximum(near_top, far_top), axis=-1, keepdims=True)
            w_left = jnp.exp(s_left - top)
            w_mid = jnp.exp(s_mid - top)
            w_right = jnp.exp(s_right - top)
            w_far = jnp.exp(s_far - top)
            total = jnp.sum(
                w_left + w_mid + w_right + w_far[:, :128] + w_far[:, 128:], axis=-1, keepdims=True
            )

            def mix(weights, values):
                return jnp.dot(
                    weights.astype(jnp.bfloat16), values, preferred_element_type=jnp.float32
                )

            mixed = mix(w_left, v_left) + mix(w_mid, v_mid) + mix(w_right, v_right) + mix(w_far, far_values)
            mixed = mixed / total
            context = jnp.zeros((TOK, WIDE), jnp.float32)
            for h in range(HEADS_LOCAL):
                context = jnp.where(lane_head == h, mixed[h * TOK : (h + 1) * TOK, :], context)
            mine = jnp.where(x == seg, 0, 1)
            out_ref[mine, part * TOK : (part + 1) * TOK, :] = context.astype(jnp.bfloat16)


def output_kernel(index, own_ref, there_ref, mine, prev, nxt, far_a, far_b, keep_ref, send_ref, table):
    z, core, x, y = index[0], index[1], index[2], index[5]
    own, there = own_ref[...], there_ref[...]
    for side in range(X):
        mixed = jnp.where(x == side, own, there)
        table[2 * side] = mixed[:, :128]
        table[2 * side + 1] = mixed[:, 128:]
    full = jnp.concatenate([table[(y + turn) & 3] for turn in (0, 3, 1, 2)], axis=1)
    for j, (way, hops) in enumerate(STEPS):
        zj = z_of(z, core, way, hops)
        here = j * 16
        far = (far_a, here) if j < 4 else (far_b, here - 64)
        weights = [
            ref[at : at + 16, i * 256 : i * 256 + 256]
            for ref, at in ((mine, here), (prev, here), (nxt, here), far)
            for i in range(8)
        ]
        out = jnp.dot(full, jnp.concatenate(weights, axis=0), preferred_element_type=jnp.float32)
        keep = jnp.where(core == 0, out[:TOK], out[TOK:])
        sent = jnp.where(core == 0, out[TOK:], out[:TOK]).astype(jnp.bfloat16)
        for side in range(X):
            lanes = pl.ds(pl.multiple_of((side * Z + zj) * 128, 128), 128)
            keep_ref[:, lanes] = keep[:, side * 128 : side * 128 + 128]
            send_ref[:, lanes] = sent[:, side * 128 : side * 128 + 128]


def on_chip(kernel, out_shape, flops, exps, args, scratch=(), in_hbm=0):
    vmem = pl.BlockSpec(memory_space=pltpu.VMEM)
    specs = [pl.BlockSpec(memory_space=pltpu.SMEM)] + [pl.BlockSpec(memory_space=pltpu.HBM)] * in_hbm
    specs += [vmem] * (len(args) - len(specs))
    return pl.pallas_call(
        kernel,
        out_shape=out_shape,
        in_specs=specs,
        out_specs=jax.tree.map(lambda _: vmem, out_shape),
        scratch_shapes=list(scratch),
        compiler_params=pltpu.CompilerParams(vmem_limit_bytes=VMEM_LIMIT),
        cost_estimate=pl.CostEstimate(flops=flops, bytes_accessed=4 << 20, transcendentals=exps),
    )(*args)


def after(value, *others):
    return lax.optimization_barrier((value, *others))[0]


def per_device(hidden_in, length, attn_gain, global_gain, w_query, w_key, w_value, w_out):
    width = hidden_in.shape[1]
    me = lax.axis_index("seq")
    core = me & 1
    z = (me >> 1) & (Z - 1)
    x = me >> 4
    limit = length[0]
    bf16 = jnp.bfloat16
    y = lax.axis_index("doc") & (Y - 1)
    index = jnp.stack([z, core, x, limit, me * TOK, y]).astype(jnp.int32)

    mine = jnp.stack([w_query.T, w_key.T, w_value.T]).reshape(3, 2, 16, width)
    first = mine[:, 0].reshape(48, width)

    normed, global_mine = on_chip(
        norm_kernel,
        (jax.ShapeDtypeStruct((TOK, width), bf16), jax.ShapeDtypeStruct((TOK // BLOCK, width), bf16)),
        8 * TOK * width,
        0,
        (index, after(hidden_in, first), attn_gain[None], global_gain[None]),
        (
            pltpu.VMEM((TOK, width), bf16),
            pltpu.VMEM((1, width), jnp.float32),
            pltpu.VMEM((1, width), jnp.float32),
            pltpu.SemaphoreType.DMA((3,)),
        ),
        in_hbm=3,
    )
    global_there = send(global_mine, OTHER_X)

    split = after(w_out, first).reshape(X, 2, HEADS_LOCAL, 2, HALF, 64)

    def slab(group):
        at = (y >> 1, group, 0, (y & 1) ^ group, 0, 0)
        return lax.dynamic_slice(split, at, (1, 1, HEADS_LOCAL, 1, HALF, 64)).reshape(128, 64)

    kept = slab(core)
    passed = send(slab(1 - core), OTHER_CORE)
    chip = jnp.concatenate([jnp.where(core == 0, kept, passed), jnp.where(core == 0, passed, kept)], axis=1)
    chip_there = send(chip, OTHER_X)
    both = jnp.concatenate([jnp.where(x == 0, chip, chip_there), jnp.where(x == 0, chip_there, chip)], axis=1)

    joining = jnp.concatenate([both[i * 16 : i * 16 + 16] for i in range(8)], axis=1)

    second = jnp.concatenate(
        [
            mine[:, 1].reshape(48, width),
            jnp.where(x == 0, global_mine, global_there),
            jnp.where(x == 0, global_there, global_mine),
        ],
        axis=0,
    )

    one, two = {(0, 0): first}, {(0, 0): second}
    a_one, a_two, b_one, b_two = first, second, first, second
    for step in range(1, 5):
        if step > 1:
            before = (two[0, step - 2], two[1, step - 2]) if step > 2 else ()
            a_one, b_one = lax.optimization_barrier((a_one, b_one, *before))[:2]
        one[0, step] = a_one = send(a_one, AHEAD)
        if step < 4:
            one[1, step] = b_one = send(b_one, BEHIND)
        if step > 1:
            a_two, b_two = lax.optimization_barrier((a_two, b_two, one[0, step - 1], one[1, step - 1]))[:2]
        if step == 2:
            a_two = jnp.concatenate([a_two, joining], axis=0)
            b_two = jnp.concatenate([b_two, joining], axis=0)
        two[0, step] = a_two = send(a_two, AHEAD)
        if step < 4:
            two[1, step] = b_two = send(b_two, BEHIND)
    last_b = send(two[1, 3][64:], BEHIND)
    last_a = send(two[0, 4][64:], AHEAD)
    joined = [joining, two[0, 2], two[1, 2], two[0, 3], two[1, 3], two[0, 4], last_b, last_a]
    firsts = [one[s] for s in STEPS]
    seconds = [two[s] for s in STEPS]

    to_send = after(normed, one[0, 1])
    across = send(to_send, OTHER_X)
    beside = send(to_send, OTHER_CORE)
    beside_across = send(across, OTHER_CORE)

    half = jax.ShapeDtypeStruct((ROWS, 3 * 128), bf16)
    keep, to_swap, g_own, far_table, *edges = on_chip(
        project_kernel,
        (
            half,
            half,
            jax.ShapeDtypeStruct((G_ROWS, width), bf16),
            jax.ShapeDtypeStruct((2 * Z * HALF, width), bf16),
            *[jax.ShapeDtypeStruct((2 * TOK, 256), bf16)] * 4,
        ),
        2 * ROWS * 768 * width,
        0,
        (index, normed, across, beside, beside_across, *firsts, *seconds),
        (pltpu.VMEM((ROWS, width), bf16), pltpu.VMEM((Z * HALF, width), bf16), pltpu.SemaphoreType.DMA((4,))),
        in_hbm=4,
    )
    got = send(to_swap, OTHER_CORE)
    g_other = send(g_own, OTHER_CORE)

    below = send(edges[2], UP), send(edges[3], UP_CROSS)
    above = send(edges[0], DOWN), send(edges[1], DOWN_CROSS)
    far_half = jax.ShapeDtypeStruct((2 * G_ROWS, 256), bf16)
    g_keep, g_swap = on_chip(
        far_kernel, (far_half, far_half), 2 * 256 * 512 * width, 0, (index, g_own, g_other, far_table)
    )
    g_got = send(g_swap, OTHER_CORE)

    out_own = on_chip(collect_kernel, jax.ShapeDtypeStruct((128, width), bf16), 0, 0, (index, *joined))
    to_pass = after(out_own, got)
    out_prev = send(to_pass, Y_UP, "doc")
    out_next = send(to_pass, Y_DOWN, "doc")
    out_far_a = send(out_prev[:64], Y_UP, "doc")
    out_far_b = send(out_next[64:], Y_DOWN, "doc")

    context = on_chip(
        attention_kernel,
        jax.ShapeDtypeStruct((2, 2 * TOK, WIDE), bf16),
        4 * 4 * TOK * 640 * WIDE * 4,
        4 * 4 * TOK * 640,
        (index, keep, got, g_keep, g_got, *below, *above),
    )

    there = send(context[1], OTHER_X)
    kept_part, sent_part = on_chip(
        output_kernel,
        (jax.ShapeDtypeStruct((TOK, width), jnp.float32), jax.ShapeDtypeStruct((TOK, width), bf16)),
        2 * 256 * 512 * width,
        0,
        (index, context[0], there, out_own, out_prev, out_next, out_far_a, out_far_b),
        (pltpu.VMEM((4, 2 * TOK, 128), bf16),),
    )
    return (kept_part + send(sent_part, OTHER_CORE).astype(jnp.float32)).astype(bf16)


def solution(mesh):
    placed = (
        P(("doc", "seq"), None),
        P("doc"),
        P(),
        P(),
        P(None, "seq"),
        P(None, "seq"),
        P(None, "seq"),
        P(None, "seq"),
    )
    return jax.shard_map(
        per_device, mesh=mesh, in_specs=placed, out_specs=P(("doc", "seq"), None), check_vma=False
    )
```

```python
import jax
import jax.numpy as jnp
from jax import lax
from jax.experimental import pallas as pl
from jax.experimental.pallas import tpu as pltpu
from jax.sharding import PartitionSpec as P

HEAD_DIM = 64
BLOCK = 16
RADIUS = 127
NEGATIVE = -1e30
EPSILON = 1e-06

X, Z, C = 2, 8, 2
SEQ_SHARDS = X * Z * C
TOK = 128
HALF = 32
HEADS_LOCAL = 4
WIDE = HEADS_LOCAL * HEAD_DIM


def place(x, z, core):
    return (x * Z + z) * C + core


def pairs(move):
    return [
        (place(x, z, c), place(*move(x, z, c))) for x in range(X) for z in range(Z) for c in range(C)
    ]


OTHER_CORE = pairs(lambda x, z, c: (x, z, 1 - c))
OTHER_X = pairs(lambda x, z, c: (1 - x, z, c))
AHEAD = pairs(lambda x, z, c: (x, (z + (1 if c == 0 else -1)) % Z, c))
BEHIND = pairs(lambda x, z, c: (x, (z - (1 if c == 0 else -1)) % Z, c))
UP = pairs(lambda x, z, c: (x, (z + 1) % Z, c))
DOWN = pairs(lambda x, z, c: (x, (z - 1) % Z, c))


Y = 4
Y_UP = [(d, (d & 4) | ((d + 1) & 3)) for d in range(2 * Y)]
Y_DOWN = [(d, (d & 4) | ((d - 1) & 3)) for d in range(2 * Y)]


UP_CROSS = pairs(lambda x, z, c: (x, (z + 1) % Z, 1 - c))
DOWN_CROSS = pairs(lambda x, z, c: (x, (z - 1) % Z, 1 - c))


def send(value, route, axis="seq"):
    return lax.ppermute(value, axis, route)


def rms_norm(values, gain_row):
    mean_square = jnp.mean(values * values, axis=-1, keepdims=True)
    return values * lax.rsqrt(mean_square + EPSILON) * gain_row


def norm_kernel(index, hidden_in, gain_in, global_in, normed_ref, blocks_ref, hidden, gain, global_gain, sems):
    copies = [
        pltpu.make_async_copy(source, into, sems.at[i])
        for i, (source, into) in enumerate(((hidden_in, hidden), (gain_in, gain), (global_in, global_gain)))
    ]
    for copy in copies:
        copy.start()
    for copy in copies:
        copy.wait()
    normed = rms_norm(hidden[...].astype(jnp.float32), gain[...]).astype(jnp.bfloat16)
    normed_ref[...] = normed
    at = index[4] + lax.broadcasted_iota(jnp.int32, (TOK, 1), 0)
    valid = (at < index[3]).astype(jnp.float32)
    kept = (normed.astype(jnp.float32) * valid).reshape(TOK // BLOCK, BLOCK, normed.shape[1])
    blocks_ref[...] = rms_norm(jnp.sum(kept, axis=1), global_gain[...]).astype(jnp.bfloat16)


def dot_nt(left, right):
    return lax.dot_general(
        left, right, (((1,), (1,)), ((), ())), preferred_element_type=jnp.float32
    )


STEPS = ((0, 0), (0, 1), (1, 1), (0, 2), (1, 2), (0, 3), (1, 3), (0, 4))
SHARDS = len(STEPS)
ROWS = 4 * TOK
G_ROWS = Z * 16
VMEM_LIMIT = 32 * 1024 * 1024


def z_of(z, core, way, hops):
    delta = -hops if way == 0 else hops
    return (z + delta * (1 - 2 * core)) & (Z - 1)


def project_kernel(index, *refs):
    blocks, firsts, seconds = refs[:4], refs[4 : 4 + SHARDS], refs[4 + SHARDS : 4 + 2 * SHARDS]
    keep_ref, send_ref, g_rows, far_table, out_rows, *edges, rows, table, sems = refs[4 + 2 * SHARDS :]
    z, core, x = index[0], index[1], index[2]
    low_core = core == 0
    copies = []
    for i, (ref, bx, bc) in enumerate(zip(blocks, (x, 1 - x, x, 1 - x), (core, core, 1 - core, 1 - core))):
        into = rows.at[pl.ds(pl.multiple_of((bx * 2 + bc) * TOK, TOK), TOK), :]
        copies.append(pltpu.make_async_copy(ref, into, sems.at[i]))
        copies[-1].start()
    for j, (way, hops) in enumerate(STEPS):
        at = z_of(z, core, way, hops) * HALF
        for kind in range(3):
            into = table if kind == 0 else far_table
            base = 0 if kind == 0 else kind * 256 - 256
            here = pl.multiple_of(base + at, 16)
            into[pl.ds(here, 16), :] = firsts[j][kind * 16 : kind * 16 + 16, :]
            there = pl.multiple_of(base + at + 16, 16)
            into[pl.ds(there, 16), :] = seconds[j][kind * 16 : kind * 16 + 16, :]
        g_rows[j * 16 : j * 16 + 16, :] = seconds[j][48:64, :]
        out_rows[j * 16 : j * 16 + 16, :] = seconds[j][64:80, :]
    for copy in copies:
        copy.wait()
    for kind in range(3):
        columns = table[...] if kind == 0 else far_table[kind * 256 - 256 : kind * 256, :]
        out = dot_nt(rows[...], columns).astype(jnp.bfloat16)
        lanes = slice(kind * 128, kind * 128 + 128)
        keep_ref[:, lanes] = jnp.where(low_core, out[:, :128], out[:, 128:])
        send_ref[:, lanes] = jnp.where(low_core, out[:, 128:], out[:, :128])
        if kind:
            lanes_out = slice(kind * 128 - 128, kind * 128)
            for part in range(2):
                for seg in range(2):
                    at = slice((seg * 2 + part) * TOK, (seg * 2 + part + 1) * TOK)
                    into = slice(seg * TOK, seg * TOK + TOK)
                    edges[2 * part][into, lanes_out] = keep_ref[at, lanes]
                    edges[2 * part + 1][into, lanes_out] = send_ref[at, lanes]


def far_kernel(index, own_ref, other_ref, table, keep_ref, send_ref):
    low_core = index[1] == 0
    for source in range(2):
        rows = jnp.where(index[1] == source, own_ref[...], other_ref[...])
        at = slice(source * G_ROWS, source * G_ROWS + G_ROWS)
        for kind in range(2):
            out = dot_nt(rows, table[kind * 256 : kind * 256 + 256, :]).astype(jnp.bfloat16)
            lanes = slice(kind * 128, kind * 128 + 128)
            keep_ref[at, lanes] = jnp.where(low_core, out[:, :128], out[:, 128:])
            send_ref[at, lanes] = jnp.where(low_core, out[:, 128:], out[:, :128])


def attention_kernel(index, keep_ref, got_ref, g_keep, g_got, below_ref, below_got, above_ref, above_got, out_ref):
    z, x, limit = index[0], index[2], index[3]
    lane_head = (lax.broadcasted_iota(jnp.int32, (TOK, WIDE), 1) % 128) // HALF
    row = lax.broadcasted_iota(jnp.int32, (HEADS_LOCAL * TOK, TOK), 0) % TOK
    col = lax.broadcasted_iota(jnp.int32, (HEADS_LOCAL * TOK, TOK), 1)
    far = lax.broadcasted_iota(jnp.int32, (1, 2 * G_ROWS), 1)
    far_core, j, far_x, far_k = far >> 7, (far >> 4) & 7, (far >> 3) & 1, far & 7
    delta = jnp.where((j & 1) == 1, -((j + 1) >> 1), j >> 1)
    far_z = (z + delta * (1 - 2 * far_core)) & (Z - 1)
    far_ok = ((far_x * Z + far_z) * C + far_core) * TOK + far_k * BLOCK < limit
    far_keys = jnp.concatenate([g_keep[:, :128], g_got[:, :128]], axis=1)
    far_values = jnp.concatenate([g_keep[:, 128:], g_got[:, 128:]], axis=1)

    def local(kind, at):
        lanes = slice(kind * 128, kind * 128 + 128)
        return jnp.concatenate([keep_ref[at : at + TOK, lanes], got_ref[at : at + TOK, lanes]], axis=1)

    def halo(ref, got, kind, seg):
        at = pl.ds(pl.multiple_of(seg * TOK, TOK), TOK)
        lanes = slice(kind * 128 - 128, kind * 128)
        return jnp.concatenate([ref[at, lanes], got[at, lanes]], axis=1)

    for seg in range(2):
        below_seg = jnp.where(z == 0, 1 - seg, seg)
        above_seg = jnp.where(z == Z - 1, 1 - seg, seg)
        for part in range(2):
            base = (seg * Z + z) * 2 * TOK + part * TOK
            at = (seg * 2 + part) * TOK
            queries = local(0, at)
            stacked = jnp.concatenate(
                [jnp.where(lane_head == h, queries, jnp.zeros_like(queries)) for h in range(HEADS_LOCAL)],
                axis=0,
            )

            def neighbours(kind):
                if part == 0:
                    return halo(below_ref, below_got, kind, below_seg), local(kind, at), local(kind, at + TOK)
                return local(kind, at - TOK), local(kind, at), halo(above_ref, above_got, kind, above_seg)

            k_left, k_mid, k_right = neighbours(1)
            v_left, v_mid, v_right = neighbours(2)
            low = base - TOK
            ok_left = (col > row) & (col + low >= 0) & (col + low < limit)
            ok_mid = col + base < limit
            ok_right = (col < row) & (col + (base + TOK) < limit)
            s_left = jnp.where(ok_left, dot_nt(stacked, k_left), NEGATIVE)
            s_mid = jnp.where(ok_mid, dot_nt(stacked, k_mid), NEGATIVE)
            s_right = jnp.where(ok_right, dot_nt(stacked, k_right), NEGATIVE)
            s_far = jnp.where(far_ok, dot_nt(stacked, far_keys), NEGATIVE)
            near_top = jnp.maximum(jnp.maximum(s_left, s_mid), s_right)
            far_top = jnp.maximum(s_far[:, :128], s_far[:, 128:])
            top = jnp.max(jnp.maximum(near_top, far_top), axis=-1, keepdims=True)
            w_left = jnp.exp(s_left - top)
            w_mid = jnp.exp(s_mid - top)
            w_right = jnp.exp(s_right - top)
            w_far = jnp.exp(s_far - top)
            total = jnp.sum(
                w_left + w_mid + w_right + w_far[:, :128] + w_far[:, 128:], axis=-1, keepdims=True
            )

            def mix(weights, values):
                return jnp.dot(
                    weights.astype(jnp.bfloat16), values, preferred_element_type=jnp.float32
                )

            mixed = mix(w_left, v_left) + mix(w_mid, v_mid) + mix(w_right, v_right) + mix(w_far, far_values)
            mixed = mixed / total
            context = jnp.zeros((TOK, WIDE), jnp.float32)
            for h in range(HEADS_LOCAL):
                context = jnp.where(lane_head == h, mixed[h * TOK : (h + 1) * TOK, :], context)
            mine = jnp.where(x == seg, 0, 1)
            out_ref[mine, part * TOK : (part + 1) * TOK, :] = context.astype(jnp.bfloat16)


def output_kernel(index, own_ref, there_ref, mine, prev, nxt, far_a, far_b, keep_ref, send_ref, table):
    z, core, x, y = index[0], index[1], index[2], index[5]
    own, there = own_ref[...], there_ref[...]
    for side in range(X):
        mixed = jnp.where(x == side, own, there)
        table[2 * side] = mixed[:, :128]
        table[2 * side + 1] = mixed[:, 128:]
    full = jnp.concatenate([table[(y + turn) & 3] for turn in (0, 3, 1, 2)], axis=1)
    for j, (way, hops) in enumerate(STEPS):
        zj = z_of(z, core, way, hops)
        here = j * 16
        far = (far_a, here) if j < 4 else (far_b, here - 64)
        weights = [
            ref[at : at + 16, i * 256 : i * 256 + 256]
            for ref, at in ((mine, here), (prev, here), (nxt, here), far)
            for i in range(8)
        ]
        out = jnp.dot(full, jnp.concatenate(weights, axis=0), preferred_element_type=jnp.float32)
        keep = jnp.where(core == 0, out[:TOK], out[TOK:])
        sent = jnp.where(core == 0, out[TOK:], out[:TOK]).astype(jnp.bfloat16)
        for side in range(X):
            lanes = pl.ds(pl.multiple_of((side * Z + zj) * 128, 128), 128)
            keep_ref[:, lanes] = keep[:, side * 128 : side * 128 + 128]
            send_ref[:, lanes] = sent[:, side * 128 : side * 128 + 128]


def on_chip(kernel, out_shape, flops, exps, args, scratch=(), in_hbm=0):
    vmem = pl.BlockSpec(memory_space=pltpu.VMEM)
    specs = [pl.BlockSpec(memory_space=pltpu.SMEM)] + [pl.BlockSpec(memory_space=pltpu.HBM)] * in_hbm
    specs += [vmem] * (len(args) - len(specs))
    return pl.pallas_call(
        kernel,
        out_shape=out_shape,
        in_specs=specs,
        out_specs=jax.tree.map(lambda _: vmem, out_shape),
        scratch_shapes=list(scratch),
        compiler_params=pltpu.CompilerParams(vmem_limit_bytes=VMEM_LIMIT),
        cost_estimate=pl.CostEstimate(flops=flops, bytes_accessed=4 << 20, transcendentals=exps),
    )(*args)


def after(value, *others):
    return lax.optimization_barrier((value, *others))[0]


def per_device(hidden_in, length, attn_gain, global_gain, w_query, w_key, w_value, w_out):
    width = hidden_in.shape[1]
    me = lax.axis_index("seq")
    core = me & 1
    z = (me >> 1) & (Z - 1)
    x = me >> 4
    limit = length[0]
    bf16 = jnp.bfloat16
    y = lax.axis_index("doc") & (Y - 1)
    index = jnp.stack([z, core, x, limit, me * TOK, y]).astype(jnp.int32)

    mine = jnp.stack([w_query.T, w_key.T, w_value.T]).reshape(3, 2, 16, width)
    first = mine[:, 0].reshape(48, width)

    normed, global_mine = on_chip(
        norm_kernel,
        (jax.ShapeDtypeStruct((TOK, width), bf16), jax.ShapeDtypeStruct((TOK // BLOCK, width), bf16)),
        8 * TOK * width,
        0,
        (index, after(hidden_in, first), attn_gain[None], global_gain[None]),
        (
            pltpu.VMEM((TOK, width), bf16),
            pltpu.VMEM((1, width), jnp.float32),
            pltpu.VMEM((1, width), jnp.float32),
            pltpu.SemaphoreType.DMA((3,)),
        ),
        in_hbm=3,
    )
    global_there = send(global_mine, OTHER_X)

    split = after(w_out, first).reshape(X, 2, HEADS_LOCAL, 2, HALF, 64)

    def slab(group):
        at = (y >> 1, group, 0, (y & 1) ^ group, 0, 0)
        return lax.dynamic_slice(split, at, (1, 1, HEADS_LOCAL, 1, HALF, 64)).reshape(128, 64)

    kept = slab(core)
    passed = send(slab(1 - core), OTHER_CORE)
    chip = jnp.concatenate([jnp.where(core == 0, kept, passed), jnp.where(core == 0, passed, kept)], axis=1)
    chip_there = send(chip, OTHER_X)
    both = jnp.concatenate([jnp.where(x == 0, chip, chip_there), jnp.where(x == 0, chip_there, chip)], axis=1)

    second = jnp.concatenate(
        [
            mine[:, 1].reshape(48, width),
            jnp.where(x == 0, global_mine, global_there),
            jnp.where(x == 0, global_there, global_mine),
            jnp.concatenate([both[i * 16 : i * 16 + 16] for i in range(8)], axis=1),
        ],
        axis=0,
    )

    one, two = {(0, 0): first}, {(0, 0): second}
    a_one, a_two, b_one, b_two = first, second, first, second
    for step in range(1, 5):
        if step == 2:
            a_two = b_two = after(second, a_one, b_one)
        if step > 1:
            if step > 2:
                before = one[0, step - 2], one[1, step - 2]
                a_two, b_two = lax.optimization_barrier((a_two, b_two, *before))[:2]
            two[0, step - 1] = a_two = send(a_two, AHEAD)
            two[1, step - 1] = b_two = send(b_two, BEHIND)
        if step > 2:
            before = two[0, step - 2], two[1, step - 2]
            a_one, b_one = lax.optimization_barrier((a_one, b_one, *before))[:2]
        one[0, step] = a_one = send(a_one, AHEAD)
        if step < 4:
            one[1, step] = b_one = send(b_one, BEHIND)
    a_two = after(a_two, one[0, 3], one[1, 3])
    two[0, 4] = send(a_two, AHEAD)
    firsts = [one[s] for s in STEPS]
    seconds = [two[s] for s in STEPS]

    to_send = after(normed, one[0, 1])
    across = send(to_send, OTHER_X)
    beside = send(to_send, OTHER_CORE)
    beside_across = send(across, OTHER_CORE)

    half = jax.ShapeDtypeStruct((ROWS, 3 * 128), bf16)
    keep, to_swap, g_own, far_table, out_own, *edges = on_chip(
        project_kernel,
        (
            half,
            half,
            jax.ShapeDtypeStruct((G_ROWS, width), bf16),
            jax.ShapeDtypeStruct((2 * Z * HALF, width), bf16),
            jax.ShapeDtypeStruct((128, width), bf16),
            *[jax.ShapeDtypeStruct((2 * TOK, 256), bf16)] * 4,
        ),
        2 * ROWS * 768 * width,
        0,
        (index, normed, across, beside, beside_across, *firsts, *seconds),
        (pltpu.VMEM((ROWS, width), bf16), pltpu.VMEM((Z * HALF, width), bf16), pltpu.SemaphoreType.DMA((4,))),
        in_hbm=4,
    )
    got = send(to_swap, OTHER_CORE)
    g_other = send(g_own, OTHER_CORE)

    below = send(edges[2], UP), send(edges[3], UP_CROSS)
    above = send(edges[0], DOWN), send(edges[1], DOWN_CROSS)
    far_half = jax.ShapeDtypeStruct((2 * G_ROWS, 256), bf16)
    g_keep, g_swap = on_chip(
        far_kernel, (far_half, far_half), 2 * 256 * 512 * width, 0, (index, g_own, g_other, far_table)
    )
    g_got = send(g_swap, OTHER_CORE)

    to_pass = out_own
    out_prev = send(to_pass, Y_UP, "doc")
    out_next = send(to_pass, Y_DOWN, "doc")
    out_far_a = send(out_prev[:64], Y_UP, "doc")
    out_far_b = send(out_next[64:], Y_DOWN, "doc")

    context = on_chip(
        attention_kernel,
        jax.ShapeDtypeStruct((2, 2 * TOK, WIDE), bf16),
        4 * 4 * TOK * 640 * WIDE * 4,
        4 * 4 * TOK * 640,
        (index, keep, got, g_keep, g_got, *below, *above),
    )

    there = send(context[1], OTHER_X)
    kept_part, sent_part = on_chip(
        output_kernel,
        (jax.ShapeDtypeStruct((TOK, width), jnp.float32), jax.ShapeDtypeStruct((TOK, width), bf16)),
        2 * 256 * 512 * width,
        0,
        (index, context[0], there, out_own, out_prev, out_next, out_far_a, out_far_b),
        (pltpu.VMEM((4, 2 * TOK, 128), bf16),),
    )
    return (kept_part + send(sent_part, OTHER_CORE).astype(jnp.float32)).astype(bf16)


def solution(mesh):
    placed = (
        P(("doc", "seq"), None),
        P("doc"),
        P(),
        P(),
        P(None, "seq"),
        P(None, "seq"),
        P(None, "seq"),
        P(None, "seq"),
    )
    return jax.shard_map(
        per_device, mesh=mesh, in_specs=placed, out_specs=P(("doc", "seq"), None), check_vma=False
    )
```

```python
import jax
import jax.numpy as jnp
from jax import lax
from jax.experimental import pallas as pl
from jax.experimental.pallas import tpu as pltpu
from jax.sharding import PartitionSpec as P

HEAD_DIM = 64
BLOCK = 16
RADIUS = 127
NEGATIVE = -1e30
EPSILON = 1e-06

X, Z, C = 2, 8, 2
SEQ_SHARDS = X * Z * C
TOK = 128
HALF = 32
HEADS_LOCAL = 4
WIDE = HEADS_LOCAL * HEAD_DIM


def place(x, z, core):
    return (x * Z + z) * C + core


def pairs(move):
    return [
        (place(x, z, c), place(*move(x, z, c))) for x in range(X) for z in range(Z) for c in range(C)
    ]


OTHER_CORE = pairs(lambda x, z, c: (x, z, 1 - c))
OTHER_X = pairs(lambda x, z, c: (1 - x, z, c))
AHEAD = pairs(lambda x, z, c: (x, (z + (1 if c == 0 else -1)) % Z, c))
BEHIND = pairs(lambda x, z, c: (x, (z - (1 if c == 0 else -1)) % Z, c))
UP = pairs(lambda x, z, c: (x, (z + 1) % Z, c))
DOWN = pairs(lambda x, z, c: (x, (z - 1) % Z, c))


Y = 4
Y_UP = [(d, (d & 4) | ((d + 1) & 3)) for d in range(2 * Y)]
Y_DOWN = [(d, (d & 4) | ((d - 1) & 3)) for d in range(2 * Y)]


UP_CROSS = pairs(lambda x, z, c: (x, (z + 1) % Z, 1 - c))
DOWN_CROSS = pairs(lambda x, z, c: (x, (z - 1) % Z, 1 - c))


def send(value, route, axis="seq"):
    return lax.ppermute(value, axis, route)


def rms_norm(values, gain_row):
    mean_square = jnp.mean(values * values, axis=-1, keepdims=True)
    return values * lax.rsqrt(mean_square + EPSILON) * gain_row


def norm_kernel(index, hidden_in, gain_in, global_in, normed_ref, blocks_ref, hidden, gain, global_gain, sems):
    copies = [
        pltpu.make_async_copy(source, into, sems.at[i])
        for i, (source, into) in enumerate(((hidden_in, hidden), (gain_in, gain), (global_in, global_gain)))
    ]
    for copy in copies:
        copy.start()
    for copy in copies:
        copy.wait()
    normed = rms_norm(hidden[...].astype(jnp.float32), gain[...]).astype(jnp.bfloat16)
    normed_ref[...] = normed
    at = index[4] + lax.broadcasted_iota(jnp.int32, (TOK, 1), 0)
    valid = (at < index[3]).astype(jnp.float32)
    kept = (normed.astype(jnp.float32) * valid).reshape(TOK // BLOCK, BLOCK, normed.shape[1])
    blocks_ref[...] = rms_norm(jnp.sum(kept, axis=1), global_gain[...]).astype(jnp.bfloat16)


def dot_nt(left, right):
    return lax.dot_general(
        left, right, (((1,), (1,)), ((), ())), preferred_element_type=jnp.float32
    )


STEPS = ((0, 0), (0, 1), (1, 1), (0, 2), (1, 2), (0, 3), (1, 3), (0, 4))
SHARDS = len(STEPS)
ROWS = 4 * TOK
G_ROWS = Z * 16
VMEM_LIMIT = 32 * 1024 * 1024


def z_of(z, core, way, hops):
    delta = -hops if way == 0 else hops
    return (z + delta * (1 - 2 * core)) & (Z - 1)


def project_kernel(index, *refs):
    blocks, firsts, seconds = refs[:4], refs[4 : 4 + SHARDS], refs[4 + SHARDS : 4 + 2 * SHARDS]
    keep_ref, send_ref, g_rows, far_table, out_rows, *edges, rows, table, sems = refs[4 + 2 * SHARDS :]
    z, core, x = index[0], index[1], index[2]
    low_core = core == 0
    copies = []
    for i, (ref, bx, bc) in enumerate(zip(blocks, (x, 1 - x, x, 1 - x), (core, core, 1 - core, 1 - core))):
        into = rows.at[pl.ds(pl.multiple_of((bx * 2 + bc) * TOK, TOK), TOK), :]
        copies.append(pltpu.make_async_copy(ref, into, sems.at[i]))
        copies[-1].start()
    for j, (way, hops) in enumerate(STEPS):
        at = z_of(z, core, way, hops) * HALF
        for kind in range(3):
            into = table if kind == 0 else far_table
            base = 0 if kind == 0 else kind * 256 - 256
            here = pl.multiple_of(base + at, 16)
            into[pl.ds(here, 16), :] = firsts[j][kind * 16 : kind * 16 + 16, :]
            there = pl.multiple_of(base + at + 16, 16)
            into[pl.ds(there, 16), :] = seconds[j][kind * 16 : kind * 16 + 16, :]
        g_rows[j * 16 : j * 16 + 16, :] = seconds[j][48:64, :]
        out_rows[j * 16 : j * 16 + 16, :] = seconds[j][64:80, :]
    for copy in copies:
        copy.wait()
    for kind in range(3):
        columns = table[...] if kind == 0 else far_table[kind * 256 - 256 : kind * 256, :]
        out = dot_nt(rows[...], columns).astype(jnp.bfloat16)
        lanes = slice(kind * 128, kind * 128 + 128)
        keep_ref[:, lanes] = jnp.where(low_core, out[:, :128], out[:, 128:])
        send_ref[:, lanes] = jnp.where(low_core, out[:, 128:], out[:, :128])
        if kind:
            lanes_out = slice(kind * 128 - 128, kind * 128)
            for part in range(2):
                for seg in range(2):
                    at = slice((seg * 2 + part) * TOK, (seg * 2 + part + 1) * TOK)
                    into = slice(seg * TOK, seg * TOK + TOK)
                    edges[2 * part][into, lanes_out] = keep_ref[at, lanes]
                    edges[2 * part + 1][into, lanes_out] = send_ref[at, lanes]


def far_kernel(index, own_ref, other_ref, table, keep_ref, send_ref):
    low_core = index[1] == 0
    for source in range(2):
        rows = jnp.where(index[1] == source, own_ref[...], other_ref[...])
        at = slice(source * G_ROWS, source * G_ROWS + G_ROWS)
        for kind in range(2):
            out = dot_nt(rows, table[kind * 256 : kind * 256 + 256, :]).astype(jnp.bfloat16)
            lanes = slice(kind * 128, kind * 128 + 128)
            keep_ref[at, lanes] = jnp.where(low_core, out[:, :128], out[:, 128:])
            send_ref[at, lanes] = jnp.where(low_core, out[:, 128:], out[:, :128])


def attention_kernel(index, keep_ref, got_ref, g_keep, g_got, below_ref, below_got, above_ref, above_got, out_ref):
    z, x, limit = index[0], index[2], index[3]
    lane_head = (lax.broadcasted_iota(jnp.int32, (TOK, WIDE), 1) % 128) // HALF
    row = lax.broadcasted_iota(jnp.int32, (HEADS_LOCAL * TOK, TOK), 0) % TOK
    col = lax.broadcasted_iota(jnp.int32, (HEADS_LOCAL * TOK, TOK), 1)
    far = lax.broadcasted_iota(jnp.int32, (1, 2 * G_ROWS), 1)
    far_core, j, far_x, far_k = far >> 7, (far >> 4) & 7, (far >> 3) & 1, far & 7
    delta = jnp.where((j & 1) == 1, -((j + 1) >> 1), j >> 1)
    far_z = (z + delta * (1 - 2 * far_core)) & (Z - 1)
    far_ok = ((far_x * Z + far_z) * C + far_core) * TOK + far_k * BLOCK < limit
    far_keys = jnp.concatenate([g_keep[:, :128], g_got[:, :128]], axis=1)
    far_values = jnp.concatenate([g_keep[:, 128:], g_got[:, 128:]], axis=1)

    def local(kind, at):
        lanes = slice(kind * 128, kind * 128 + 128)
        return jnp.concatenate([keep_ref[at : at + TOK, lanes], got_ref[at : at + TOK, lanes]], axis=1)

    def halo(ref, got, kind, seg):
        at = pl.ds(pl.multiple_of(seg * TOK, TOK), TOK)
        lanes = slice(kind * 128 - 128, kind * 128)
        return jnp.concatenate([ref[at, lanes], got[at, lanes]], axis=1)

    for seg in range(2):
        below_seg = jnp.where(z == 0, 1 - seg, seg)
        above_seg = jnp.where(z == Z - 1, 1 - seg, seg)
        for part in range(2):
            base = (seg * Z + z) * 2 * TOK + part * TOK
            at = (seg * 2 + part) * TOK
            queries = local(0, at)
            stacked = jnp.concatenate(
                [jnp.where(lane_head == h, queries, jnp.zeros_like(queries)) for h in range(HEADS_LOCAL)],
                axis=0,
            )

            def neighbours(kind):
                if part == 0:
                    return halo(below_ref, below_got, kind, below_seg), local(kind, at), local(kind, at + TOK)
                return local(kind, at - TOK), local(kind, at), halo(above_ref, above_got, kind, above_seg)

            k_left, k_mid, k_right = neighbours(1)
            v_left, v_mid, v_right = neighbours(2)
            low = base - TOK
            ok_left = (col > row) & (col + low >= 0) & (col + low < limit)
            ok_mid = col + base < limit
            ok_right = (col < row) & (col + (base + TOK) < limit)
            s_left = jnp.where(ok_left, dot_nt(stacked, k_left), NEGATIVE)
            s_mid = jnp.where(ok_mid, dot_nt(stacked, k_mid), NEGATIVE)
            s_right = jnp.where(ok_right, dot_nt(stacked, k_right), NEGATIVE)
            s_far = jnp.where(far_ok, dot_nt(stacked, far_keys), NEGATIVE)
            near_top = jnp.maximum(jnp.maximum(s_left, s_mid), s_right)
            far_top = jnp.maximum(s_far[:, :128], s_far[:, 128:])
            top = jnp.max(jnp.maximum(near_top, far_top), axis=-1, keepdims=True)
            w_left = jnp.exp(s_left - top)
            w_mid = jnp.exp(s_mid - top)
            w_right = jnp.exp(s_right - top)
            w_far = jnp.exp(s_far - top)
            total = jnp.sum(
                w_left + w_mid + w_right + w_far[:, :128] + w_far[:, 128:], axis=-1, keepdims=True
            )

            def mix(weights, values):
                return jnp.dot(
                    weights.astype(jnp.bfloat16), values, preferred_element_type=jnp.float32
                )

            mixed = mix(w_left, v_left) + mix(w_mid, v_mid) + mix(w_right, v_right) + mix(w_far, far_values)
            mixed = mixed / total
            context = jnp.zeros((TOK, WIDE), jnp.float32)
            for h in range(HEADS_LOCAL):
                context = jnp.where(lane_head == h, mixed[h * TOK : (h + 1) * TOK, :], context)
            mine = jnp.where(x == seg, 0, 1)
            out_ref[mine, part * TOK : (part + 1) * TOK, :] = context.astype(jnp.bfloat16)


def output_kernel(index, own_ref, there_ref, mine, prev, nxt, far_a, far_b, keep_ref, send_ref, table):
    z, core, x, y = index[0], index[1], index[2], index[5]
    own, there = own_ref[...], there_ref[...]
    for side in range(X):
        mixed = jnp.where(x == side, own, there)
        table[2 * side] = mixed[:, :128]
        table[2 * side + 1] = mixed[:, 128:]
    full = jnp.concatenate([table[(y + turn) & 3] for turn in (0, 3, 1, 2)], axis=1)
    for j, (way, hops) in enumerate(STEPS):
        zj = z_of(z, core, way, hops)
        here = j * 16
        far = (far_a, here) if j < 4 else (far_b, here - 64)
        weights = [
            ref[at : at + 16, i * 256 : i * 256 + 256]
            for ref, at in ((mine, here), (prev, here), (nxt, here), far)
            for i in range(8)
        ]
        out = jnp.dot(full, jnp.concatenate(weights, axis=0), preferred_element_type=jnp.float32)
        keep = jnp.where(core == 0, out[:TOK], out[TOK:])
        sent = jnp.where(core == 0, out[TOK:], out[:TOK]).astype(jnp.bfloat16)
        for side in range(X):
            lanes = pl.ds(pl.multiple_of((side * Z + zj) * 128, 128), 128)
            keep_ref[:, lanes] = keep[:, side * 128 : side * 128 + 128]
            send_ref[:, lanes] = sent[:, side * 128 : side * 128 + 128]


def on_chip(kernel, out_shape, flops, exps, args, scratch=(), in_hbm=0):
    vmem = pl.BlockSpec(memory_space=pltpu.VMEM)
    specs = [pl.BlockSpec(memory_space=pltpu.SMEM)] + [pl.BlockSpec(memory_space=pltpu.HBM)] * in_hbm
    specs += [vmem] * (len(args) - len(specs))
    return pl.pallas_call(
        kernel,
        out_shape=out_shape,
        in_specs=specs,
        out_specs=jax.tree.map(lambda _: vmem, out_shape),
        scratch_shapes=list(scratch),
        compiler_params=pltpu.CompilerParams(vmem_limit_bytes=VMEM_LIMIT),
        cost_estimate=pl.CostEstimate(flops=flops, bytes_accessed=4 << 20, transcendentals=exps),
    )(*args)


def after(value, *others):
    return lax.optimization_barrier((value, *others))[0]


def per_device(hidden_in, length, attn_gain, global_gain, w_query, w_key, w_value, w_out):
    width = hidden_in.shape[1]
    me = lax.axis_index("seq")
    core = me & 1
    z = (me >> 1) & (Z - 1)
    x = me >> 4
    limit = length[0]
    bf16 = jnp.bfloat16
    y = lax.axis_index("doc") & (Y - 1)
    index = jnp.stack([z, core, x, limit, me * TOK, y]).astype(jnp.int32)

    mine = jnp.stack([w_query.T, w_key.T, w_value.T]).reshape(3, 2, 16, width)
    first = mine[:, 0].reshape(48, width)

    normed, global_mine = on_chip(
        norm_kernel,
        (jax.ShapeDtypeStruct((TOK, width), bf16), jax.ShapeDtypeStruct((TOK // BLOCK, width), bf16)),
        8 * TOK * width,
        0,
        (index, after(hidden_in, first), attn_gain[None], global_gain[None]),
        (
            pltpu.VMEM((TOK, width), bf16),
            pltpu.VMEM((1, width), jnp.float32),
            pltpu.VMEM((1, width), jnp.float32),
            pltpu.SemaphoreType.DMA((3,)),
        ),
        in_hbm=3,
    )
    global_there = send(global_mine, OTHER_X)

    split = after(w_out, first).reshape(X, 2, HEADS_LOCAL, 2, HALF, 64)

    def slab(group):
        at = (y >> 1, group, 0, (y & 1) ^ group, 0, 0)
        return lax.dynamic_slice(split, at, (1, 1, HEADS_LOCAL, 1, HALF, 64)).reshape(128, 64)

    kept = slab(core)
    passed = send(slab(1 - core), OTHER_CORE)
    chip = jnp.concatenate([jnp.where(core == 0, kept, passed), jnp.where(core == 0, passed, kept)], axis=1)
    chip_there = send(chip, OTHER_X)
    both = jnp.concatenate([jnp.where(x == 0, chip, chip_there), jnp.where(x == 0, chip_there, chip)], axis=1)

    second = jnp.concatenate(
        [
            mine[:, 1].reshape(48, width),
            jnp.where(x == 0, global_mine, global_there),
            jnp.where(x == 0, global_there, global_mine),
            jnp.concatenate([both[i * 16 : i * 16 + 16] for i in range(8)], axis=1),
        ],
        axis=0,
    )

    one, two = {(0, 0): first}, {(0, 0): second}
    a_one, a_two, b_one, b_two = first, second, first, second
    for step in range(1, 5):
        if step == 2:
            a_two = b_two = after(second, a_one, b_one)
        if step > 1:
            if step > 3:
                before = one[0, step - 3], one[1, step - 3]
                a_two, b_two = lax.optimization_barrier((a_two, b_two, *before))[:2]
            two[0, step - 1] = a_two = send(a_two, AHEAD)
            two[1, step - 1] = b_two = send(b_two, BEHIND)
        if step > 2:
            before = two[0, step - 1], two[1, step - 1]
            a_one, b_one = lax.optimization_barrier((a_one, b_one, *before))[:2]
        one[0, step] = a_one = send(a_one, AHEAD)
        if step < 4:
            one[1, step] = b_one = send(b_one, BEHIND)
    a_two = after(a_two, one[0, 2], one[1, 2])
    two[0, 4] = send(a_two, AHEAD)
    firsts = [one[s] for s in STEPS]
    seconds = [two[s] for s in STEPS]

    to_send = after(normed, one[0, 1])
    across = send(to_send, OTHER_X)
    beside = send(to_send, OTHER_CORE)
    beside_across = send(across, OTHER_CORE)

    half = jax.ShapeDtypeStruct((ROWS, 3 * 128), bf16)
    keep, to_swap, g_own, far_table, out_own, *edges = on_chip(
        project_kernel,
        (
            half,
            half,
            jax.ShapeDtypeStruct((G_ROWS, width), bf16),
            jax.ShapeDtypeStruct((2 * Z * HALF, width), bf16),
            jax.ShapeDtypeStruct((128, width), bf16),
            *[jax.ShapeDtypeStruct((2 * TOK, 256), bf16)] * 4,
        ),
        2 * ROWS * 768 * width,
        0,
        (index, normed, across, beside, beside_across, *firsts, *seconds),
        (pltpu.VMEM((ROWS, width), bf16), pltpu.VMEM((Z * HALF, width), bf16), pltpu.SemaphoreType.DMA((4,))),
        in_hbm=4,
    )
    got = send(to_swap, OTHER_CORE)
    g_other = send(g_own, OTHER_CORE)

    below = send(edges[2], UP), send(edges[3], UP_CROSS)
    above = send(edges[0], DOWN), send(edges[1], DOWN_CROSS)
    far_half = jax.ShapeDtypeStruct((2 * G_ROWS, 256), bf16)
    g_keep, g_swap = on_chip(
        far_kernel, (far_half, far_half), 2 * 256 * 512 * width, 0, (index, g_own, g_other, far_table)
    )
    g_got = send(g_swap, OTHER_CORE)

    to_pass = out_own
    out_prev = send(to_pass, Y_UP, "doc")
    out_next = send(to_pass, Y_DOWN, "doc")
    out_far_a = send(after(out_prev[:64], *below, *above), Y_UP, "doc")
    out_far_b = send(after(out_next[64:], *below, *above), Y_DOWN, "doc")

    context = on_chip(
        attention_kernel,
        jax.ShapeDtypeStruct((2, 2 * TOK, WIDE), bf16),
        4 * 4 * TOK * 640 * WIDE * 4,
        4 * 4 * TOK * 640,
        (index, keep, got, g_keep, g_got, *below, *above),
    )

    there = send(context[1], OTHER_X)
    kept_part, sent_part = on_chip(
        output_kernel,
        (jax.ShapeDtypeStruct((TOK, width), jnp.float32), jax.ShapeDtypeStruct((TOK, width), bf16)),
        2 * 256 * 512 * width,
        0,
        (index, context[0], there, out_own, out_prev, out_next, out_far_a, out_far_b),
        (pltpu.VMEM((4, 2 * TOK, 128), bf16),),
    )
    return (kept_part + send(sent_part, OTHER_CORE).astype(jnp.float32)).astype(bf16)


def solution(mesh):
    placed = (
        P(("doc", "seq"), None),
        P("doc"),
        P(),
        P(),
        P(None, "seq"),
        P(None, "seq"),
        P(None, "seq"),
        P(None, "seq"),
    )
    return jax.shard_map(
        per_device, mesh=mesh, in_specs=placed, out_specs=P(("doc", "seq"), None), check_vma=False
    )
```

```python
import jax
import jax.numpy as jnp
from jax import lax
from jax.experimental import pallas as pl
from jax.experimental.pallas import tpu as pltpu
from jax.sharding import PartitionSpec as P

HEAD_DIM = 64
BLOCK = 16
RADIUS = 127
NEGATIVE = -1e30
EPSILON = 1e-06

X, Z, C = 2, 8, 2
SEQ_SHARDS = X * Z * C
TOK = 128
HALF = 32
HEADS_LOCAL = 4
WIDE = HEADS_LOCAL * HEAD_DIM


def place(x, z, core):
    return (x * Z + z) * C + core


def pairs(move):
    return [
        (place(x, z, c), place(*move(x, z, c))) for x in range(X) for z in range(Z) for c in range(C)
    ]


OTHER_CORE = pairs(lambda x, z, c: (x, z, 1 - c))
OTHER_X = pairs(lambda x, z, c: (1 - x, z, c))
AHEAD = pairs(lambda x, z, c: (x, (z + (1 if c == 0 else -1)) % Z, c))
BEHIND = pairs(lambda x, z, c: (x, (z - (1 if c == 0 else -1)) % Z, c))
UP = pairs(lambda x, z, c: (x, (z + 1) % Z, c))
DOWN = pairs(lambda x, z, c: (x, (z - 1) % Z, c))


Y = 4
Y_UP = [(d, (d & 4) | ((d + 1) & 3)) for d in range(2 * Y)]
Y_DOWN = [(d, (d & 4) | ((d - 1) & 3)) for d in range(2 * Y)]


UP_CROSS = pairs(lambda x, z, c: (x, (z + 1) % Z, 1 - c))
DOWN_CROSS = pairs(lambda x, z, c: (x, (z - 1) % Z, 1 - c))


def send(value, route, axis="seq"):
    return lax.ppermute(value, axis, route)


def rms_norm(values, gain_row):
    mean_square = jnp.mean(values * values, axis=-1, keepdims=True)
    return values * lax.rsqrt(mean_square + EPSILON) * gain_row


def norm_kernel(index, hidden_in, gain_in, global_in, normed_ref, blocks_ref, hidden, gain, global_gain, sems):
    copies = [
        pltpu.make_async_copy(source, into, sems.at[i])
        for i, (source, into) in enumerate(((hidden_in, hidden), (gain_in, gain), (global_in, global_gain)))
    ]
    for copy in copies:
        copy.start()
    for copy in copies:
        copy.wait()
    normed = rms_norm(hidden[...].astype(jnp.float32), gain[...]).astype(jnp.bfloat16)
    normed_ref[...] = normed
    at = index[4] + lax.broadcasted_iota(jnp.int32, (TOK, 1), 0)
    valid = (at < index[3]).astype(jnp.float32)
    kept = (normed.astype(jnp.float32) * valid).reshape(TOK // BLOCK, BLOCK, normed.shape[1])
    blocks_ref[...] = rms_norm(jnp.sum(kept, axis=1), global_gain[...]).astype(jnp.bfloat16)


def dot_nt(left, right):
    return lax.dot_general(
        left, right, (((1,), (1,)), ((), ())), preferred_element_type=jnp.float32
    )


STEPS = ((0, 0), (0, 1), (1, 1), (0, 2), (1, 2), (0, 3), (1, 3), (0, 4))
SHARDS = len(STEPS)
ROWS = 4 * TOK
G_ROWS = Z * 16
VMEM_LIMIT = 32 * 1024 * 1024


def z_of(z, core, way, hops):
    delta = -hops if way == 0 else hops
    return (z + delta * (1 - 2 * core)) & (Z - 1)


def project_kernel(index, *refs):
    blocks, firsts, seconds = refs[:4], refs[4 : 4 + SHARDS], refs[4 + SHARDS : 4 + 2 * SHARDS]
    keep_ref, send_ref, g_rows, far_table, out_rows, *edges, rows, table, sems = refs[4 + 2 * SHARDS :]
    z, core, x = index[0], index[1], index[2]
    low_core = core == 0
    copies = []
    for i, (ref, bx, bc) in enumerate(zip(blocks, (x, 1 - x, x, 1 - x), (core, core, 1 - core, 1 - core))):
        into = rows.at[pl.ds(pl.multiple_of((bx * 2 + bc) * TOK, TOK), TOK), :]
        copies.append(pltpu.make_async_copy(ref, into, sems.at[i]))
        copies[-1].start()
    for j, (way, hops) in enumerate(STEPS):
        at = z_of(z, core, way, hops) * HALF
        for kind in range(3):
            into = table if kind == 0 else far_table
            base = 0 if kind == 0 else kind * 256 - 256
            here = pl.multiple_of(base + at, 16)
            into[pl.ds(here, 16), :] = firsts[j][kind * 16 : kind * 16 + 16, :]
            there = pl.multiple_of(base + at + 16, 16)
            into[pl.ds(there, 16), :] = seconds[j][kind * 16 : kind * 16 + 16, :]
        g_rows[j * 16 : j * 16 + 16, :] = seconds[j][48:64, :]
        out_rows[j * 16 : j * 16 + 16, :] = seconds[j][64:80, :]
    for copy in copies:
        copy.wait()
    for kind in range(3):
        columns = table[...] if kind == 0 else far_table[kind * 256 - 256 : kind * 256, :]
        out = dot_nt(rows[...], columns).astype(jnp.bfloat16)
        lanes = slice(kind * 128, kind * 128 + 128)
        keep_ref[:, lanes] = jnp.where(low_core, out[:, :128], out[:, 128:])
        send_ref[:, lanes] = jnp.where(low_core, out[:, 128:], out[:, :128])
        if kind:
            lanes_out = slice(kind * 128 - 128, kind * 128)
            for part in range(2):
                for seg in range(2):
                    at = slice((seg * 2 + part) * TOK, (seg * 2 + part + 1) * TOK)
                    into = slice(seg * TOK, seg * TOK + TOK)
                    edges[2 * part][into, lanes_out] = keep_ref[at, lanes]
                    edges[2 * part + 1][into, lanes_out] = send_ref[at, lanes]


def far_kernel(index, own_ref, other_ref, table, keep_ref, send_ref):
    low_core = index[1] == 0
    for source in range(2):
        rows = jnp.where(index[1] == source, own_ref[...], other_ref[...])
        at = slice(source * G_ROWS, source * G_ROWS + G_ROWS)
        for kind in range(2):
            out = dot_nt(rows, table[kind * 256 : kind * 256 + 256, :]).astype(jnp.bfloat16)
            lanes = slice(kind * 128, kind * 128 + 128)
            keep_ref[at, lanes] = jnp.where(low_core, out[:, :128], out[:, 128:])
            send_ref[at, lanes] = jnp.where(low_core, out[:, 128:], out[:, :128])


def attention_kernel(index, keep_ref, got_ref, g_keep, g_got, below_ref, below_got, above_ref, above_got, out_ref):
    z, x, limit = index[0], index[2], index[3]
    lane_head = (lax.broadcasted_iota(jnp.int32, (TOK, WIDE), 1) % 128) // HALF
    row = lax.broadcasted_iota(jnp.int32, (HEADS_LOCAL * TOK, TOK), 0) % TOK
    col = lax.broadcasted_iota(jnp.int32, (HEADS_LOCAL * TOK, TOK), 1)
    far = lax.broadcasted_iota(jnp.int32, (1, 2 * G_ROWS), 1)
    far_core, j, far_x, far_k = far >> 7, (far >> 4) & 7, (far >> 3) & 1, far & 7
    delta = jnp.where((j & 1) == 1, -((j + 1) >> 1), j >> 1)
    far_z = (z + delta * (1 - 2 * far_core)) & (Z - 1)
    far_ok = ((far_x * Z + far_z) * C + far_core) * TOK + far_k * BLOCK < limit
    far_keys = jnp.concatenate([g_keep[:, :128], g_got[:, :128]], axis=1)
    far_values = jnp.concatenate([g_keep[:, 128:], g_got[:, 128:]], axis=1)

    def local(kind, at):
        lanes = slice(kind * 128, kind * 128 + 128)
        return jnp.concatenate([keep_ref[at : at + TOK, lanes], got_ref[at : at + TOK, lanes]], axis=1)

    def halo(ref, got, kind, seg):
        at = pl.ds(pl.multiple_of(seg * TOK, TOK), TOK)
        lanes = slice(kind * 128 - 128, kind * 128)
        return jnp.concatenate([ref[at, lanes], got[at, lanes]], axis=1)

    for seg in range(2):
        below_seg = jnp.where(z == 0, 1 - seg, seg)
        above_seg = jnp.where(z == Z - 1, 1 - seg, seg)
        for part in range(2):
            base = (seg * Z + z) * 2 * TOK + part * TOK
            at = (seg * 2 + part) * TOK
            queries = local(0, at)
            stacked = jnp.concatenate(
                [jnp.where(lane_head == h, queries, jnp.zeros_like(queries)) for h in range(HEADS_LOCAL)],
                axis=0,
            )

            def neighbours(kind):
                if part == 0:
                    return halo(below_ref, below_got, kind, below_seg), local(kind, at), local(kind, at + TOK)
                return local(kind, at - TOK), local(kind, at), halo(above_ref, above_got, kind, above_seg)

            k_left, k_mid, k_right = neighbours(1)
            v_left, v_mid, v_right = neighbours(2)
            low = base - TOK
            ok_left = (col > row) & (col + low >= 0) & (col + low < limit)
            ok_mid = col + base < limit
            ok_right = (col < row) & (col + (base + TOK) < limit)
            s_left = jnp.where(ok_left, dot_nt(stacked, k_left), NEGATIVE)
            s_mid = jnp.where(ok_mid, dot_nt(stacked, k_mid), NEGATIVE)
            s_right = jnp.where(ok_right, dot_nt(stacked, k_right), NEGATIVE)
            s_far = jnp.where(far_ok, dot_nt(stacked, far_keys), NEGATIVE)
            near_top = jnp.maximum(jnp.maximum(s_left, s_mid), s_right)
            far_top = jnp.maximum(s_far[:, :128], s_far[:, 128:])
            top = jnp.max(jnp.maximum(near_top, far_top), axis=-1, keepdims=True)
            w_left = jnp.exp(s_left - top)
            w_mid = jnp.exp(s_mid - top)
            w_right = jnp.exp(s_right - top)
            w_far = jnp.exp(s_far - top)
            total = jnp.sum(
                w_left + w_mid + w_right + w_far[:, :128] + w_far[:, 128:], axis=-1, keepdims=True
            )

            def mix(weights, values):
                return jnp.dot(
                    weights.astype(jnp.bfloat16), values, preferred_element_type=jnp.float32
                )

            mixed = mix(w_left, v_left) + mix(w_mid, v_mid) + mix(w_right, v_right) + mix(w_far, far_values)
            mixed = mixed / total
            context = jnp.zeros((TOK, WIDE), jnp.float32)
            for h in range(HEADS_LOCAL):
                context = jnp.where(lane_head == h, mixed[h * TOK : (h + 1) * TOK, :], context)
            mine = jnp.where(x == seg, 0, 1)
            out_ref[mine, part * TOK : (part + 1) * TOK, :] = context.astype(jnp.bfloat16)


def output_kernel(index, own_ref, there_ref, mine, prev, nxt, far_a, far_b, keep_ref, send_ref, table):
    z, core, x, y = index[0], index[1], index[2], index[5]
    own, there = own_ref[...], there_ref[...]
    for side in range(X):
        mixed = jnp.where(x == side, own, there)
        table[2 * side] = mixed[:, :128]
        table[2 * side + 1] = mixed[:, 128:]
    full = jnp.concatenate([table[(y + turn) & 3] for turn in (0, 3, 1, 2)], axis=1)
    for j, (way, hops) in enumerate(STEPS):
        zj = z_of(z, core, way, hops)
        here = j * 16
        far = (far_a, here) if j < 4 else (far_b, here - 64)
        weights = [
            ref[at : at + 16, i * 256 : i * 256 + 256]
            for ref, at in ((mine, here), (prev, here), (nxt, here), far)
            for i in range(8)
        ]
        out = jnp.dot(full, jnp.concatenate(weights, axis=0), preferred_element_type=jnp.float32)
        keep = jnp.where(core == 0, out[:TOK], out[TOK:])
        sent = jnp.where(core == 0, out[TOK:], out[:TOK]).astype(jnp.bfloat16)
        for side in range(X):
            lanes = pl.ds(pl.multiple_of((side * Z + zj) * 128, 128), 128)
            keep_ref[:, lanes] = keep[:, side * 128 : side * 128 + 128]
            send_ref[:, lanes] = sent[:, side * 128 : side * 128 + 128]


def on_chip(kernel, out_shape, flops, exps, args, scratch=(), in_hbm=0):
    vmem = pl.BlockSpec(memory_space=pltpu.VMEM)
    specs = [pl.BlockSpec(memory_space=pltpu.SMEM)] + [pl.BlockSpec(memory_space=pltpu.HBM)] * in_hbm
    specs += [vmem] * (len(args) - len(specs))
    return pl.pallas_call(
        kernel,
        out_shape=out_shape,
        in_specs=specs,
        out_specs=jax.tree.map(lambda _: vmem, out_shape),
        scratch_shapes=list(scratch),
        compiler_params=pltpu.CompilerParams(vmem_limit_bytes=VMEM_LIMIT),
        cost_estimate=pl.CostEstimate(flops=flops, bytes_accessed=4 << 20, transcendentals=exps),
    )(*args)


def after(value, *others):
    return lax.optimization_barrier((value, *others))[0]


def per_device(hidden_in, length, attn_gain, global_gain, w_query, w_key, w_value, w_out):
    width = hidden_in.shape[1]
    me = lax.axis_index("seq")
    core = me & 1
    z = (me >> 1) & (Z - 1)
    x = me >> 4
    limit = length[0]
    bf16 = jnp.bfloat16
    y = lax.axis_index("doc") & (Y - 1)
    index = jnp.stack([z, core, x, limit, me * TOK, y]).astype(jnp.int32)

    mine = jnp.stack([w_query.T, w_key.T, w_value.T]).reshape(3, 2, 16, width)
    first = mine[:, 0].reshape(48, width)

    normed, global_mine = on_chip(
        norm_kernel,
        (jax.ShapeDtypeStruct((TOK, width), bf16), jax.ShapeDtypeStruct((TOK // BLOCK, width), bf16)),
        8 * TOK * width,
        0,
        (index, after(hidden_in, first), attn_gain[None], global_gain[None]),
        (
            pltpu.VMEM((TOK, width), bf16),
            pltpu.VMEM((1, width), jnp.float32),
            pltpu.VMEM((1, width), jnp.float32),
            pltpu.SemaphoreType.DMA((3,)),
        ),
        in_hbm=3,
    )
    global_there = send(global_mine, OTHER_X)

    split = after(w_out, first).reshape(X, 2, HEADS_LOCAL, 2, HALF, 64)

    def slab(group):
        at = (y >> 1, group, 0, (y & 1) ^ group, 0, 0)
        return lax.dynamic_slice(split, at, (1, 1, HEADS_LOCAL, 1, HALF, 64)).reshape(128, 64)

    kept = slab(core)
    passed = send(slab(1 - core), OTHER_CORE)
    chip = jnp.concatenate([jnp.where(core == 0, kept, passed), jnp.where(core == 0, passed, kept)], axis=1)
    chip_there = send(chip, OTHER_X)
    both = jnp.concatenate([jnp.where(x == 0, chip, chip_there), jnp.where(x == 0, chip_there, chip)], axis=1)

    second = jnp.concatenate(
        [
            mine[:, 1].reshape(48, width),
            jnp.where(x == 0, global_mine, global_there),
            jnp.where(x == 0, global_there, global_mine),
            jnp.concatenate([both[i * 16 : i * 16 + 16] for i in range(8)], axis=1),
        ],
        axis=0,
    )

    one, two = {(0, 0): first}, {(0, 0): second}
    a_one, a_two, b_one, b_two = first, second, first, second
    for step in range(1, 5):
        if step == 2:
            to_send = after(normed, one[0, 1])
            across = send(to_send, OTHER_X)
            beside = send(to_send, OTHER_CORE)
            beside_across = send(across, OTHER_CORE)
            a_two = b_two = after(second, a_one, b_one)
        if step > 1:
            if step > 2:
                before = one[0, step - 2], one[1, step - 2]
                if step == 4:
                    before = *before, across, beside, beside_across
                a_two, b_two = lax.optimization_barrier((a_two, b_two, *before))[:2]
            two[0, step - 1] = a_two = send(a_two, AHEAD)
            two[1, step - 1] = b_two = send(b_two, BEHIND)
        if step > 2:
            before = two[0, step - 2], two[1, step - 2]
            if step == 3:
                before = *before, across, beside, beside_across
            a_one, b_one = lax.optimization_barrier((a_one, b_one, *before))[:2]
        one[0, step] = a_one = send(a_one, AHEAD)
        if step < 4:
            one[1, step] = b_one = send(b_one, BEHIND)
    a_two = after(a_two, one[0, 3], one[1, 3])
    two[0, 4] = send(a_two, AHEAD)
    firsts = [one[s] for s in STEPS]
    seconds = [two[s] for s in STEPS]

    half = jax.ShapeDtypeStruct((ROWS, 3 * 128), bf16)
    keep, to_swap, g_own, far_table, out_own, *edges = on_chip(
        project_kernel,
        (
            half,
            half,
            jax.ShapeDtypeStruct((G_ROWS, width), bf16),
            jax.ShapeDtypeStruct((2 * Z * HALF, width), bf16),
            jax.ShapeDtypeStruct((128, width), bf16),
            *[jax.ShapeDtypeStruct((2 * TOK, 256), bf16)] * 4,
        ),
        2 * ROWS * 768 * width,
        0,
        (index, normed, across, beside, beside_across, *firsts, *seconds),
        (pltpu.VMEM((ROWS, width), bf16), pltpu.VMEM((Z * HALF, width), bf16), pltpu.SemaphoreType.DMA((4,))),
        in_hbm=4,
    )
    got = send(to_swap, OTHER_CORE)
    g_other = send(g_own, OTHER_CORE)
    g_other, got = lax.optimization_barrier((g_other, got))

    below = send(edges[2], UP), send(edges[3], UP_CROSS)
    above = send(edges[0], DOWN), send(edges[1], DOWN_CROSS)
    far_half = jax.ShapeDtypeStruct((2 * G_ROWS, 256), bf16)
    g_keep, g_swap = on_chip(
        far_kernel, (far_half, far_half), 2 * 256 * 512 * width, 0, (index, g_own, g_other, far_table)
    )
    g_got = send(g_swap, OTHER_CORE)

    to_pass = out_own
    out_prev = send(to_pass, Y_UP, "doc")
    out_next = send(to_pass, Y_DOWN, "doc")
    out_far_a = send(out_prev[:64], Y_UP, "doc")
    out_far_b = send(out_next[64:], Y_DOWN, "doc")

    context = on_chip(
        attention_kernel,
        jax.ShapeDtypeStruct((2, 2 * TOK, WIDE), bf16),
        4 * 4 * TOK * 640 * WIDE * 4,
        4 * 4 * TOK * 640,
        (index, keep, got, g_keep, g_got, *below, *above),
    )

    there = send(context[1], OTHER_X)
    kept_part, sent_part = on_chip(
        output_kernel,
        (jax.ShapeDtypeStruct((TOK, width), jnp.float32), jax.ShapeDtypeStruct((TOK, width), bf16)),
        2 * 256 * 512 * width,
        0,
        (index, context[0], there, out_own, out_prev, out_next, out_far_a, out_far_b),
        (pltpu.VMEM((4, 2 * TOK, 128), bf16),),
    )
    return (kept_part + send(sent_part, OTHER_CORE).astype(jnp.float32)).astype(bf16)


def solution(mesh):
    placed = (
        P(("doc", "seq"), None),
        P("doc"),
        P(),
        P(),
        P(None, "seq"),
        P(None, "seq"),
        P(None, "seq"),
        P(None, "seq"),
    )
    return jax.shard_map(
        per_device, mesh=mesh, in_specs=placed, out_specs=P(("doc", "seq"), None), check_vma=False
    )
```

```python
import jax
import jax.numpy as jnp
from jax import lax
from jax.experimental import pallas as pl
from jax.experimental.pallas import tpu as pltpu
from jax.sharding import PartitionSpec as P

HEAD_DIM = 64
BLOCK = 16
RADIUS = 127
NEGATIVE = -1e30
EPSILON = 1e-06

X, Z, C = 2, 8, 2
SEQ_SHARDS = X * Z * C
TOK = 128
HALF = 32
HEADS_LOCAL = 4
WIDE = HEADS_LOCAL * HEAD_DIM


def place(x, z, core):
    return (x * Z + z) * C + core


def pairs(move):
    return [
        (place(x, z, c), place(*move(x, z, c))) for x in range(X) for z in range(Z) for c in range(C)
    ]


OTHER_CORE = pairs(lambda x, z, c: (x, z, 1 - c))
OTHER_X = pairs(lambda x, z, c: (1 - x, z, c))
AHEAD = pairs(lambda x, z, c: (x, (z + (1 if c == 0 else -1)) % Z, c))
BEHIND = pairs(lambda x, z, c: (x, (z - (1 if c == 0 else -1)) % Z, c))
UP = pairs(lambda x, z, c: (x, (z + 1) % Z, c))
DOWN = pairs(lambda x, z, c: (x, (z - 1) % Z, c))


Y = 4
Y_UP = [(d, (d & 4) | ((d + 1) & 3)) for d in range(2 * Y)]
Y_DOWN = [(d, (d & 4) | ((d - 1) & 3)) for d in range(2 * Y)]


UP_CROSS = pairs(lambda x, z, c: (x, (z + 1) % Z, 1 - c))
DOWN_CROSS = pairs(lambda x, z, c: (x, (z - 1) % Z, 1 - c))


def send(value, route, axis="seq"):
    return lax.ppermute(value, axis, route)


def rms_norm(values, gain_row):
    mean_square = jnp.mean(values * values, axis=-1, keepdims=True)
    return values * lax.rsqrt(mean_square + EPSILON) * gain_row


def norm_kernel(index, hidden_in, gain_in, global_in, normed_ref, blocks_ref, hidden, gain, global_gain, sems):
    copies = [
        pltpu.make_async_copy(source, into, sems.at[i])
        for i, (source, into) in enumerate(((hidden_in, hidden), (gain_in, gain), (global_in, global_gain)))
    ]
    for copy in copies:
        copy.start()
    for copy in copies:
        copy.wait()
    normed = rms_norm(hidden[...].astype(jnp.float32), gain[...]).astype(jnp.bfloat16)
    normed_ref[...] = normed
    at = index[4] + lax.broadcasted_iota(jnp.int32, (TOK, 1), 0)
    valid = (at < index[3]).astype(jnp.float32)
    kept = (normed.astype(jnp.float32) * valid).reshape(TOK // BLOCK, BLOCK, normed.shape[1])
    blocks_ref[...] = rms_norm(jnp.sum(kept, axis=1), global_gain[...]).astype(jnp.bfloat16)


def dot_nt(left, right):
    return lax.dot_general(
        left, right, (((1,), (1,)), ((), ())), preferred_element_type=jnp.float32
    )


STEPS = ((0, 0), (0, 1), (1, 1), (0, 2), (1, 2), (0, 3), (1, 3), (0, 4))
SHARDS = len(STEPS)
ROWS = 4 * TOK
G_ROWS = Z * 16
VMEM_LIMIT = 32 * 1024 * 1024


def z_of(z, core, way, hops):
    delta = -hops if way == 0 else hops
    return (z + delta * (1 - 2 * core)) & (Z - 1)


def project_kernel(index, *refs):
    blocks, firsts, seconds = refs[:4], refs[4 : 4 + SHARDS], refs[4 + SHARDS : 4 + 2 * SHARDS]
    keep_ref, send_ref, g_rows, far_table, *edges, rows, table, sems = refs[4 + 2 * SHARDS :]
    z, core, x = index[0], index[1], index[2]
    low_core = core == 0
    copies = []
    for i, (ref, bx, bc) in enumerate(zip(blocks, (x, 1 - x, x, 1 - x), (core, core, 1 - core, 1 - core))):
        into = rows.at[pl.ds(pl.multiple_of((bx * 2 + bc) * TOK, TOK), TOK), :]
        copies.append(pltpu.make_async_copy(ref, into, sems.at[i]))
        copies[-1].start()
    for j, (way, hops) in enumerate(STEPS):
        at = z_of(z, core, way, hops) * HALF
        for kind in range(3):
            into = table if kind == 0 else far_table
            base = 0 if kind == 0 else kind * 256 - 256
            here = pl.multiple_of(base + at, 16)
            into[pl.ds(here, 16), :] = firsts[j][kind * 16 : kind * 16 + 16, :]
            there = pl.multiple_of(base + at + 16, 16)
            into[pl.ds(there, 16), :] = seconds[j][kind * 16 : kind * 16 + 16, :]
        g_rows[j * 16 : j * 16 + 16, :] = seconds[j][48:64, :]
    for copy in copies:
        copy.wait()
    for kind in range(3):
        columns = table[...] if kind == 0 else far_table[kind * 256 - 256 : kind * 256, :]
        out = dot_nt(rows[...], columns).astype(jnp.bfloat16)
        lanes = slice(kind * 128, kind * 128 + 128)
        keep_ref[:, lanes] = jnp.where(low_core, out[:, :128], out[:, 128:])
        send_ref[:, lanes] = jnp.where(low_core, out[:, 128:], out[:, :128])
        if kind:
            lanes_out = slice(kind * 128 - 128, kind * 128)
            for part in range(2):
                for seg in range(2):
                    at = slice((seg * 2 + part) * TOK, (seg * 2 + part + 1) * TOK)
                    into = slice(seg * TOK, seg * TOK + TOK)
                    edges[2 * part][into, lanes_out] = keep_ref[at, lanes]
                    edges[2 * part + 1][into, lanes_out] = send_ref[at, lanes]


def collect_kernel(*refs):
    for j, ref in enumerate(refs[1 : 1 + SHARDS]):
        refs[1 + SHARDS][j * 16 : j * 16 + 16, :] = ref[64:80, :]


def far_kernel(index, own_ref, other_ref, table, keep_ref, send_ref):
    low_core = index[1] == 0
    for source in range(2):
        rows = jnp.where(index[1] == source, own_ref[...], other_ref[...])
        at = slice(source * G_ROWS, source * G_ROWS + G_ROWS)
        for kind in range(2):
            out = dot_nt(rows, table[kind * 256 : kind * 256 + 256, :]).astype(jnp.bfloat16)
            lanes = slice(kind * 128, kind * 128 + 128)
            keep_ref[at, lanes] = jnp.where(low_core, out[:, :128], out[:, 128:])
            send_ref[at, lanes] = jnp.where(low_core, out[:, 128:], out[:, :128])


def attention_kernel(index, keep_ref, got_ref, g_keep, g_got, below_ref, below_got, above_ref, above_got, out_ref):
    z, x, limit = index[0], index[2], index[3]
    lane_head = (lax.broadcasted_iota(jnp.int32, (TOK, WIDE), 1) % 128) // HALF
    row = lax.broadcasted_iota(jnp.int32, (HEADS_LOCAL * TOK, TOK), 0) % TOK
    col = lax.broadcasted_iota(jnp.int32, (HEADS_LOCAL * TOK, TOK), 1)
    far = lax.broadcasted_iota(jnp.int32, (1, 2 * G_ROWS), 1)
    far_core, j, far_x, far_k = far >> 7, (far >> 4) & 7, (far >> 3) & 1, far & 7
    delta = jnp.where((j & 1) == 1, -((j + 1) >> 1), j >> 1)
    far_z = (z + delta * (1 - 2 * far_core)) & (Z - 1)
    far_ok = ((far_x * Z + far_z) * C + far_core) * TOK + far_k * BLOCK < limit
    far_keys = jnp.concatenate([g_keep[:, :128], g_got[:, :128]], axis=1)
    far_values = jnp.concatenate([g_keep[:, 128:], g_got[:, 128:]], axis=1)

    def local(kind, at):
        lanes = slice(kind * 128, kind * 128 + 128)
        return jnp.concatenate([keep_ref[at : at + TOK, lanes], got_ref[at : at + TOK, lanes]], axis=1)

    def halo(ref, got, kind, seg):
        at = pl.ds(pl.multiple_of(seg * TOK, TOK), TOK)
        lanes = slice(kind * 128 - 128, kind * 128)
        return jnp.concatenate([ref[at, lanes], got[at, lanes]], axis=1)

    for seg in range(2):
        below_seg = jnp.where(z == 0, 1 - seg, seg)
        above_seg = jnp.where(z == Z - 1, 1 - seg, seg)
        for part in range(2):
            base = (seg * Z + z) * 2 * TOK + part * TOK
            at = (seg * 2 + part) * TOK
            queries = local(0, at)
            stacked = jnp.concatenate(
                [jnp.where(lane_head == h, queries, jnp.zeros_like(queries)) for h in range(HEADS_LOCAL)],
                axis=0,
            )

            def neighbours(kind):
                if part == 0:
                    return halo(below_ref, below_got, kind, below_seg), local(kind, at), local(kind, at + TOK)
                return local(kind, at - TOK), local(kind, at), halo(above_ref, above_got, kind, above_seg)

            k_left, k_mid, k_right = neighbours(1)
            v_left, v_mid, v_right = neighbours(2)
            low = base - TOK
            ok_left = (col > row) & (col + low >= 0) & (col + low < limit)
            ok_mid = col + base < limit
            ok_right = (col < row) & (col + (base + TOK) < limit)
            s_left = jnp.where(ok_left, dot_nt(stacked, k_left), NEGATIVE)
            s_mid = jnp.where(ok_mid, dot_nt(stacked, k_mid), NEGATIVE)
            s_right = jnp.where(ok_right, dot_nt(stacked, k_right), NEGATIVE)
            s_far = jnp.where(far_ok, dot_nt(stacked, far_keys), NEGATIVE)
            near_top = jnp.maximum(jnp.maximum(s_left, s_mid), s_right)
            far_top = jnp.maximum(s_far[:, :128], s_far[:, 128:])
            top = jnp.max(jnp.maximum(near_top, far_top), axis=-1, keepdims=True)
            w_left = jnp.exp(s_left - top)
            w_mid = jnp.exp(s_mid - top)
            w_right = jnp.exp(s_right - top)
            w_far = jnp.exp(s_far - top)
            total = jnp.sum(
                w_left + w_mid + w_right + w_far[:, :128] + w_far[:, 128:], axis=-1, keepdims=True
            )

            def mix(weights, values):
                return jnp.dot(
                    weights.astype(jnp.bfloat16), values, preferred_element_type=jnp.float32
                )

            mixed = mix(w_left, v_left) + mix(w_mid, v_mid) + mix(w_right, v_right) + mix(w_far, far_values)
            mixed = mixed / total
            context = jnp.zeros((TOK, WIDE), jnp.float32)
            for h in range(HEADS_LOCAL):
                context = jnp.where(lane_head == h, mixed[h * TOK : (h + 1) * TOK, :], context)
            mine = jnp.where(x == seg, 0, 1)
            out_ref[mine, part * TOK : (part + 1) * TOK, :] = context.astype(jnp.bfloat16)


def output_kernel(index, own_ref, there_ref, mine, prev, nxt, far_a, far_b, keep_ref, send_ref, table):
    z, core, x, y = index[0], index[1], index[2], index[5]
    own, there = own_ref[...], there_ref[...]
    for side in range(X):
        mixed = jnp.where(x == side, own, there)
        table[2 * side] = mixed[:, :128]
        table[2 * side + 1] = mixed[:, 128:]
    full = jnp.concatenate([table[(y + turn) & 3] for turn in (0, 3, 1, 2)], axis=1)
    for j, (way, hops) in enumerate(STEPS):
        zj = z_of(z, core, way, hops)
        here = j * 16
        far = (far_a, here) if j < 4 else (far_b, here - 64)
        weights = [
            ref[at : at + 16, i * 256 : i * 256 + 256]
            for ref, at in ((mine, here), (prev, here), (nxt, here), far)
            for i in range(8)
        ]
        out = jnp.dot(full, jnp.concatenate(weights, axis=0), preferred_element_type=jnp.float32)
        keep = jnp.where(core == 0, out[:TOK], out[TOK:])
        sent = jnp.where(core == 0, out[TOK:], out[:TOK]).astype(jnp.bfloat16)
        for side in range(X):
            lanes = pl.ds(pl.multiple_of((side * Z + zj) * 128, 128), 128)
            keep_ref[:, lanes] = keep[:, side * 128 : side * 128 + 128]
            send_ref[:, lanes] = sent[:, side * 128 : side * 128 + 128]


def on_chip(kernel, out_shape, flops, exps, args, scratch=(), in_hbm=0):
    vmem = pl.BlockSpec(memory_space=pltpu.VMEM)
    specs = [pl.BlockSpec(memory_space=pltpu.SMEM)] + [pl.BlockSpec(memory_space=pltpu.HBM)] * in_hbm
    specs += [vmem] * (len(args) - len(specs))
    return pl.pallas_call(
        kernel,
        out_shape=out_shape,
        in_specs=specs,
        out_specs=jax.tree.map(lambda _: vmem, out_shape),
        scratch_shapes=list(scratch),
        compiler_params=pltpu.CompilerParams(vmem_limit_bytes=VMEM_LIMIT),
        cost_estimate=pl.CostEstimate(flops=flops, bytes_accessed=4 << 20, transcendentals=exps),
    )(*args)


def after(value, *others):
    return lax.optimization_barrier((value, *others))[0]


def per_device(hidden_in, length, attn_gain, global_gain, w_query, w_key, w_value, w_out):
    width = hidden_in.shape[1]
    me = lax.axis_index("seq")
    core = me & 1
    z = (me >> 1) & (Z - 1)
    x = me >> 4
    limit = length[0]
    bf16 = jnp.bfloat16
    y = lax.axis_index("doc") & (Y - 1)
    index = jnp.stack([z, core, x, limit, me * TOK, y]).astype(jnp.int32)

    mine = jnp.stack([w_query.T, w_key.T, w_value.T]).reshape(3, 2, 16, width)
    first = mine[:, 0].reshape(48, width)

    normed, global_mine = on_chip(
        norm_kernel,
        (jax.ShapeDtypeStruct((TOK, width), bf16), jax.ShapeDtypeStruct((TOK // BLOCK, width), bf16)),
        8 * TOK * width,
        0,
        (index, after(hidden_in, first), attn_gain[None], global_gain[None]),
        (
            pltpu.VMEM((TOK, width), bf16),
            pltpu.VMEM((1, width), jnp.float32),
            pltpu.VMEM((1, width), jnp.float32),
            pltpu.SemaphoreType.DMA((3,)),
        ),
        in_hbm=3,
    )
    global_there = send(global_mine, OTHER_X)

    split = after(w_out, first).reshape(X, 2, HEADS_LOCAL, 2, HALF, 64)

    def slab(group):
        at = (y >> 1, group, 0, (y & 1) ^ group, 0, 0)
        return lax.dynamic_slice(split, at, (1, 1, HEADS_LOCAL, 1, HALF, 64)).reshape(128, 64)

    kept = slab(core)
    passed = send(slab(1 - core), OTHER_CORE)
    chip = jnp.concatenate([jnp.where(core == 0, kept, passed), jnp.where(core == 0, passed, kept)], axis=1)
    chip_there = send(chip, OTHER_X)
    both = jnp.concatenate([jnp.where(x == 0, chip, chip_there), jnp.where(x == 0, chip_there, chip)], axis=1)

    second = jnp.concatenate(
        [
            mine[:, 1].reshape(48, width),
            jnp.where(x == 0, global_mine, global_there),
            jnp.where(x == 0, global_there, global_mine),
            jnp.concatenate([both[i * 16 : i * 16 + 16] for i in range(8)], axis=1),
        ],
        axis=0,
    )

    one, two = {(0, 0): first}, {(0, 0): second}
    a_one, a_two, b_one, b_two = first, second, first, second
    for step in range(1, 5):
        if step == 2:
            a_two = b_two = after(second, a_one, b_one)
        if step > 1:
            if step > 2:
                before = one[0, step - 2], one[1, step - 2]
                a_two, b_two = lax.optimization_barrier((a_two, b_two, *before))[:2]
            two[0, step - 1] = a_two = send(a_two, AHEAD)
            two[1, step - 1] = b_two = send(b_two, BEHIND)
        if step > 2:
            before = two[0, step - 2], two[1, step - 2]
            a_one, b_one = lax.optimization_barrier((a_one, b_one, *before))[:2]
        one[0, step] = a_one = send(a_one, AHEAD)
        if step < 4:
            one[1, step] = b_one = send(b_one, BEHIND)
    a_two = after(a_two, one[0, 3], one[1, 3])
    two[0, 4] = send(a_two, AHEAD)
    firsts = [one[s] for s in STEPS]
    seconds = [two[s] for s in STEPS]

    to_send = after(normed, one[0, 2])
    across = send(to_send, OTHER_X)
    beside = send(to_send, OTHER_CORE)
    beside_across = send(across, OTHER_CORE)

    half = jax.ShapeDtypeStruct((ROWS, 3 * 128), bf16)
    keep, to_swap, g_own, far_table, *edges = on_chip(
        project_kernel,
        (
            half,
            half,
            jax.ShapeDtypeStruct((G_ROWS, width), bf16),
            jax.ShapeDtypeStruct((2 * Z * HALF, width), bf16),
            *[jax.ShapeDtypeStruct((2 * TOK, 256), bf16)] * 4,
        ),
        2 * ROWS * 768 * width,
        0,
        (index, normed, across, beside, beside_across, *firsts, *seconds),
        (pltpu.VMEM((ROWS, width), bf16), pltpu.VMEM((Z * HALF, width), bf16), pltpu.SemaphoreType.DMA((4,))),
        in_hbm=4,
    )
    got = send(to_swap, OTHER_CORE)
    g_other = send(g_own, OTHER_CORE)

    below = send(edges[2], UP), send(edges[3], UP_CROSS)
    above = send(edges[0], DOWN), send(edges[1], DOWN_CROSS)
    far_half = jax.ShapeDtypeStruct((2 * G_ROWS, 256), bf16)
    g_keep, g_swap = on_chip(
        far_kernel, (far_half, far_half), 2 * 256 * 512 * width, 0, (index, g_own, g_other, far_table)
    )
    g_got = send(g_swap, OTHER_CORE)

    to_pass = out_own = on_chip(collect_kernel, jax.ShapeDtypeStruct((128, width), bf16), 0, 0, (index, *seconds))
    out_prev = send(to_pass, Y_UP, "doc")
    out_next = send(to_pass, Y_DOWN, "doc")
    out_far_a = send(out_prev[:64], Y_UP, "doc")
    out_far_b = send(out_next[64:], Y_DOWN, "doc")

    context = on_chip(
        attention_kernel,
        jax.ShapeDtypeStruct((2, 2 * TOK, WIDE), bf16),
        4 * 4 * TOK * 640 * WIDE * 4,
        4 * 4 * TOK * 640,
        (index, keep, got, g_keep, g_got, *below, *above),
    )

    there = send(context[1], OTHER_X)
    kept_part, sent_part = on_chip(
        output_kernel,
        (jax.ShapeDtypeStruct((TOK, width), jnp.float32), jax.ShapeDtypeStruct((TOK, width), bf16)),
        2 * 256 * 512 * width,
        0,
        (index, context[0], there, out_own, out_prev, out_next, out_far_a, out_far_b),
        (pltpu.VMEM((4, 2 * TOK, 128), bf16),),
    )
    return (kept_part + send(sent_part, OTHER_CORE).astype(jnp.float32)).astype(bf16)


def solution(mesh):
    placed = (
        P(("doc", "seq"), None),
        P("doc"),
        P(),
        P(),
        P(None, "seq"),
        P(None, "seq"),
        P(None, "seq"),
        P(None, "seq"),
    )
    return jax.shard_map(
        per_device, mesh=mesh, in_specs=placed, out_specs=P(("doc", "seq"), None), check_vma=False
    )
```

```python
import jax
import jax.numpy as jnp
from jax import lax
from jax.experimental import pallas as pl
from jax.experimental.pallas import tpu as pltpu
from jax.sharding import PartitionSpec as P

HEAD_DIM = 64
BLOCK = 16
RADIUS = 127
NEGATIVE = -1e30
EPSILON = 1e-06

X, Z, C = 2, 8, 2
SEQ_SHARDS = X * Z * C
TOK = 128
HALF = 32
HEADS_LOCAL = 4
WIDE = HEADS_LOCAL * HEAD_DIM


def place(x, z, core):
    return (x * Z + z) * C + core


def pairs(move):
    return [
        (place(x, z, c), place(*move(x, z, c))) for x in range(X) for z in range(Z) for c in range(C)
    ]


OTHER_CORE = pairs(lambda x, z, c: (x, z, 1 - c))
OTHER_X = pairs(lambda x, z, c: (1 - x, z, c))
AHEAD = pairs(lambda x, z, c: (x, (z + (1 if c == 0 else -1)) % Z, c))
BEHIND = pairs(lambda x, z, c: (x, (z - (1 if c == 0 else -1)) % Z, c))
UP = pairs(lambda x, z, c: (x, (z + 1) % Z, c))
DOWN = pairs(lambda x, z, c: (x, (z - 1) % Z, c))


Y = 4
Y_UP = [(d, (d & 4) | ((d + 1) & 3)) for d in range(2 * Y)]
Y_DOWN = [(d, (d & 4) | ((d - 1) & 3)) for d in range(2 * Y)]


def send(value, route, axis="seq"):
    return lax.ppermute(value, axis, route)


def rms_norm(values, gain_row):
    mean_square = jnp.mean(values * values, axis=-1, keepdims=True)
    return values * lax.rsqrt(mean_square + EPSILON) * gain_row


def norm_kernel(index, hidden_in, gain_in, global_in, normed_ref, blocks_ref, hidden, gain, global_gain, sems):
    copies = [
        pltpu.make_async_copy(source, into, sems.at[i])
        for i, (source, into) in enumerate(((hidden_in, hidden), (gain_in, gain), (global_in, global_gain)))
    ]
    for copy in copies:
        copy.start()
    for copy in copies:
        copy.wait()
    normed = rms_norm(hidden[...].astype(jnp.float32), gain[...]).astype(jnp.bfloat16)
    normed_ref[...] = normed
    at = index[4] + lax.broadcasted_iota(jnp.int32, (TOK, 1), 0)
    valid = (at < index[3]).astype(jnp.float32)
    kept = (normed.astype(jnp.float32) * valid).reshape(TOK // BLOCK, BLOCK, normed.shape[1])
    blocks_ref[...] = rms_norm(jnp.sum(kept, axis=1), global_gain[...]).astype(jnp.bfloat16)


def dot_nt(left, right):
    return lax.dot_general(
        left, right, (((1,), (1,)), ((), ())), preferred_element_type=jnp.float32
    )


STEPS = ((0, 0), (0, 1), (1, 1), (0, 2), (1, 2), (0, 3), (1, 3), (0, 4))
SHARDS = len(STEPS)
ROWS = 4 * TOK
G_ROWS = Z * 16
VMEM_LIMIT = 32 * 1024 * 1024


def z_of(z, core, way, hops):
    delta = -hops if way == 0 else hops
    return (z + delta * (1 - 2 * core)) & (Z - 1)


def project_kernel(index, *refs):
    blocks, firsts, seconds = refs[:4], refs[4 : 4 + SHARDS], refs[4 + SHARDS : 4 + 2 * SHARDS]
    keep_ref, send_ref, g_rows, far_table, out_rows, *edges, rows, table, sems = refs[4 + 2 * SHARDS :]
    z, core, x = index[0], index[1], index[2]
    low_core = core == 0
    copies = []
    for i, (ref, bx, bc) in enumerate(zip(blocks, (x, 1 - x, x, 1 - x), (core, core, 1 - core, 1 - core))):
        into = rows.at[pl.ds(pl.multiple_of((bx * 2 + bc) * TOK, TOK), TOK), :]
        copies.append(pltpu.make_async_copy(ref, into, sems.at[i]))
        copies[-1].start()
    for j, (way, hops) in enumerate(STEPS):
        at = z_of(z, core, way, hops) * HALF
        for kind in range(3):
            into = table if kind == 0 else far_table
            base = 0 if kind == 0 else kind * 256 - 256
            here = pl.multiple_of(base + at, 16)
            into[pl.ds(here, 16), :] = firsts[j][kind * 16 : kind * 16 + 16, :]
            there = pl.multiple_of(base + at + 16, 16)
            into[pl.ds(there, 16), :] = seconds[j][kind * 16 : kind * 16 + 16, :]
        g_rows[j * 16 : j * 16 + 16, :] = seconds[j][48:64, :]
        out_rows[j * 16 : j * 16 + 16, :] = seconds[j][64:80, :]
    for copy in copies:
        copy.wait()
    for kind in range(3):
        columns = table[...] if kind == 0 else far_table[kind * 256 - 256 : kind * 256, :]
        out = dot_nt(rows[...], columns).astype(jnp.bfloat16)
        lanes = slice(kind * 128, kind * 128 + 128)
        keep_ref[:, lanes] = jnp.where(low_core, out[:, :128], out[:, 128:])
        send_ref[:, lanes] = jnp.where(low_core, out[:, 128:], out[:, :128])
        if kind:
            lanes_out = slice(kind * 128 - 128, kind * 128)
            for part in range(2):
                for seg in range(2):
                    at = slice((seg * 2 + part) * TOK, (seg * 2 + part + 1) * TOK)
                    into = slice(seg * TOK, seg * TOK + TOK)
                    edges[part][into, lanes_out] = keep_ref[at, lanes]
                    into = slice(2 * TOK + seg * TOK, 2 * TOK + seg * TOK + TOK)
                    edges[part][into, lanes_out] = send_ref[at, lanes]


def far_kernel(index, own_ref, other_ref, table, keep_ref, send_ref):
    low_core = index[1] == 0
    for source in range(2):
        rows = jnp.where(index[1] == source, own_ref[...], other_ref[...])
        at = slice(source * G_ROWS, source * G_ROWS + G_ROWS)
        for kind in range(2):
            out = dot_nt(rows, table[kind * 256 : kind * 256 + 256, :]).astype(jnp.bfloat16)
            lanes = slice(kind * 128, kind * 128 + 128)
            keep_ref[at, lanes] = jnp.where(low_core, out[:, :128], out[:, 128:])
            send_ref[at, lanes] = jnp.where(low_core, out[:, 128:], out[:, :128])


def attention_kernel(index, keep_ref, got_ref, g_keep, g_got, below_ref, below_got, above_ref, above_got, out_ref):
    z, x, limit = index[0], index[2], index[3]
    lane_head = (lax.broadcasted_iota(jnp.int32, (TOK, WIDE), 1) % 128) // HALF
    row = lax.broadcasted_iota(jnp.int32, (HEADS_LOCAL * TOK, TOK), 0) % TOK
    col = lax.broadcasted_iota(jnp.int32, (HEADS_LOCAL * TOK, TOK), 1)
    far = lax.broadcasted_iota(jnp.int32, (1, 2 * G_ROWS), 1)
    far_core, j, far_x, far_k = far >> 7, (far >> 4) & 7, (far >> 3) & 1, far & 7
    delta = jnp.where((j & 1) == 1, -((j + 1) >> 1), j >> 1)
    far_z = (z + delta * (1 - 2 * far_core)) & (Z - 1)
    far_ok = ((far_x * Z + far_z) * C + far_core) * TOK + far_k * BLOCK < limit
    far_keys = jnp.concatenate([g_keep[:, :128], g_got[:, :128]], axis=1)
    far_values = jnp.concatenate([g_keep[:, 128:], g_got[:, 128:]], axis=1)

    def local(kind, at):
        lanes = slice(kind * 128, kind * 128 + 128)
        return jnp.concatenate([keep_ref[at : at + TOK, lanes], got_ref[at : at + TOK, lanes]], axis=1)

    def halo(ref, got, kind, seg):
        at = pl.ds(pl.multiple_of(seg * TOK, TOK), TOK)
        lanes = slice(kind * 128 - 128, kind * 128)
        return jnp.concatenate([ref[at, lanes], got[at, lanes]], axis=1)

    for seg in range(2):
        below_seg = jnp.where(z == 0, 1 - seg, seg)
        above_seg = jnp.where(z == Z - 1, 1 - seg, seg)
        for part in range(2):
            base = (seg * Z + z) * 2 * TOK + part * TOK
            at = (seg * 2 + part) * TOK
            queries = local(0, at)
            stacked = jnp.concatenate(
                [jnp.where(lane_head == h, queries, jnp.zeros_like(queries)) for h in range(HEADS_LOCAL)],
                axis=0,
            )

            def neighbours(kind):
                if part == 0:
                    return halo(below_ref, below_got, kind, below_seg), local(kind, at), local(kind, at + TOK)
                return local(kind, at - TOK), local(kind, at), halo(above_ref, above_got, kind, above_seg)

            k_left, k_mid, k_right = neighbours(1)
            v_left, v_mid, v_right = neighbours(2)
            low = base - TOK
            ok_left = (col > row) & (col + low >= 0) & (col + low < limit)
            ok_mid = col + base < limit
            ok_right = (col < row) & (col + (base + TOK) < limit)
            s_left = jnp.where(ok_left, dot_nt(stacked, k_left), NEGATIVE)
            s_mid = jnp.where(ok_mid, dot_nt(stacked, k_mid), NEGATIVE)
            s_right = jnp.where(ok_right, dot_nt(stacked, k_right), NEGATIVE)
            s_far = jnp.where(far_ok, dot_nt(stacked, far_keys), NEGATIVE)
            near_top = jnp.maximum(jnp.maximum(s_left, s_mid), s_right)
            far_top = jnp.maximum(s_far[:, :128], s_far[:, 128:])
            top = jnp.max(jnp.maximum(near_top, far_top), axis=-1, keepdims=True)
            w_left = jnp.exp(s_left - top)
            w_mid = jnp.exp(s_mid - top)
            w_right = jnp.exp(s_right - top)
            w_far = jnp.exp(s_far - top)
            total = jnp.sum(
                w_left + w_mid + w_right + w_far[:, :128] + w_far[:, 128:], axis=-1, keepdims=True
            )

            def mix(weights, values):
                return jnp.dot(
                    weights.astype(jnp.bfloat16), values, preferred_element_type=jnp.float32
                )

            mixed = mix(w_left, v_left) + mix(w_mid, v_mid) + mix(w_right, v_right) + mix(w_far, far_values)
            mixed = mixed / total
            context = jnp.zeros((TOK, WIDE), jnp.float32)
            for h in range(HEADS_LOCAL):
                context = jnp.where(lane_head == h, mixed[h * TOK : (h + 1) * TOK, :], context)
            mine = jnp.where(x == seg, 0, 1)
            out_ref[mine, part * TOK : (part + 1) * TOK, :] = context.astype(jnp.bfloat16)


def output_kernel(index, own_ref, there_ref, mine, prev, nxt, far_a, far_b, keep_ref, send_ref, table):
    z, core, x, y = index[0], index[1], index[2], index[5]
    own, there = own_ref[...], there_ref[...]
    for side in range(X):
        mixed = jnp.where(x == side, own, there)
        table[2 * side] = mixed[:, :128]
        table[2 * side + 1] = mixed[:, 128:]
    full = jnp.concatenate([table[(y + turn) & 3] for turn in (0, 3, 1, 2)], axis=1)
    for j, (way, hops) in enumerate(STEPS):
        zj = z_of(z, core, way, hops)
        here = j * 16
        far = (far_a, here) if j < 4 else (far_b, here - 64)
        weights = [
            ref[at : at + 16, i * 256 : i * 256 + 256]
            for ref, at in ((mine, here), (prev, here), (nxt, here), far)
            for i in range(8)
        ]
        out = jnp.dot(full, jnp.concatenate(weights, axis=0), preferred_element_type=jnp.float32)
        keep = jnp.where(core == 0, out[:TOK], out[TOK:])
        sent = jnp.where(core == 0, out[TOK:], out[:TOK]).astype(jnp.bfloat16)
        for side in range(X):
            lanes = pl.ds(pl.multiple_of((side * Z + zj) * 128, 128), 128)
            keep_ref[:, lanes] = keep[:, side * 128 : side * 128 + 128]
            send_ref[:, lanes] = sent[:, side * 128 : side * 128 + 128]


def on_chip(kernel, out_shape, flops, exps, args, scratch=(), in_hbm=0):
    vmem = pl.BlockSpec(memory_space=pltpu.VMEM)
    specs = [pl.BlockSpec(memory_space=pltpu.SMEM)] + [pl.BlockSpec(memory_space=pltpu.HBM)] * in_hbm
    specs += [vmem] * (len(args) - len(specs))
    return pl.pallas_call(
        kernel,
        out_shape=out_shape,
        in_specs=specs,
        out_specs=jax.tree.map(lambda _: vmem, out_shape),
        scratch_shapes=list(scratch),
        compiler_params=pltpu.CompilerParams(vmem_limit_bytes=VMEM_LIMIT),
        cost_estimate=pl.CostEstimate(flops=flops, bytes_accessed=4 << 20, transcendentals=exps),
    )(*args)


def after(value, *others):
    return lax.optimization_barrier((value, *others))[0]


def per_device(hidden_in, length, attn_gain, global_gain, w_query, w_key, w_value, w_out):
    width = hidden_in.shape[1]
    me = lax.axis_index("seq")
    core = me & 1
    z = (me >> 1) & (Z - 1)
    x = me >> 4
    limit = length[0]
    bf16 = jnp.bfloat16
    y = lax.axis_index("doc") & (Y - 1)
    index = jnp.stack([z, core, x, limit, me * TOK, y]).astype(jnp.int32)

    mine = jnp.stack([w_query.T, w_key.T, w_value.T]).reshape(3, 2, 16, width)
    first = mine[:, 0].reshape(48, width)

    normed, global_mine = on_chip(
        norm_kernel,
        (jax.ShapeDtypeStruct((TOK, width), bf16), jax.ShapeDtypeStruct((TOK // BLOCK, width), bf16)),
        8 * TOK * width,
        0,
        (index, after(hidden_in, first), attn_gain[None], global_gain[None]),
        (
            pltpu.VMEM((TOK, width), bf16),
            pltpu.VMEM((1, width), jnp.float32),
            pltpu.VMEM((1, width), jnp.float32),
            pltpu.SemaphoreType.DMA((3,)),
        ),
        in_hbm=3,
    )
    global_there = send(global_mine, OTHER_X)

    split = after(w_out, first).reshape(X, 2, HEADS_LOCAL, 2, HALF, 64)

    def slab(group):
        at = (y >> 1, group, 0, (y & 1) ^ group, 0, 0)
        return lax.dynamic_slice(split, at, (1, 1, HEADS_LOCAL, 1, HALF, 64)).reshape(128, 64)

    kept = slab(core)
    passed = send(slab(1 - core), OTHER_CORE)
    chip = jnp.concatenate([jnp.where(core == 0, kept, passed), jnp.where(core == 0, passed, kept)], axis=1)
    chip_there = send(chip, OTHER_X)
    both = jnp.concatenate([jnp.where(x == 0, chip, chip_there), jnp.where(x == 0, chip_there, chip)], axis=1)

    second = jnp.concatenate(
        [
            mine[:, 1].reshape(48, width),
            jnp.where(x == 0, global_mine, global_there),
            jnp.where(x == 0, global_there, global_mine),
            jnp.concatenate([both[i * 16 : i * 16 + 16] for i in range(8)], axis=1),
        ],
        axis=0,
    )

    one, two = {(0, 0): first}, {(0, 0): second}
    a_one, a_two, b_one, b_two = first, second, first, second
    for step in range(1, 5):
        if step == 2:
            a_two = b_two = after(second, a_one, b_one)
        if step > 1:
            if step > 2:
                before = one[0, step - 2], one[1, step - 2]
                a_two, b_two = lax.optimization_barrier((a_two, b_two, *before))[:2]
            two[0, step - 1] = a_two = send(a_two, AHEAD)
            two[1, step - 1] = b_two = send(b_two, BEHIND)
        if step > 2:
            before = two[0, step - 2], two[1, step - 2]
            a_one, b_one = lax.optimization_barrier((a_one, b_one, *before))[:2]
        one[0, step] = a_one = send(a_one, AHEAD)
        if step < 4:
            one[1, step] = b_one = send(b_one, BEHIND)
    a_two = after(a_two, one[0, 3], one[1, 3])
    two[0, 4] = send(a_two, AHEAD)
    firsts = [one[s] for s in STEPS]
    seconds = [two[s] for s in STEPS]

    to_send = after(normed, one[0, 1])
    across = send(to_send, OTHER_X)
    beside = send(to_send, OTHER_CORE)
    beside_across = send(across, OTHER_CORE)

    half = jax.ShapeDtypeStruct((ROWS, 3 * 128), bf16)
    keep, to_swap, g_own, far_table, out_own, *edges = on_chip(
        project_kernel,
        (
            half,
            half,
            jax.ShapeDtypeStruct((G_ROWS, width), bf16),
            jax.ShapeDtypeStruct((2 * Z * HALF, width), bf16),
            jax.ShapeDtypeStruct((128, width), bf16),
            *[jax.ShapeDtypeStruct((4 * TOK, 256), bf16)] * 2,
        ),
        2 * ROWS * 768 * width,
        0,
        (index, normed, across, beside, beside_across, *firsts, *seconds),
        (pltpu.VMEM((ROWS, width), bf16), pltpu.VMEM((Z * HALF, width), bf16), pltpu.SemaphoreType.DMA((4,))),
        in_hbm=4,
    )
    got = send(to_swap, OTHER_CORE)
    g_other = send(g_own, OTHER_CORE)

    below, above = send(edges[1], UP), send(edges[0], DOWN)
    below = below, send(below[2 * TOK :], OTHER_CORE)
    above = above, send(above[2 * TOK :], OTHER_CORE)
    far_half = jax.ShapeDtypeStruct((2 * G_ROWS, 256), bf16)
    g_keep, g_swap = on_chip(
        far_kernel, (far_half, far_half), 2 * 256 * 512 * width, 0, (index, g_own, g_other, far_table)
    )
    g_got = send(g_swap, OTHER_CORE)

    to_pass = out_own
    out_prev = send(to_pass, Y_UP, "doc")
    out_next = send(to_pass, Y_DOWN, "doc")
    out_far_a = send(out_prev[:64], Y_UP, "doc")
    out_far_b = send(out_next[64:], Y_DOWN, "doc")

    context = on_chip(
        attention_kernel,
        jax.ShapeDtypeStruct((2, 2 * TOK, WIDE), bf16),
        4 * 4 * TOK * 640 * WIDE * 4,
        4 * 4 * TOK * 640,
        (index, keep, got, g_keep, g_got, *below, *above),
    )

    there = send(context[1], OTHER_X)
    kept_part, sent_part = on_chip(
        output_kernel,
        (jax.ShapeDtypeStruct((TOK, width), jnp.float32), jax.ShapeDtypeStruct((TOK, width), bf16)),
        2 * 256 * 512 * width,
        0,
        (index, context[0], there, out_own, out_prev, out_next, out_far_a, out_far_b),
        (pltpu.VMEM((4, 2 * TOK, 128), bf16),),
    )
    return (kept_part + send(sent_part, OTHER_CORE).astype(jnp.float32)).astype(bf16)


def solution(mesh):
    placed = (
        P(("doc", "seq"), None),
        P("doc"),
        P(),
        P(),
        P(None, "seq"),
        P(None, "seq"),
        P(None, "seq"),
        P(None, "seq"),
    )
    return jax.shard_map(
        per_device, mesh=mesh, in_specs=placed, out_specs=P(("doc", "seq"), None), check_vma=False
    )
```

```python
import jax
import jax.numpy as jnp
from jax import lax
from jax.experimental import pallas as pl
from jax.experimental.pallas import tpu as pltpu
from jax.sharding import PartitionSpec as P

HEAD_DIM = 64
BLOCK = 16
RADIUS = 127
NEGATIVE = -1e30
EPSILON = 1e-06

X, Z, C = 2, 8, 2
SEQ_SHARDS = X * Z * C
TOK = 128
HALF = 32
HEADS_LOCAL = 4
WIDE = HEADS_LOCAL * HEAD_DIM


def place(x, z, core):
    return (x * Z + z) * C + core


def pairs(move):
    return [
        (place(x, z, c), place(*move(x, z, c))) for x in range(X) for z in range(Z) for c in range(C)
    ]


OTHER_CORE = pairs(lambda x, z, c: (x, z, 1 - c))
OTHER_X = pairs(lambda x, z, c: (1 - x, z, c))
AHEAD = pairs(lambda x, z, c: (x, (z + (1 if c == 0 else -1)) % Z, c))
BEHIND = pairs(lambda x, z, c: (x, (z - (1 if c == 0 else -1)) % Z, c))
UP = pairs(lambda x, z, c: (x, (z + 1) % Z, c))
DOWN = pairs(lambda x, z, c: (x, (z - 1) % Z, c))


Y = 4
Y_UP = [(d, (d & 4) | ((d + 1) & 3)) for d in range(2 * Y)]
Y_DOWN = [(d, (d & 4) | ((d - 1) & 3)) for d in range(2 * Y)]


def send(value, route, axis="seq"):
    return lax.ppermute(value, axis, route)


def rms_norm(values, gain_row):
    mean_square = jnp.mean(values * values, axis=-1, keepdims=True)
    return values * lax.rsqrt(mean_square + EPSILON) * gain_row


def norm_kernel(index, hidden_in, gain_in, global_in, normed_ref, blocks_ref, hidden, gain, global_gain, sems):
    copies = [
        pltpu.make_async_copy(source, into, sems.at[i])
        for i, (source, into) in enumerate(((hidden_in, hidden), (gain_in, gain), (global_in, global_gain)))
    ]
    for copy in copies:
        copy.start()
    for copy in copies:
        copy.wait()
    normed = rms_norm(hidden[...].astype(jnp.float32), gain[...]).astype(jnp.bfloat16)
    normed_ref[...] = normed
    at = index[4] + lax.broadcasted_iota(jnp.int32, (TOK, 1), 0)
    valid = (at < index[3]).astype(jnp.float32)
    kept = (normed.astype(jnp.float32) * valid).reshape(TOK // BLOCK, BLOCK, normed.shape[1])
    blocks_ref[...] = rms_norm(jnp.sum(kept, axis=1), global_gain[...]).astype(jnp.bfloat16)


def dot_nt(left, right):
    return lax.dot_general(
        left, right, (((1,), (1,)), ((), ())), preferred_element_type=jnp.float32
    )


STEPS = ((0, 0), (0, 1), (1, 1), (0, 2), (1, 2), (0, 3), (1, 3), (0, 4))
SHARDS = len(STEPS)
ROWS = 4 * TOK
G_ROWS = Z * 16
VMEM_LIMIT = 32 * 1024 * 1024


def z_of(z, core, way, hops):
    delta = -hops if way == 0 else hops
    return (z + delta * (1 - 2 * core)) & (Z - 1)


def project_kernel(index, *refs):
    blocks, firsts, seconds = refs[:4], refs[4 : 4 + SHARDS], refs[4 + SHARDS : 4 + 2 * SHARDS]
    keep_ref, send_ref, g_rows, far_table, out_rows, *edges, rows, table, sems = refs[4 + 2 * SHARDS :]
    z, core, x = index[0], index[1], index[2]
    low_core = core == 0
    copies = []
    for i, (ref, bx, bc) in enumerate(zip(blocks, (x, 1 - x, x, 1 - x), (core, core, 1 - core, 1 - core))):
        into = rows.at[pl.ds(pl.multiple_of((bx * 2 + bc) * TOK, TOK), TOK), :]
        copies.append(pltpu.make_async_copy(ref, into, sems.at[i]))
        copies[-1].start()
    for j, (way, hops) in enumerate(STEPS):
        at = z_of(z, core, way, hops) * HALF
        for kind in range(3):
            into = table if kind == 0 else far_table
            base = 0 if kind == 0 else kind * 256 - 256
            here = pl.multiple_of(base + at, 16)
            into[pl.ds(here, 16), :] = firsts[j][kind * 16 : kind * 16 + 16, :]
            there = pl.multiple_of(base + at + 16, 16)
            into[pl.ds(there, 16), :] = seconds[j][kind * 16 : kind * 16 + 16, :]
        g_rows[j * 16 : j * 16 + 16, :] = seconds[j][48:64, :]
        out_rows[j * 16 : j * 16 + 16, :] = seconds[j][64:80, :]
    for copy in copies:
        copy.wait()
    for kind in range(3):
        columns = table[...] if kind == 0 else far_table[kind * 256 - 256 : kind * 256, :]
        out = dot_nt(rows[...], columns).astype(jnp.bfloat16)
        lanes = slice(kind * 128, kind * 128 + 128)
        keep_ref[:, lanes] = jnp.where(low_core, out[:, :128], out[:, 128:])
        send_ref[:, lanes] = jnp.where(low_core, out[:, 128:], out[:, :128])
        if kind:
            lanes_out = slice(kind * 128 - 128, kind * 128)
            for part in range(2):
                for seg in range(2):
                    at = slice((seg * 2 + part) * TOK, (seg * 2 + part + 1) * TOK)
                    into = slice(seg * TOK, seg * TOK + TOK)
                    edges[part][into, lanes_out] = keep_ref[at, lanes]
                    into = slice(2 * TOK + seg * TOK, 2 * TOK + seg * TOK + TOK)
                    edges[part][into, lanes_out] = send_ref[at, lanes]


def far_kernel(index, own_ref, other_ref, table, keep_ref, send_ref):
    low_core = index[1] == 0
    for source in range(2):
        rows = jnp.where(index[1] == source, own_ref[...], other_ref[...])
        at = slice(source * G_ROWS, source * G_ROWS + G_ROWS)
        for kind in range(2):
            out = dot_nt(rows, table[kind * 256 : kind * 256 + 256, :]).astype(jnp.bfloat16)
            lanes = slice(kind * 128, kind * 128 + 128)
            keep_ref[at, lanes] = jnp.where(low_core, out[:, :128], out[:, 128:])
            send_ref[at, lanes] = jnp.where(low_core, out[:, 128:], out[:, :128])


def attention_kernel(index, keep_ref, got_ref, g_keep, g_got, below_ref, below_got, above_ref, above_got, out_ref):
    z, x, limit = index[0], index[2], index[3]
    lane_head = (lax.broadcasted_iota(jnp.int32, (TOK, WIDE), 1) % 128) // HALF
    row = lax.broadcasted_iota(jnp.int32, (HEADS_LOCAL * TOK, TOK), 0) % TOK
    col = lax.broadcasted_iota(jnp.int32, (HEADS_LOCAL * TOK, TOK), 1)
    far = lax.broadcasted_iota(jnp.int32, (1, 2 * G_ROWS), 1)
    far_core, j, far_x, far_k = far >> 7, (far >> 4) & 7, (far >> 3) & 1, far & 7
    delta = jnp.where((j & 1) == 1, -((j + 1) >> 1), j >> 1)
    far_z = (z + delta * (1 - 2 * far_core)) & (Z - 1)
    far_ok = ((far_x * Z + far_z) * C + far_core) * TOK + far_k * BLOCK < limit
    far_keys = jnp.concatenate([g_keep[:, :128], g_got[:, :128]], axis=1)
    far_values = jnp.concatenate([g_keep[:, 128:], g_got[:, 128:]], axis=1)

    def local(kind, at):
        lanes = slice(kind * 128, kind * 128 + 128)
        return jnp.concatenate([keep_ref[at : at + TOK, lanes], got_ref[at : at + TOK, lanes]], axis=1)

    def halo(ref, got, kind, seg):
        at = pl.ds(pl.multiple_of(seg * TOK, TOK), TOK)
        lanes = slice(kind * 128 - 128, kind * 128)
        return jnp.concatenate([ref[at, lanes], got[at, lanes]], axis=1)

    for seg in range(2):
        below_seg = jnp.where(z == 0, 1 - seg, seg)
        above_seg = jnp.where(z == Z - 1, 1 - seg, seg)
        for part in range(2):
            base = (seg * Z + z) * 2 * TOK + part * TOK
            at = (seg * 2 + part) * TOK
            queries = local(0, at)
            stacked = jnp.concatenate(
                [jnp.where(lane_head == h, queries, jnp.zeros_like(queries)) for h in range(HEADS_LOCAL)],
                axis=0,
            )

            def neighbours(kind):
                if part == 0:
                    return halo(below_ref, below_got, kind, below_seg), local(kind, at), local(kind, at + TOK)
                return local(kind, at - TOK), local(kind, at), halo(above_ref, above_got, kind, above_seg)

            k_left, k_mid, k_right = neighbours(1)
            v_left, v_mid, v_right = neighbours(2)
            low = base - TOK
            ok_left = (col > row) & (col + low >= 0) & (col + low < limit)
            ok_mid = col + base < limit
            ok_right = (col < row) & (col + (base + TOK) < limit)
            s_left = jnp.where(ok_left, dot_nt(stacked, k_left), NEGATIVE)
            s_mid = jnp.where(ok_mid, dot_nt(stacked, k_mid), NEGATIVE)
            s_right = jnp.where(ok_right, dot_nt(stacked, k_right), NEGATIVE)
            s_far = jnp.where(far_ok, dot_nt(stacked, far_keys), NEGATIVE)
            near_top = jnp.maximum(jnp.maximum(s_left, s_mid), s_right)
            far_top = jnp.maximum(s_far[:, :128], s_far[:, 128:])
            top = jnp.max(jnp.maximum(near_top, far_top), axis=-1, keepdims=True)
            w_left = jnp.exp(s_left - top)
            w_mid = jnp.exp(s_mid - top)
            w_right = jnp.exp(s_right - top)
            w_far = jnp.exp(s_far - top)
            total = jnp.sum(
                w_left + w_mid + w_right + w_far[:, :128] + w_far[:, 128:], axis=-1, keepdims=True
            )

            def mix(weights, values):
                return jnp.dot(
                    weights.astype(jnp.bfloat16), values, preferred_element_type=jnp.float32
                )

            mixed = mix(w_left, v_left) + mix(w_mid, v_mid) + mix(w_right, v_right) + mix(w_far, far_values)
            mixed = mixed / total
            context = jnp.zeros((TOK, WIDE), jnp.float32)
            for h in range(HEADS_LOCAL):
                context = jnp.where(lane_head == h, mixed[h * TOK : (h + 1) * TOK, :], context)
            mine = jnp.where(x == seg, 0, 1)
            out_ref[mine, part * TOK : (part + 1) * TOK, :] = context.astype(jnp.bfloat16)


def output_kernel(index, own_ref, there_ref, mine, prev, nxt, far_a, far_b, keep_ref, send_ref, table):
    z, core, x, y = index[0], index[1], index[2], index[5]
    own, there = own_ref[...], there_ref[...]
    for side in range(X):
        mixed = jnp.where(x == side, own, there)
        table[2 * side] = mixed[:, :128]
        table[2 * side + 1] = mixed[:, 128:]
    full = jnp.concatenate([table[(y + turn) & 3] for turn in (0, 3, 1, 2)], axis=1)
    for j, (way, hops) in enumerate(STEPS):
        zj = z_of(z, core, way, hops)
        here = j * 16
        far = (far_a, here) if j < 4 else (far_b, here - 64)
        weights = [
            ref[at : at + 16, i * 256 : i * 256 + 256]
            for ref, at in ((mine, here), (prev, here), (nxt, here), far)
            for i in range(8)
        ]
        out = jnp.dot(full, jnp.concatenate(weights, axis=0), preferred_element_type=jnp.float32)
        keep = jnp.where(core == 0, out[:TOK], out[TOK:])
        sent = jnp.where(core == 0, out[TOK:], out[:TOK]).astype(jnp.bfloat16)
        for side in range(X):
            lanes = pl.ds(pl.multiple_of((side * Z + zj) * 128, 128), 128)
            keep_ref[:, lanes] = keep[:, side * 128 : side * 128 + 128]
            send_ref[:, lanes] = sent[:, side * 128 : side * 128 + 128]


def on_chip(kernel, out_shape, flops, exps, args, scratch=(), in_hbm=0):
    vmem = pl.BlockSpec(memory_space=pltpu.VMEM)
    specs = [pl.BlockSpec(memory_space=pltpu.SMEM)] + [pl.BlockSpec(memory_space=pltpu.HBM)] * in_hbm
    specs += [vmem] * (len(args) - len(specs))
    return pl.pallas_call(
        kernel,
        out_shape=out_shape,
        in_specs=specs,
        out_specs=jax.tree.map(lambda _: vmem, out_shape),
        scratch_shapes=list(scratch),
        compiler_params=pltpu.CompilerParams(vmem_limit_bytes=VMEM_LIMIT),
        cost_estimate=pl.CostEstimate(flops=flops, bytes_accessed=4 << 20, transcendentals=exps),
    )(*args)


def after(value, *others):
    return lax.optimization_barrier((value, *others))[0]


def per_device(hidden_in, length, attn_gain, global_gain, w_query, w_key, w_value, w_out):
    width = hidden_in.shape[1]
    me = lax.axis_index("seq")
    core = me & 1
    z = (me >> 1) & (Z - 1)
    x = me >> 4
    limit = length[0]
    bf16 = jnp.bfloat16
    y = lax.axis_index("doc") & (Y - 1)
    index = jnp.stack([z, core, x, limit, me * TOK, y]).astype(jnp.int32)

    mine = jnp.stack([w_query.T, w_key.T, w_value.T]).reshape(3, 2, 16, width)
    first = mine[:, 0].reshape(48, width)

    normed, global_mine = on_chip(
        norm_kernel,
        (jax.ShapeDtypeStruct((TOK, width), bf16), jax.ShapeDtypeStruct((TOK // BLOCK, width), bf16)),
        8 * TOK * width,
        0,
        (index, after(hidden_in, first), attn_gain[None], global_gain[None]),
        (
            pltpu.VMEM((TOK, width), bf16),
            pltpu.VMEM((1, width), jnp.float32),
            pltpu.VMEM((1, width), jnp.float32),
            pltpu.SemaphoreType.DMA((3,)),
        ),
        in_hbm=3,
    )
    global_there = send(global_mine, OTHER_X)

    split = after(w_out, first).reshape(X, 2, HEADS_LOCAL, 2, HALF, 64)

    def slab(group):
        at = (y >> 1, group, 0, (y & 1) ^ group, 0, 0)
        return lax.dynamic_slice(split, at, (1, 1, HEADS_LOCAL, 1, HALF, 64)).reshape(128, 64)

    kept = slab(core)
    passed = send(slab(1 - core), OTHER_CORE)
    chip = jnp.concatenate([jnp.where(core == 0, kept, passed), jnp.where(core == 0, passed, kept)], axis=1)
    chip_there = send(chip, OTHER_X)
    both = jnp.concatenate([jnp.where(x == 0, chip, chip_there), jnp.where(x == 0, chip_there, chip)], axis=1)

    second = jnp.concatenate(
        [
            mine[:, 1].reshape(48, width),
            jnp.where(x == 0, global_mine, global_there),
            jnp.where(x == 0, global_there, global_mine),
            jnp.concatenate([both[i * 16 : i * 16 + 16] for i in range(8)], axis=1),
        ],
        axis=0,
    )

    one, two = {(0, 0): first}, {(0, 0): second}
    a_one, a_two, b_one, b_two = first, second, first, second
    for step in range(1, 5):
        if step == 2:
            to_send = after(normed, one[0, 1])
            across = send(to_send, OTHER_X)
            beside = send(to_send, OTHER_CORE)
            beside_across = send(across, OTHER_CORE)
            a_two = b_two = after(second, a_one, b_one)
        if step > 1:
            if step > 2:
                before = one[0, step - 2], one[1, step - 2]
                a_two, b_two = lax.optimization_barrier((a_two, b_two, *before))[:2]
            two[0, step - 1] = a_two = send(a_two, AHEAD)
            if step == 4:
                b_two = after(b_two, across, beside, beside_across)
            two[1, step - 1] = b_two = send(b_two, BEHIND)
        if step > 2:
            before = two[0, step - 2], two[1, step - 2]
            a_one, b_one = lax.optimization_barrier((a_one, b_one, *before))[:2]
        one[0, step] = a_one = send(a_one, AHEAD)
        if step < 4:
            one[1, step] = b_one = send(b_one, BEHIND)
    a_two = after(a_two, one[0, 3], one[1, 3])
    two[0, 4] = send(a_two, AHEAD)
    firsts = [one[s] for s in STEPS]
    seconds = [two[s] for s in STEPS]

    half = jax.ShapeDtypeStruct((ROWS, 3 * 128), bf16)
    keep, to_swap, g_own, far_table, out_own, *edges = on_chip(
        project_kernel,
        (
            half,
            half,
            jax.ShapeDtypeStruct((G_ROWS, width), bf16),
            jax.ShapeDtypeStruct((2 * Z * HALF, width), bf16),
            jax.ShapeDtypeStruct((128, width), bf16),
            *[jax.ShapeDtypeStruct((4 * TOK, 256), bf16)] * 2,
        ),
        2 * ROWS * 768 * width,
        0,
        (index, normed, across, beside, beside_across, *firsts, *seconds),
        (pltpu.VMEM((ROWS, width), bf16), pltpu.VMEM((Z * HALF, width), bf16), pltpu.SemaphoreType.DMA((4,))),
        in_hbm=4,
    )
    got = send(to_swap, OTHER_CORE)
    g_other = send(g_own, OTHER_CORE)

    below, above = send(edges[1], UP), send(edges[0], DOWN)
    below = below, send(below[2 * TOK :], OTHER_CORE)
    above = above, send(above[2 * TOK :], OTHER_CORE)
    far_half = jax.ShapeDtypeStruct((2 * G_ROWS, 256), bf16)
    g_keep, g_swap = on_chip(
        far_kernel, (far_half, far_half), 2 * 256 * 512 * width, 0, (index, g_own, g_other, far_table)
    )
    g_got = send(g_swap, OTHER_CORE)

    to_pass = out_own
    out_prev = send(to_pass, Y_UP, "doc")
    out_next = send(to_pass, Y_DOWN, "doc")
    out_far_a = send(out_prev[:64], Y_UP, "doc")
    out_far_b = send(out_next[64:], Y_DOWN, "doc")

    context = on_chip(
        attention_kernel,
        jax.ShapeDtypeStruct((2, 2 * TOK, WIDE), bf16),
        4 * 4 * TOK * 640 * WIDE * 4,
        4 * 4 * TOK * 640,
        (index, keep, got, g_keep, g_got, *below, *above),
    )

    there = send(context[1], OTHER_X)
    kept_part, sent_part = on_chip(
        output_kernel,
        (jax.ShapeDtypeStruct((TOK, width), jnp.float32), jax.ShapeDtypeStruct((TOK, width), bf16)),
        2 * 256 * 512 * width,
        0,
        (index, context[0], there, out_own, out_prev, out_next, out_far_a, out_far_b),
        (pltpu.VMEM((4, 2 * TOK, 128), bf16),),
    )
    return (kept_part + send(sent_part, OTHER_CORE).astype(jnp.float32)).astype(bf16)


def solution(mesh):
    placed = (
        P(("doc", "seq"), None),
        P("doc"),
        P(),
        P(),
        P(None, "seq"),
        P(None, "seq"),
        P(None, "seq"),
        P(None, "seq"),
    )
    return jax.shard_map(
        per_device, mesh=mesh, in_specs=placed, out_specs=P(("doc", "seq"), None), check_vma=False
    )
```

```python
import jax
import jax.numpy as jnp
from jax import lax
from jax.experimental import pallas as pl
from jax.experimental.pallas import tpu as pltpu
from jax.sharding import PartitionSpec as P

HEAD_DIM = 64
BLOCK = 16
RADIUS = 127
NEGATIVE = -1e30
EPSILON = 1e-06

X, Z, C = 2, 8, 2
SEQ_SHARDS = X * Z * C
TOK = 128
HALF = 32
HEADS_LOCAL = 4
WIDE = HEADS_LOCAL * HEAD_DIM


def place(x, z, core):
    return (x * Z + z) * C + core


def pairs(move):
    return [
        (place(x, z, c), place(*move(x, z, c))) for x in range(X) for z in range(Z) for c in range(C)
    ]


OTHER_CORE = pairs(lambda x, z, c: (x, z, 1 - c))
OTHER_X = pairs(lambda x, z, c: (1 - x, z, c))
AHEAD = pairs(lambda x, z, c: (x, (z + (1 if c == 0 else -1)) % Z, c))
BEHIND = pairs(lambda x, z, c: (x, (z - (1 if c == 0 else -1)) % Z, c))
UP = pairs(lambda x, z, c: (x, (z + 1) % Z, c))
DOWN = pairs(lambda x, z, c: (x, (z - 1) % Z, c))


Y = 4
Y_UP = [(d, (d & 4) | ((d + 1) & 3)) for d in range(2 * Y)]
Y_DOWN = [(d, (d & 4) | ((d - 1) & 3)) for d in range(2 * Y)]


def send(value, route, axis="seq"):
    return lax.ppermute(value, axis, route)


def rms_norm(values, gain_row):
    mean_square = jnp.mean(values * values, axis=-1, keepdims=True)
    return values * lax.rsqrt(mean_square + EPSILON) * gain_row


def norm_kernel(index, hidden_in, gain_in, global_in, normed_ref, blocks_ref, hidden, gain, global_gain, sems):
    copies = [
        pltpu.make_async_copy(source, into, sems.at[i])
        for i, (source, into) in enumerate(((hidden_in, hidden), (gain_in, gain), (global_in, global_gain)))
    ]
    for copy in copies:
        copy.start()
    for copy in copies:
        copy.wait()
    normed = rms_norm(hidden[...].astype(jnp.float32), gain[...]).astype(jnp.bfloat16)
    normed_ref[...] = normed
    at = index[4] + lax.broadcasted_iota(jnp.int32, (TOK, 1), 0)
    valid = (at < index[3]).astype(jnp.float32)
    kept = (normed.astype(jnp.float32) * valid).reshape(TOK // BLOCK, BLOCK, normed.shape[1])
    blocks_ref[...] = rms_norm(jnp.sum(kept, axis=1), global_gain[...]).astype(jnp.bfloat16)


def dot_nt(left, right):
    return lax.dot_general(
        left, right, (((1,), (1,)), ((), ())), preferred_element_type=jnp.float32
    )


STEPS = ((0, 0), (0, 1), (1, 1), (0, 2), (1, 2), (0, 3), (1, 3), (0, 4))
SHARDS = len(STEPS)
ROWS = 4 * TOK
G_ROWS = Z * 16
VMEM_LIMIT = 32 * 1024 * 1024


def z_of(z, core, way, hops):
    delta = -hops if way == 0 else hops
    return (z + delta * (1 - 2 * core)) & (Z - 1)


def project_kernel(index, *refs):
    blocks, firsts, seconds = refs[:4], refs[4 : 4 + SHARDS], refs[4 + SHARDS : 4 + 2 * SHARDS]
    keep_ref, send_ref, g_rows, far_table, out_rows, *edges, rows, table, sems = refs[4 + 2 * SHARDS :]
    z, core, x = index[0], index[1], index[2]
    low_core = core == 0
    copies = []
    for i, (ref, bx, bc) in enumerate(zip(blocks, (x, 1 - x, x, 1 - x), (core, core, 1 - core, 1 - core))):
        into = rows.at[pl.ds(pl.multiple_of((bx * 2 + bc) * TOK, TOK), TOK), :]
        copies.append(pltpu.make_async_copy(ref, into, sems.at[i]))
        copies[-1].start()
    for j, (way, hops) in enumerate(STEPS):
        at = z_of(z, core, way, hops) * HALF
        for kind in range(3):
            into = table if kind == 0 else far_table
            base = 0 if kind == 0 else kind * 256 - 256
            here = pl.multiple_of(base + at, 16)
            into[pl.ds(here, 16), :] = firsts[j][kind * 16 : kind * 16 + 16, :]
            there = pl.multiple_of(base + at + 16, 16)
            into[pl.ds(there, 16), :] = seconds[j][kind * 16 : kind * 16 + 16, :]
        g_rows[j * 16 : j * 16 + 16, :] = seconds[j][48:64, :]
        out_rows[j * 16 : j * 16 + 16, :] = seconds[j][64:80, :]
    for copy in copies:
        copy.wait()
    for kind in range(3):
        columns = table[...] if kind == 0 else far_table[kind * 256 - 256 : kind * 256, :]
        out = dot_nt(rows[...], columns).astype(jnp.bfloat16)
        lanes = slice(kind * 128, kind * 128 + 128)
        keep_ref[:, lanes] = jnp.where(low_core, out[:, :128], out[:, 128:])
        send_ref[:, lanes] = jnp.where(low_core, out[:, 128:], out[:, :128])
        if kind:
            lanes_out = slice(kind * 128 - 128, kind * 128)
            for part in range(2):
                for seg in range(2):
                    at = slice((seg * 2 + part) * TOK, (seg * 2 + part + 1) * TOK)
                    into = slice(seg * TOK, seg * TOK + TOK)
                    edges[part][into, lanes_out] = keep_ref[at, lanes]
                    into = slice(2 * TOK + seg * TOK, 2 * TOK + seg * TOK + TOK)
                    edges[part][into, lanes_out] = send_ref[at, lanes]


def far_kernel(index, own_ref, other_ref, table, keep_ref, send_ref):
    low_core = index[1] == 0
    for source in range(2):
        rows = jnp.where(index[1] == source, own_ref[...], other_ref[...])
        at = slice(source * G_ROWS, source * G_ROWS + G_ROWS)
        for kind in range(2):
            out = dot_nt(rows, table[kind * 256 : kind * 256 + 256, :]).astype(jnp.bfloat16)
            lanes = slice(kind * 128, kind * 128 + 128)
            keep_ref[at, lanes] = jnp.where(low_core, out[:, :128], out[:, 128:])
            send_ref[at, lanes] = jnp.where(low_core, out[:, 128:], out[:, :128])


def attention_kernel(index, keep_ref, got_ref, g_keep, g_got, below_ref, below_got, above_ref, above_got, out_ref):
    z, x, limit = index[0], index[2], index[3]
    lane_head = (lax.broadcasted_iota(jnp.int32, (TOK, WIDE), 1) % 128) // HALF
    row = lax.broadcasted_iota(jnp.int32, (HEADS_LOCAL * TOK, TOK), 0) % TOK
    col = lax.broadcasted_iota(jnp.int32, (HEADS_LOCAL * TOK, TOK), 1)
    far = lax.broadcasted_iota(jnp.int32, (1, 2 * G_ROWS), 1)
    far_core, j, far_x, far_k = far >> 7, (far >> 4) & 7, (far >> 3) & 1, far & 7
    delta = jnp.where((j & 1) == 1, -((j + 1) >> 1), j >> 1)
    far_z = (z + delta * (1 - 2 * far_core)) & (Z - 1)
    far_ok = ((far_x * Z + far_z) * C + far_core) * TOK + far_k * BLOCK < limit
    far_keys = jnp.concatenate([g_keep[:, :128], g_got[:, :128]], axis=1)
    far_values = jnp.concatenate([g_keep[:, 128:], g_got[:, 128:]], axis=1)

    def local(kind, at):
        lanes = slice(kind * 128, kind * 128 + 128)
        return jnp.concatenate([keep_ref[at : at + TOK, lanes], got_ref[at : at + TOK, lanes]], axis=1)

    def halo(ref, got, kind, seg):
        at = pl.ds(pl.multiple_of(seg * TOK, TOK), TOK)
        lanes = slice(kind * 128 - 128, kind * 128)
        return jnp.concatenate([ref[at, lanes], got[at, lanes]], axis=1)

    for seg in range(2):
        below_seg = jnp.where(z == 0, 1 - seg, seg)
        above_seg = jnp.where(z == Z - 1, 1 - seg, seg)
        for part in range(2):
            base = (seg * Z + z) * 2 * TOK + part * TOK
            at = (seg * 2 + part) * TOK
            queries = local(0, at)
            stacked = jnp.concatenate(
                [jnp.where(lane_head == h, queries, jnp.zeros_like(queries)) for h in range(HEADS_LOCAL)],
                axis=0,
            )

            def neighbours(kind):
                if part == 0:
                    return halo(below_ref, below_got, kind, below_seg), local(kind, at), local(kind, at + TOK)
                return local(kind, at - TOK), local(kind, at), halo(above_ref, above_got, kind, above_seg)

            k_left, k_mid, k_right = neighbours(1)
            v_left, v_mid, v_right = neighbours(2)
            low = base - TOK
            ok_left = (col > row) & (col + low >= 0) & (col + low < limit)
            ok_mid = col + base < limit
            ok_right = (col < row) & (col + (base + TOK) < limit)
            s_left = jnp.where(ok_left, dot_nt(stacked, k_left), NEGATIVE)
            s_mid = jnp.where(ok_mid, dot_nt(stacked, k_mid), NEGATIVE)
            s_right = jnp.where(ok_right, dot_nt(stacked, k_right), NEGATIVE)
            s_far = jnp.where(far_ok, dot_nt(stacked, far_keys), NEGATIVE)
            near_top = jnp.maximum(jnp.maximum(s_left, s_mid), s_right)
            far_top = jnp.maximum(s_far[:, :128], s_far[:, 128:])
            top = jnp.max(jnp.maximum(near_top, far_top), axis=-1, keepdims=True)
            w_left = jnp.exp(s_left - top)
            w_mid = jnp.exp(s_mid - top)
            w_right = jnp.exp(s_right - top)
            w_far = jnp.exp(s_far - top)
            total = jnp.sum(
                w_left + w_mid + w_right + w_far[:, :128] + w_far[:, 128:], axis=-1, keepdims=True
            )

            def mix(weights, values):
                return jnp.dot(
                    weights.astype(jnp.bfloat16), values, preferred_element_type=jnp.float32
                )

            mixed = mix(w_left, v_left) + mix(w_mid, v_mid) + mix(w_right, v_right) + mix(w_far, far_values)
            mixed = mixed / total
            context = jnp.zeros((TOK, WIDE), jnp.float32)
            for h in range(HEADS_LOCAL):
                context = jnp.where(lane_head == h, mixed[h * TOK : (h + 1) * TOK, :], context)
            mine = jnp.where(x == seg, 0, 1)
            out_ref[mine, part * TOK : (part + 1) * TOK, :] = context.astype(jnp.bfloat16)


def output_kernel(index, own_ref, there_ref, mine, prev, nxt, far_a, far_b, keep_ref, send_ref, table):
    z, core, x, y = index[0], index[1], index[2], index[5]
    own, there = own_ref[...], there_ref[...]
    for side in range(X):
        mixed = jnp.where(x == side, own, there)
        table[2 * side] = mixed[:, :128]
        table[2 * side + 1] = mixed[:, 128:]
    full = jnp.concatenate([table[(y + turn) & 3] for turn in (0, 3, 1, 2)], axis=1)
    for j, (way, hops) in enumerate(STEPS):
        zj = z_of(z, core, way, hops)
        here = j * 16
        far = (far_a, here) if j < 4 else (far_b, here - 64)
        weights = [
            ref[at : at + 16, i * 256 : i * 256 + 256]
            for ref, at in ((mine, here), (prev, here), (nxt, here), far)
            for i in range(8)
        ]
        out = jnp.dot(full, jnp.concatenate(weights, axis=0), preferred_element_type=jnp.float32)
        keep = jnp.where(core == 0, out[:TOK], out[TOK:])
        sent = jnp.where(core == 0, out[TOK:], out[:TOK]).astype(jnp.bfloat16)
        for side in range(X):
            lanes = pl.ds(pl.multiple_of((side * Z + zj) * 128, 128), 128)
            keep_ref[:, lanes] = keep[:, side * 128 : side * 128 + 128]
            send_ref[:, lanes] = sent[:, side * 128 : side * 128 + 128]


def on_chip(kernel, out_shape, flops, exps, args, scratch=(), in_hbm=0):
    vmem = pl.BlockSpec(memory_space=pltpu.VMEM)
    specs = [pl.BlockSpec(memory_space=pltpu.SMEM)] + [pl.BlockSpec(memory_space=pltpu.HBM)] * in_hbm
    specs += [vmem] * (len(args) - len(specs))
    return pl.pallas_call(
        kernel,
        out_shape=out_shape,
        in_specs=specs,
        out_specs=jax.tree.map(lambda _: vmem, out_shape),
        scratch_shapes=list(scratch),
        compiler_params=pltpu.CompilerParams(vmem_limit_bytes=VMEM_LIMIT),
        cost_estimate=pl.CostEstimate(flops=flops, bytes_accessed=4 << 20, transcendentals=exps),
    )(*args)


def after(value, *others):
    return lax.optimization_barrier((value, *others))[0]


def per_device(hidden_in, length, attn_gain, global_gain, w_query, w_key, w_value, w_out):
    width = hidden_in.shape[1]
    me = lax.axis_index("seq")
    core = me & 1
    z = (me >> 1) & (Z - 1)
    x = me >> 4
    limit = length[0]
    bf16 = jnp.bfloat16
    y = lax.axis_index("doc") & (Y - 1)
    index = jnp.stack([z, core, x, limit, me * TOK, y]).astype(jnp.int32)

    mine = jnp.stack([w_query.T, w_key.T, w_value.T]).reshape(3, 2, 16, width)
    first = mine[:, 0].reshape(48, width)

    normed, global_mine = on_chip(
        norm_kernel,
        (jax.ShapeDtypeStruct((TOK, width), bf16), jax.ShapeDtypeStruct((TOK // BLOCK, width), bf16)),
        8 * TOK * width,
        0,
        (index, after(hidden_in, first), attn_gain[None], global_gain[None]),
        (
            pltpu.VMEM((TOK, width), bf16),
            pltpu.VMEM((1, width), jnp.float32),
            pltpu.VMEM((1, width), jnp.float32),
            pltpu.SemaphoreType.DMA((3,)),
        ),
        in_hbm=3,
    )
    global_there = send(global_mine, OTHER_X)

    split = after(w_out, first).reshape(X, 2, HEADS_LOCAL, 2, HALF, 64)

    def slab(group):
        at = (y >> 1, group, 0, (y & 1) ^ group, 0, 0)
        return lax.dynamic_slice(split, at, (1, 1, HEADS_LOCAL, 1, HALF, 64)).reshape(128, 64)

    kept = slab(core)
    passed = send(slab(1 - core), OTHER_CORE)
    chip = jnp.concatenate([jnp.where(core == 0, kept, passed), jnp.where(core == 0, passed, kept)], axis=1)
    chip_there = send(chip, OTHER_X)
    both = jnp.concatenate([jnp.where(x == 0, chip, chip_there), jnp.where(x == 0, chip_there, chip)], axis=1)

    second = jnp.concatenate(
        [
            mine[:, 1].reshape(48, width),
            jnp.where(x == 0, global_mine, global_there),
            jnp.where(x == 0, global_there, global_mine),
            jnp.concatenate([both[i * 16 : i * 16 + 16] for i in range(8)], axis=1),
        ],
        axis=0,
    )

    one, two = {(0, 0): first}, {(0, 0): second}
    a_one, a_two, b_one, b_two = first, second, first, second
    for step in range(1, 5):
        if step == 2:
            to_send = after(normed, one[0, 1])
            across = send(to_send, OTHER_X)
            beside = send(to_send, OTHER_CORE)
            beside_across = send(across, OTHER_CORE)
            a_two = b_two = after(second, a_one, b_one)
        if step > 1:
            if step > 2:
                before = one[0, step - 2], one[1, step - 2]
                a_two, b_two = lax.optimization_barrier((a_two, b_two, *before))[:2]
            if step == 4:
                a_two, b_two = lax.optimization_barrier((a_two, b_two, across, beside, beside_across))[:2]
            two[0, step - 1] = a_two = send(a_two, AHEAD)
            two[1, step - 1] = b_two = send(b_two, BEHIND)
        if step > 2:
            before = two[0, step - 2], two[1, step - 2]
            a_one, b_one = lax.optimization_barrier((a_one, b_one, *before))[:2]
        one[0, step] = a_one = send(a_one, AHEAD)
        if step < 4:
            one[1, step] = b_one = send(b_one, BEHIND)
    a_two = after(a_two, one[0, 3], one[1, 3])
    two[0, 4] = send(a_two, AHEAD)
    firsts = [one[s] for s in STEPS]
    seconds = [two[s] for s in STEPS]

    half = jax.ShapeDtypeStruct((ROWS, 3 * 128), bf16)
    keep, to_swap, g_own, far_table, out_own, *edges = on_chip(
        project_kernel,
        (
            half,
            half,
            jax.ShapeDtypeStruct((G_ROWS, width), bf16),
            jax.ShapeDtypeStruct((2 * Z * HALF, width), bf16),
            jax.ShapeDtypeStruct((128, width), bf16),
            *[jax.ShapeDtypeStruct((4 * TOK, 256), bf16)] * 2,
        ),
        2 * ROWS * 768 * width,
        0,
        (index, normed, across, beside, beside_across, *firsts, *seconds),
        (pltpu.VMEM((ROWS, width), bf16), pltpu.VMEM((Z * HALF, width), bf16), pltpu.SemaphoreType.DMA((4,))),
        in_hbm=4,
    )
    got = send(to_swap, OTHER_CORE)
    g_other = send(g_own, OTHER_CORE)

    below, above = send(edges[1], UP), send(edges[0], DOWN)
    below = below, send(below[2 * TOK :], OTHER_CORE)
    above = above, send(above[2 * TOK :], OTHER_CORE)
    far_half = jax.ShapeDtypeStruct((2 * G_ROWS, 256), bf16)
    g_keep, g_swap = on_chip(
        far_kernel, (far_half, far_half), 2 * 256 * 512 * width, 0, (index, g_own, g_other, far_table)
    )
    g_got = send(g_swap, OTHER_CORE)

    to_pass = out_own
    out_prev = send(to_pass, Y_UP, "doc")
    out_next = send(to_pass, Y_DOWN, "doc")
    out_far_a = send(out_prev[:64], Y_UP, "doc")
    out_far_b = send(out_next[64:], Y_DOWN, "doc")

    context = on_chip(
        attention_kernel,
        jax.ShapeDtypeStruct((2, 2 * TOK, WIDE), bf16),
        4 * 4 * TOK * 640 * WIDE * 4,
        4 * 4 * TOK * 640,
        (index, keep, got, g_keep, g_got, *below, *above),
    )

    there = send(context[1], OTHER_X)
    kept_part, sent_part = on_chip(
        output_kernel,
        (jax.ShapeDtypeStruct((TOK, width), jnp.float32), jax.ShapeDtypeStruct((TOK, width), bf16)),
        2 * 256 * 512 * width,
        0,
        (index, context[0], there, out_own, out_prev, out_next, out_far_a, out_far_b),
        (pltpu.VMEM((4, 2 * TOK, 128), bf16),),
    )
    return (kept_part + send(sent_part, OTHER_CORE).astype(jnp.float32)).astype(bf16)


def solution(mesh):
    placed = (
        P(("doc", "seq"), None),
        P("doc"),
        P(),
        P(),
        P(None, "seq"),
        P(None, "seq"),
        P(None, "seq"),
        P(None, "seq"),
    )
    return jax.shard_map(
        per_device, mesh=mesh, in_specs=placed, out_specs=P(("doc", "seq"), None), check_vma=False
    )
```

```python
import jax
import jax.numpy as jnp
from jax import lax
from jax.experimental import pallas as pl
from jax.experimental.pallas import tpu as pltpu
from jax.sharding import PartitionSpec as P

HEAD_DIM = 64
BLOCK = 16
RADIUS = 127
NEGATIVE = -1e30
EPSILON = 1e-06

X, Z, C = 2, 8, 2
SEQ_SHARDS = X * Z * C
TOK = 128
HALF = 32
HEADS_LOCAL = 4
WIDE = HEADS_LOCAL * HEAD_DIM


def place(x, z, core):
    return (x * Z + z) * C + core


def pairs(move):
    return [
        (place(x, z, c), place(*move(x, z, c))) for x in range(X) for z in range(Z) for c in range(C)
    ]


OTHER_CORE = pairs(lambda x, z, c: (x, z, 1 - c))
OTHER_X = pairs(lambda x, z, c: (1 - x, z, c))
AHEAD = pairs(lambda x, z, c: (x, (z + (1 if c == 0 else -1)) % Z, c))
BEHIND = pairs(lambda x, z, c: (x, (z - (1 if c == 0 else -1)) % Z, c))
UP = pairs(lambda x, z, c: (x, (z + 1) % Z, c))
DOWN = pairs(lambda x, z, c: (x, (z - 1) % Z, c))


Y = 4
Y_UP = [(d, (d & 4) | ((d + 1) & 3)) for d in range(2 * Y)]
Y_DOWN = [(d, (d & 4) | ((d - 1) & 3)) for d in range(2 * Y)]


def send(value, route, axis="seq"):
    return lax.ppermute(value, axis, route)


def rms_norm(values, gain_row):
    mean_square = jnp.mean(values * values, axis=-1, keepdims=True)
    return values * lax.rsqrt(mean_square + EPSILON) * gain_row


def norm_kernel(index, hidden_in, gain_in, global_in, normed_ref, blocks_ref, hidden, gain, global_gain, sems):
    copies = [
        pltpu.make_async_copy(source, into, sems.at[i])
        for i, (source, into) in enumerate(((hidden_in, hidden), (gain_in, gain), (global_in, global_gain)))
    ]
    for copy in copies:
        copy.start()
    for copy in copies:
        copy.wait()
    normed = rms_norm(hidden[...].astype(jnp.float32), gain[...]).astype(jnp.bfloat16)
    normed_ref[...] = normed
    at = index[4] + lax.broadcasted_iota(jnp.int32, (TOK, 1), 0)
    valid = (at < index[3]).astype(jnp.float32)
    kept = (normed.astype(jnp.float32) * valid).reshape(TOK // BLOCK, BLOCK, normed.shape[1])
    blocks_ref[...] = rms_norm(jnp.sum(kept, axis=1), global_gain[...]).astype(jnp.bfloat16)


def dot_nt(left, right):
    return lax.dot_general(
        left, right, (((1,), (1,)), ((), ())), preferred_element_type=jnp.float32
    )


STEPS = ((0, 0), (0, 1), (1, 1), (0, 2), (1, 2), (0, 3), (1, 3), (0, 4))
SHARDS = len(STEPS)
ROWS = 4 * TOK
G_ROWS = Z * 16
VMEM_LIMIT = 32 * 1024 * 1024


def z_of(z, core, way, hops):
    delta = -hops if way == 0 else hops
    return (z + delta * (1 - 2 * core)) & (Z - 1)


def project_kernel(index, *refs):
    blocks, firsts, seconds = refs[:4], refs[4 : 4 + SHARDS], refs[4 + SHARDS : 4 + 2 * SHARDS]
    keep_ref, send_ref, g_rows, far_table, out_rows, *edges, rows, table, sems = refs[4 + 2 * SHARDS :]
    z, core, x = index[0], index[1], index[2]
    low_core = core == 0
    copies = []
    for i, (ref, bx, bc) in enumerate(zip(blocks, (x, 1 - x, x, 1 - x), (core, core, 1 - core, 1 - core))):
        into = rows.at[pl.ds(pl.multiple_of((bx * 2 + bc) * TOK, TOK), TOK), :]
        copies.append(pltpu.make_async_copy(ref, into, sems.at[i]))
        copies[-1].start()
    for j, (way, hops) in enumerate(STEPS):
        at = z_of(z, core, way, hops) * HALF
        for kind in range(3):
            into = table if kind == 0 else far_table
            base = 0 if kind == 0 else kind * 256 - 256
            here = pl.multiple_of(base + at, 16)
            into[pl.ds(here, 16), :] = firsts[j][kind * 16 : kind * 16 + 16, :]
            there = pl.multiple_of(base + at + 16, 16)
            into[pl.ds(there, 16), :] = seconds[j][kind * 16 : kind * 16 + 16, :]
        g_rows[j * 16 : j * 16 + 16, :] = seconds[j][48:64, :]
        out_rows[j * 16 : j * 16 + 16, :] = seconds[j][64:80, :]
    for copy in copies:
        copy.wait()
    for kind in range(3):
        columns = table[...] if kind == 0 else far_table[kind * 256 - 256 : kind * 256, :]
        out = dot_nt(rows[...], columns).astype(jnp.bfloat16)
        lanes = slice(kind * 128, kind * 128 + 128)
        keep_ref[:, lanes] = jnp.where(low_core, out[:, :128], out[:, 128:])
        send_ref[:, lanes] = jnp.where(low_core, out[:, 128:], out[:, :128])
        if kind:
            lanes_out = slice(kind * 128 - 128, kind * 128)
            for part in range(2):
                for seg in range(2):
                    at = slice((seg * 2 + part) * TOK, (seg * 2 + part + 1) * TOK)
                    into = slice(seg * TOK, seg * TOK + TOK)
                    edges[part][into, lanes_out] = keep_ref[at, lanes]
                    into = slice(2 * TOK + seg * TOK, 2 * TOK + seg * TOK + TOK)
                    edges[part][into, lanes_out] = send_ref[at, lanes]


def far_kernel(index, own_ref, other_ref, table, keep_ref, send_ref):
    low_core = index[1] == 0
    for source in range(2):
        rows = jnp.where(index[1] == source, own_ref[...], other_ref[...])
        at = slice(source * G_ROWS, source * G_ROWS + G_ROWS)
        for kind in range(2):
            out = dot_nt(rows, table[kind * 256 : kind * 256 + 256, :]).astype(jnp.bfloat16)
            lanes = slice(kind * 128, kind * 128 + 128)
            keep_ref[at, lanes] = jnp.where(low_core, out[:, :128], out[:, 128:])
            send_ref[at, lanes] = jnp.where(low_core, out[:, 128:], out[:, :128])


def attention_kernel(index, keep_ref, got_ref, g_keep, g_got, below_ref, below_got, above_ref, above_got, out_ref):
    z, x, limit = index[0], index[2], index[3]
    lane_head = (lax.broadcasted_iota(jnp.int32, (TOK, WIDE), 1) % 128) // HALF
    row = lax.broadcasted_iota(jnp.int32, (HEADS_LOCAL * TOK, TOK), 0) % TOK
    col = lax.broadcasted_iota(jnp.int32, (HEADS_LOCAL * TOK, TOK), 1)
    far = lax.broadcasted_iota(jnp.int32, (1, 2 * G_ROWS), 1)
    far_core, j, far_x, far_k = far >> 7, (far >> 4) & 7, (far >> 3) & 1, far & 7
    delta = jnp.where((j & 1) == 1, -((j + 1) >> 1), j >> 1)
    far_z = (z + delta * (1 - 2 * far_core)) & (Z - 1)
    far_ok = ((far_x * Z + far_z) * C + far_core) * TOK + far_k * BLOCK < limit
    far_keys = jnp.concatenate([g_keep[:, :128], g_got[:, :128]], axis=1)
    far_values = jnp.concatenate([g_keep[:, 128:], g_got[:, 128:]], axis=1)

    def local(kind, at):
        lanes = slice(kind * 128, kind * 128 + 128)
        return jnp.concatenate([keep_ref[at : at + TOK, lanes], got_ref[at : at + TOK, lanes]], axis=1)

    def halo(ref, got, kind, seg):
        at = pl.ds(pl.multiple_of(seg * TOK, TOK), TOK)
        lanes = slice(kind * 128 - 128, kind * 128)
        return jnp.concatenate([ref[at, lanes], got[at, lanes]], axis=1)

    for seg in range(2):
        below_seg = jnp.where(z == 0, 1 - seg, seg)
        above_seg = jnp.where(z == Z - 1, 1 - seg, seg)
        for part in range(2):
            base = (seg * Z + z) * 2 * TOK + part * TOK
            at = (seg * 2 + part) * TOK
            queries = local(0, at)
            stacked = jnp.concatenate(
                [jnp.where(lane_head == h, queries, jnp.zeros_like(queries)) for h in range(HEADS_LOCAL)],
                axis=0,
            )

            def neighbours(kind):
                if part == 0:
                    return halo(below_ref, below_got, kind, below_seg), local(kind, at), local(kind, at + TOK)
                return local(kind, at - TOK), local(kind, at), halo(above_ref, above_got, kind, above_seg)

            k_left, k_mid, k_right = neighbours(1)
            v_left, v_mid, v_right = neighbours(2)
            low = base - TOK
            ok_left = (col > row) & (col + low >= 0) & (col + low < limit)
            ok_mid = col + base < limit
            ok_right = (col < row) & (col + (base + TOK) < limit)
            s_left = jnp.where(ok_left, dot_nt(stacked, k_left), NEGATIVE)
            s_mid = jnp.where(ok_mid, dot_nt(stacked, k_mid), NEGATIVE)
            s_right = jnp.where(ok_right, dot_nt(stacked, k_right), NEGATIVE)
            s_far = jnp.where(far_ok, dot_nt(stacked, far_keys), NEGATIVE)
            near_top = jnp.maximum(jnp.maximum(s_left, s_mid), s_right)
            far_top = jnp.maximum(s_far[:, :128], s_far[:, 128:])
            top = jnp.max(jnp.maximum(near_top, far_top), axis=-1, keepdims=True)
            w_left = jnp.exp(s_left - top)
            w_mid = jnp.exp(s_mid - top)
            w_right = jnp.exp(s_right - top)
            w_far = jnp.exp(s_far - top)
            total = jnp.sum(
                w_left + w_mid + w_right + w_far[:, :128] + w_far[:, 128:], axis=-1, keepdims=True
            )

            def mix(weights, values):
                return jnp.dot(
                    weights.astype(jnp.bfloat16), values, preferred_element_type=jnp.float32
                )

            mixed = mix(w_left, v_left) + mix(w_mid, v_mid) + mix(w_right, v_right) + mix(w_far, far_values)
            mixed = mixed / total
            context = jnp.zeros((TOK, WIDE), jnp.float32)
            for h in range(HEADS_LOCAL):
                context = jnp.where(lane_head == h, mixed[h * TOK : (h + 1) * TOK, :], context)
            mine = jnp.where(x == seg, 0, 1)
            out_ref[mine, part * TOK : (part + 1) * TOK, :] = context.astype(jnp.bfloat16)


def output_kernel(index, own_ref, there_ref, mine, prev, nxt, far_a, far_b, keep_ref, send_ref, table):
    z, core, x, y = index[0], index[1], index[2], index[5]
    own, there = own_ref[...], there_ref[...]
    for side in range(X):
        mixed = jnp.where(x == side, own, there)
        table[2 * side] = mixed[:, :128]
        table[2 * side + 1] = mixed[:, 128:]
    full = jnp.concatenate([table[(y + turn) & 3] for turn in (0, 3, 1, 2)], axis=1)
    for j, (way, hops) in enumerate(STEPS):
        zj = z_of(z, core, way, hops)
        here = j * 16
        far = (far_a, here) if j < 4 else (far_b, here - 64)
        weights = [
            ref[at : at + 16, i * 256 : i * 256 + 256]
            for ref, at in ((mine, here), (prev, here), (nxt, here), far)
            for i in range(8)
        ]
        out = jnp.dot(full, jnp.concatenate(weights, axis=0), preferred_element_type=jnp.float32)
        keep = jnp.where(core == 0, out[:TOK], out[TOK:])
        sent = jnp.where(core == 0, out[TOK:], out[:TOK]).astype(jnp.bfloat16)
        for side in range(X):
            lanes = pl.ds(pl.multiple_of((side * Z + zj) * 128, 128), 128)
            keep_ref[:, lanes] = keep[:, side * 128 : side * 128 + 128]
            send_ref[:, lanes] = sent[:, side * 128 : side * 128 + 128]


def on_chip(kernel, out_shape, flops, exps, args, scratch=(), in_hbm=0):
    vmem = pl.BlockSpec(memory_space=pltpu.VMEM)
    specs = [pl.BlockSpec(memory_space=pltpu.SMEM)] + [pl.BlockSpec(memory_space=pltpu.HBM)] * in_hbm
    specs += [vmem] * (len(args) - len(specs))
    return pl.pallas_call(
        kernel,
        out_shape=out_shape,
        in_specs=specs,
        out_specs=jax.tree.map(lambda _: vmem, out_shape),
        scratch_shapes=list(scratch),
        compiler_params=pltpu.CompilerParams(vmem_limit_bytes=VMEM_LIMIT),
        cost_estimate=pl.CostEstimate(flops=flops, bytes_accessed=4 << 20, transcendentals=exps),
    )(*args)


def after(value, *others):
    return lax.optimization_barrier((value, *others))[0]


def per_device(hidden_in, length, attn_gain, global_gain, w_query, w_key, w_value, w_out):
    width = hidden_in.shape[1]
    me = lax.axis_index("seq")
    core = me & 1
    z = (me >> 1) & (Z - 1)
    x = me >> 4
    limit = length[0]
    bf16 = jnp.bfloat16
    y = lax.axis_index("doc") & (Y - 1)
    index = jnp.stack([z, core, x, limit, me * TOK, y]).astype(jnp.int32)

    mine = jnp.stack([w_query.T, w_key.T, w_value.T]).reshape(3, 2, 16, width)
    first = mine[:, 0].reshape(48, width)

    normed, global_mine = on_chip(
        norm_kernel,
        (jax.ShapeDtypeStruct((TOK, width), bf16), jax.ShapeDtypeStruct((TOK // BLOCK, width), bf16)),
        8 * TOK * width,
        0,
        (index, after(hidden_in, first), attn_gain[None], global_gain[None]),
        (
            pltpu.VMEM((TOK, width), bf16),
            pltpu.VMEM((1, width), jnp.float32),
            pltpu.VMEM((1, width), jnp.float32),
            pltpu.SemaphoreType.DMA((3,)),
        ),
        in_hbm=3,
    )
    global_there = send(global_mine, OTHER_X)

    split = after(w_out, first).reshape(X, 2, HEADS_LOCAL, 2, HALF, 64)

    def slab(group):
        at = (y >> 1, group, 0, (y & 1) ^ group, 0, 0)
        return lax.dynamic_slice(split, at, (1, 1, HEADS_LOCAL, 1, HALF, 64)).reshape(128, 64)

    kept = slab(core)
    passed = send(slab(1 - core), OTHER_CORE)
    chip = jnp.concatenate([jnp.where(core == 0, kept, passed), jnp.where(core == 0, passed, kept)], axis=1)
    chip_there = send(chip, OTHER_X)
    both = jnp.concatenate([jnp.where(x == 0, chip, chip_there), jnp.where(x == 0, chip_there, chip)], axis=1)

    second = jnp.concatenate(
        [
            mine[:, 1].reshape(48, width),
            jnp.where(x == 0, global_mine, global_there),
            jnp.where(x == 0, global_there, global_mine),
            jnp.concatenate([both[i * 16 : i * 16 + 16] for i in range(8)], axis=1),
        ],
        axis=0,
    )

    one, two = {(0, 0): first}, {(0, 0): second}
    a_one, a_two, b_one, b_two = first, second, first, second
    for step in range(1, 5):
        if step == 2:
            to_send = after(normed, one[0, 1])
            across = send(to_send, OTHER_X)
            beside = send(to_send, OTHER_CORE)
            beside_across = send(across, OTHER_CORE)
            a_two = b_two = after(second, a_one, b_one)
        if step > 1:
            if step > 2:
                before = one[0, step - 2], one[1, step - 2]
                a_two, b_two = lax.optimization_barrier((a_two, b_two, *before))[:2]
            two[0, step - 1] = a_two = send(a_two, AHEAD)
            if step == 4:
                b_two = after(b_two, across, beside, beside_across)
            two[1, step - 1] = b_two = send(b_two, BEHIND)
        if step > 2:
            before = two[0, step - 2], two[1, step - 2]
            a_one, b_one = lax.optimization_barrier((a_one, b_one, *before))[:2]
        one[0, step] = a_one = send(a_one, AHEAD)
        if step < 4:
            one[1, step] = b_one = send(b_one, BEHIND)
    a_two = after(a_two, one[0, 3], one[1, 3])
    two[0, 4] = send(a_two, AHEAD)
    firsts = [one[s] for s in STEPS]
    seconds = [two[s] for s in STEPS]

    half = jax.ShapeDtypeStruct((ROWS, 3 * 128), bf16)
    keep, to_swap, g_own, far_table, out_own, *edges = on_chip(
        project_kernel,
        (
            half,
            half,
            jax.ShapeDtypeStruct((G_ROWS, width), bf16),
            jax.ShapeDtypeStruct((2 * Z * HALF, width), bf16),
            jax.ShapeDtypeStruct((128, width), bf16),
            *[jax.ShapeDtypeStruct((4 * TOK, 256), bf16)] * 2,
        ),
        2 * ROWS * 768 * width,
        0,
        (index, normed, across, beside, beside_across, *firsts, *seconds),
        (pltpu.VMEM((ROWS, width), bf16), pltpu.VMEM((Z * HALF, width), bf16), pltpu.SemaphoreType.DMA((4,))),
        in_hbm=4,
    )
    got = send(to_swap, OTHER_CORE)
    g_other = send(g_own, OTHER_CORE)

    below, above = send(edges[1], UP), send(edges[0], DOWN)
    below = below, send(below[2 * TOK :], OTHER_CORE)
    above = above, send(above[2 * TOK :], OTHER_CORE)
    far_half = jax.ShapeDtypeStruct((2 * G_ROWS, 256), bf16)
    g_keep, g_swap = on_chip(
        far_kernel, (far_half, far_half), 2 * 256 * 512 * width, 0, (index, g_own, g_other, far_table)
    )
    g_got = send(g_swap, OTHER_CORE)

    to_pass = after(out_own, g_other)
    out_prev = send(to_pass, Y_UP, "doc")
    out_next = send(to_pass, Y_DOWN, "doc")
    out_far_a = send(out_prev[:64], Y_UP, "doc")
    out_far_b = send(out_next[64:], Y_DOWN, "doc")

    context = on_chip(
        attention_kernel,
        jax.ShapeDtypeStruct((2, 2 * TOK, WIDE), bf16),
        4 * 4 * TOK * 640 * WIDE * 4,
        4 * 4 * TOK * 640,
        (index, keep, got, g_keep, g_got, *below, *above),
    )

    there = send(context[1], OTHER_X)
    kept_part, sent_part = on_chip(
        output_kernel,
        (jax.ShapeDtypeStruct((TOK, width), jnp.float32), jax.ShapeDtypeStruct((TOK, width), bf16)),
        2 * 256 * 512 * width,
        0,
        (index, context[0], there, out_own, out_prev, out_next, out_far_a, out_far_b),
        (pltpu.VMEM((4, 2 * TOK, 128), bf16),),
    )
    return (kept_part + send(sent_part, OTHER_CORE).astype(jnp.float32)).astype(bf16)


def solution(mesh):
    placed = (
        P(("doc", "seq"), None),
        P("doc"),
        P(),
        P(),
        P(None, "seq"),
        P(None, "seq"),
        P(None, "seq"),
        P(None, "seq"),
    )
    return jax.shard_map(
        per_device, mesh=mesh, in_specs=placed, out_specs=P(("doc", "seq"), None), check_vma=False
    )
```
